128 devices in a mesh: shard: 4 (over x), rep: 32 (over y, z, core).
Axes of the slice: x: 4, y: 4, z: 4, core: 2. Of those that a mesh axis runs over, the one named last changes fastest.
Arguments:
- tokens: bfloat16 [65536, 8192], P('rep', 'shard'), may hold values from -21 to 21
- key_cotangent: bfloat16 [65536, 1024], P('rep'), may hold values from -21 to 21
- value_cotangent: bfloat16 [65536, 1024], P('rep'), may hold values from -21 to 21
- key_weight: float32 [8192, 1024], P(('shard', 'rep')), may hold values from -0.75 to 0.75
- value_weight: float32 [8192, 1024], P(('shard', 'rep')), may hold values from -0.75 to 0.75
- key_moment: float32 [8192, 1024], P(('shard', 'rep')), may hold values from -6 to 6
- value_moment: float32 [8192, 1024], P(('shard', 'rep')), may hold values from -6 to 6
Outputs:
- new_key_weight: float32 [8192, 1024], P(('shard', 'rep'))
- new_value_weight: float32 [8192, 1024], P(('shard', 'rep'))
- new_key_moment: float32 [8192, 1024], P(('shard', 'rep'))
- new_value_moment: float32 [8192, 1024], P(('shard', 'rep'))
The draws below stay inside these ranges and needn't reach their ends.
All inputs are finite; a program needn't handle non-finite values.
Results may differ from the reference program's by a relative error of at most 0.0003.
Values may be sent and summed in bfloat16 or wider, within the bound.
No kernel may reach another device: no remote copies, remote signals or barrier semaphores. Data moves between devices by JAX's collectives and lax.ppermute only.
A program may use at most 128 MiB of HBM per device.

```python
import math
import jax
import jax.numpy as jnp
from jax import lax

D = 8192
KV = 1024
TOK_DEV = 2048
TOKENS = 65536
N_REP = 32


def shifted_draw(key, columns, column_scale):
    shift_key, noise_key = jax.random.split(key, 2)
    shift_size = 1.22 * TOK_DEV ** (-0.25)
    shifted = jnp.clip(jax.random.normal(shift_key, (columns,), jnp.float32), -4.0, 4.0) * shift_size
    jitter = jnp.clip(jax.random.normal(noise_key, (TOKENS, columns), jnp.float32), -4.0, 4.0)
    return (column_scale[None, :] * (shifted[None, :] + jitter)).astype(jnp.bfloat16)


def draw_tokens(key, part):
    folded = jax.random.fold_in(key, 11)
    position_ramp = jnp.arange(D, dtype=jnp.float32) / (D - 1)
    column_scale = 3.0 ** position_ramp
    return shifted_draw(folded, D, column_scale)


def cotangent_draw(key, salt_value):
    folded = jax.random.fold_in(key, salt_value)
    scale_key, remaining = jax.random.split(folded, 2)
    column_scale = jnp.exp(jax.random.uniform(scale_key, (KV,), jnp.float32, math.log(0.3), math.log(3.0)))
    return shifted_draw(remaining, KV, column_scale)


def draw_key_cotangent(key, part):
    return cotangent_draw(key, 23)


def draw_value_cotangent(key, part):
    return cotangent_draw(key, 37)


def block_levels(rng, dims, cuts, least, top_value):
    def one(position, blocks):
        draws = jax.random.uniform(jax.random.fold_in(jax.random.fold_in(rng, 6), position), (blocks,), jnp.float32, least / len(cuts), top_value / len(cuts))
        return jnp.repeat(jnp.exp(draws), dims[position] // blocks).reshape((-1,) + (1,) * (len(dims) - position - 1))

    factor_of = one(*cuts[0])
    for cut in cuts[1:]:
        factor_of = factor_of * one(*cut)
    return factor_of


def normal_values(rng, shape, deviation, reach, cuts=(), kind=jnp.bfloat16):
    result = deviation * jax.random.normal(rng, shape, jnp.float32)
    if cuts:
        result = result * block_levels(rng, shape, cuts, -0.22, 0.18)
    return jnp.clip(result, -reach, reach).astype(kind)


def setup_inputs(seed: int = 0) -> dict:
    seeds = jax.random.split(jax.random.key(seed), 8)
    return {
        "tokens": draw_tokens(jax.random.fold_in(seeds[7], 71), 0),
        "key_cotangent": draw_key_cotangent(jax.random.fold_in(seeds[7], 71), 0),
        "value_cotangent": draw_value_cotangent(jax.random.fold_in(seeds[7], 71), 0),
        "key_weight": normal_values(seeds[3], (D, KV), 0.05, 0.75, ((0, 128),), jnp.float32),
        "value_weight": normal_values(seeds[4], (D, KV), 0.05, 0.75, ((0, 128),), jnp.float32),
        "key_moment": normal_values(seeds[5], (D, KV), 1.0, 6.0, ((0, 128),), jnp.float32),
        "value_moment": normal_values(seeds[6], (D, KV), 1.0, 6.0, ((0, 128),), jnp.float32),
    }


EPSILON = 1e-06
MOMENTUM_DECAY = 0.9
STEP_SIZE = 0.01

def replica_grad(tokens, cotangent, replica):
    token_rows = tokens[replica * TOK_DEV:(replica + 1) * TOK_DEV]
    cotangent_rows = cotangent[replica * TOK_DEV:(replica + 1) * TOK_DEV]
    product = lax.dot_general(token_rows, cotangent_rows, (((0,), (0,)), ((), ())), preferred_element_type=jnp.float32)
    return product * (1.0 / math.sqrt(TOK_DEV))

def combine(left_part, right_part):
    cross = jnp.sum(left_part * right_part)
    left_square = jnp.sum(left_part * left_part)
    right_square = jnp.sum(right_part * right_part)
    left_coef = 1.0 - cross / (2.0 * (left_square + EPSILON))
    right_coef = 1.0 - cross / (2.0 * (right_square + EPSILON))
    return left_coef * left_part + right_coef * right_part

def merged_tree(tokens, cotangent, start_index, members):
    if members == 1:
        return replica_grad(tokens, cotangent, start_index)
    half_members = members // 2
    left_part = merged_tree(tokens, cotangent, start_index, half_members)
    right_part = merged_tree(tokens, cotangent, start_index + half_members, half_members)
    return combine(left_part, right_part)

def reference(tokens, key_cotangent, value_cotangent, key_weight, value_weight, key_moment, value_moment):
    key_merged = merged_tree(tokens, key_cotangent, 0, N_REP)
    value_merged = merged_tree(tokens, value_cotangent, 0, N_REP)
    new_key_moment = MOMENTUM_DECAY * key_moment + key_merged
    new_value_moment = MOMENTUM_DECAY * value_moment + value_merged
    new_key_weight = key_weight - STEP_SIZE * new_key_moment
    new_value_weight = value_weight - STEP_SIZE * new_value_moment
    return (new_key_weight, new_value_weight, new_key_moment, new_value_moment)
```

```python
import functools
import math

import jax
import jax.numpy as jnp
from jax import lax
from jax.experimental import pallas as pl
from jax.experimental.pallas import tpu as pltpu
from jax.sharding import PartitionSpec as P

EPSILON = 1e-06
MOMENTUM_DECAY = 0.9
STEP_SIZE = 0.01
CHIPS = 16
ROWS = 64
FEATURES = 1024
SENT_NORM = 16384.0
LIMIT = 60 << 20


def grad_kernel(core_ref, x_ref, y_ref, own_ref, other_ref, *, factor):
    product = lax.dot_general(
        x_ref[...], y_ref[...], (((0,), (0,)), ((), ())), preferred_element_type=jnp.float32
    )
    blocks = (product * factor).reshape(-1, 2, ROWS, FEATURES)
    first, second = blocks[:, 0], blocks[:, 1]
    is_first = core_ref[0] == 0
    own_ref[...] = jnp.where(is_first, first, second)
    other_ref[...] = jnp.where(is_first, second, first)


def half_grads(core, tokens, cotangent, start, count):
    depth = tokens.shape[0]
    width = 512
    steps = count // width
    first = start // width
    per = width // (2 * ROWS)
    out = jax.ShapeDtypeStruct((count // (2 * ROWS), ROWS, FEATURES), jnp.float32)
    spec = pl.BlockSpec((per, ROWS, FEATURES), lambda i, c: (i, 0, 0))
    return pl.pallas_call(
        functools.partial(grad_kernel, factor=1.0 / math.sqrt(depth)),
        out_shape=(out, out),
        grid_spec=pltpu.PrefetchScalarGridSpec(
            num_scalar_prefetch=1,
            grid=(steps,),
            in_specs=[
                pl.BlockSpec((depth, width), lambda i, c: (0, i + first)),
                pl.BlockSpec((depth, FEATURES), lambda i, c: (0, 0)),
            ],
            out_specs=[spec, spec],
        ),
        compiler_params=pltpu.CompilerParams(vmem_limit_bytes=LIMIT),
        cost_estimate=pl.CostEstimate(
            flops=2 * depth * count * FEATURES, bytes_accessed=16 << 20, transcendentals=0
        ),
    )(core, tokens, cotangent)


def pair_kernel(a_ref, b_ref, o_ref, acc_ref):
    step = pl.program_id(0)

    @pl.when(step == 0)
    def _():
        acc_ref[...] = jnp.zeros_like(acc_ref)

    a = a_ref[...].reshape(-1, 8, FEATURES)
    b = b_ref[...].reshape(-1, 8, FEATURES)
    acc_ref[0] += jnp.sum(a * b, axis=0)
    acc_ref[1] += jnp.sum(a * a, axis=0)
    acc_ref[2] += jnp.sum(b * b, axis=0)

    @pl.when(step == pl.num_programs(0) - 1)
    def _():
        for k in range(3):
            row = jnp.sum(acc_ref[k], axis=0, keepdims=True)
            total = jnp.sum(row.reshape(1, FEATURES), axis=1, keepdims=True)
            o_ref[pl.ds(k, 1), :] = jnp.broadcast_to(total, (1, 128))


def pair_sums(a, b):
    count = a.shape[0]
    spec = pl.BlockSpec((4, ROWS, FEATURES), lambda i: (i, 0, 0))
    return pl.pallas_call(
        pair_kernel,
        out_shape=jax.ShapeDtypeStruct((8, 128), jnp.float32),
        grid=(count // 4,),
        in_specs=[spec, spec],
        out_specs=pl.BlockSpec((8, 128), lambda i: (0, 0)),
        scratch_shapes=[pltpu.VMEM((3, 8, FEATURES), jnp.float32)],
        compiler_params=pltpu.CompilerParams(vmem_limit_bytes=LIMIT),
        cost_estimate=pl.CostEstimate(
            flops=6 * a.size, bytes_accessed=8 * a.size, transcendentals=0
        ),
    )(a, b)


def gram_kernel(v_ref, o_ref, t_ref):
    t_ref[...] = jnp.zeros_like(t_ref)
    for gi in range(4):
        for gj in range(gi, 4):
            pairs = [
                (i, j)
                for i in range(4 * gi, 4 * gi + 4)
                for j in range(4 * gj, 4 * gj + 4)
                if i <= j
            ]

            def body(r, sums, pairs=pairs):
                sums = list(sums)
                rows = pl.ds(pl.multiple_of(r * 8, 8), 8)
                for lane in range(FEATURES // 128):
                    held = {}
                    for i, j in pairs:
                        for k in (i, j):
                            if k not in held:
                                held[k] = v_ref[k, rows, pl.ds(lane * 128, 128)]
                    for n, (i, j) in enumerate(pairs):
                        sums[n] = sums[n] + held[i] * held[j]
                return tuple(sums)

            zero = jnp.zeros((8, 128), jnp.float32)
            sums = lax.fori_loop(0, ROWS // 8, body, (zero,) * len(pairs))
            for (i, j), total in zip(pairs, sums):
                t_ref[pl.ds(i * CHIPS + j, 1), :] = jnp.sum(total, axis=0, keepdims=True)
    for part in range(2):
        o_ref[:, pl.ds(part * 128, 128)] = jnp.sum(
            t_ref[pl.ds(part * 128, 128), :].T, axis=0, keepdims=True
        )


def gram(v):
    whole = pl.BlockSpec(memory_space=pltpu.VMEM)
    return pl.pallas_call(
        gram_kernel,
        out_shape=jax.ShapeDtypeStruct((1, CHIPS * CHIPS), jnp.float32),
        in_specs=[whole],
        out_specs=whole,
        scratch_shapes=[pltpu.VMEM((CHIPS * CHIPS, 128), jnp.float32)],
        compiler_params=pltpu.CompilerParams(vmem_limit_bytes=LIMIT),
        cost_estimate=pl.CostEstimate(
            flops=20 << 20, bytes_accessed=4 * v.size, transcendentals=0
        ),
    )(v)


def tree_coefs(read):
    count = CHIPS
    scales = [read(CHIPS * CHIPS + i) for i in range(count)]
    table = {
        (i, j): read(i * CHIPS + j) * (scales[i] * scales[j])
        for i in range(count)
        for j in range(i, count)
    }
    weights = list(scales)
    span = 1
    while count > 1:
        own = []
        for k in range(count // 2):
            cross = table[2 * k, 2 * k + 1]
            own.append(1.0 - cross / (2.0 * (table[2 * k, 2 * k] + EPSILON)))
            own.append(1.0 - cross / (2.0 * (table[2 * k + 1, 2 * k + 1] + EPSILON)))
        weights = [w * own[i // span] for i, w in enumerate(weights)]
        table = {key: value * (own[key[0]] * own[key[1]]) for key, value in table.items()}
        count //= 2
        merged = {}
        for k in range(count):
            merged[k, k] = (
                table[2 * k, 2 * k]
                + 2.0 * table[2 * k, 2 * k + 1]
                + table[2 * k + 1, 2 * k + 1]
            )
            for m in range(k + 1, count):
                merged[k, m] = (
                    table[2 * k, 2 * m]
                    + table[2 * k, 2 * m + 1]
                    + table[2 * k + 1, 2 * m]
                    + table[2 * k + 1, 2 * m + 1]
                )
        table = merged
        span *= 2
    return weights


def update_kernel(totals_ref, v_ref, weight_ref, moment_ref, new_weight_ref, new_moment_ref, coef_ref):
    @pl.when(pl.program_id(0) == 0)
    def _():
        for i, w in enumerate(tree_coefs(lambda n: totals_ref[n])):
            coef_ref[i] = w

    merged = coef_ref[0] * v_ref[0]
    for i in range(1, CHIPS):
        merged = merged + coef_ref[i] * v_ref[i]
    moment = MOMENTUM_DECAY * moment_ref[...] + merged
    new_moment_ref[...] = moment
    new_weight_ref[...] = weight_ref[...] - STEP_SIZE * moment


def update(totals, v, weight, moment):
    step = 16
    rows = pl.BlockSpec((step, FEATURES), lambda i: (i, 0))
    out = jax.ShapeDtypeStruct(weight.shape, jnp.float32)
    return pl.pallas_call(
        update_kernel,
        out_shape=(out, out),
        grid=(ROWS // step,),
        in_specs=[
            pl.BlockSpec(memory_space=pltpu.SMEM),
            pl.BlockSpec((CHIPS, step, FEATURES), lambda i: (0, i, 0)),
            rows,
            rows,
        ],
        out_specs=[rows, rows],
        scratch_shapes=[pltpu.SMEM((CHIPS,), jnp.float32)],
        compiler_params=pltpu.CompilerParams(vmem_limit_bytes=LIMIT),
        cost_estimate=pl.CostEstimate(
            flops=2 * v.size, bytes_accessed=4 * v.size, transcendentals=0
        ),
    )(totals, v, weight, moment)


def summed(vector, axes, groups, count):
    copies = jnp.broadcast_to(vector[None], (count,) + vector.shape)
    arrived = lax.all_to_all(copies, axes, 0, 0, axis_index_groups=groups)
    return jnp.sum(arrived, axis=0)


def shards(
    tokens, key_cotangent, value_cotangent, key_weight, value_weight, key_moment, value_moment
):
    shard_count, replicas = lax.axis_size("shard"), lax.axis_size("rep")
    index = lax.axis_index("rep")
    core = (index & 1).astype(jnp.int32)
    chip = index >> 1
    is_first = core == 0
    half = tokens.shape[1] // 2
    swap = [(i, i ^ 1) for i in range(replicas)]
    chip_groups = [
        [s * replicas + 2 * i + c for s in range(shard_count) for c in range(2)]
        for i in range(CHIPS)
    ]
    core_groups = [list(range(c, replicas, 2)) for c in range(2)]
    leader = (lax.axis_index("shard") == 0) & is_first
    place = jnp.where((jnp.arange(128) == chip) & leader, 1.0, 0.0)[None]

    def pair_merge(own, arrived):
        sums = pair_sums(own, arrived)[:3]
        ordered = jnp.stack(
            [
                sums[0],
                jnp.where(is_first, sums[1], sums[2]),
                jnp.where(is_first, sums[2], sums[1]),
            ]
        )
        cross, p, q = summed(ordered, ("shard", "rep"), chip_groups, 2 * shard_count)[:, 0]
        a = 1.0 - cross / (2.0 * (p + EPSILON))
        b = 1.0 - cross / (2.0 * (q + EPSILON))
        squares = a * a * p + b * b * q
        square = jnp.maximum(squares + 2.0 * a * b * cross, 1e-6 * squares)
        norm = jnp.sqrt(jnp.maximum(square, 1e-30))
        scale = SENT_NORM / norm
        own_coef = jnp.where(is_first, a, b) * scale
        other_coef = jnp.where(is_first, b, a) * scale
        merged = (own_coef * own + other_coef * arrived).astype(jnp.float16)
        return merged, norm * (1.0 / SENT_NORM)

    def gathered(merged):
        return lax.all_to_all(merged, "rep", 0, 0, axis_index_groups=core_groups)

    def finish(arrived, norm, weight, moment):
        v = arrived.astype(jnp.float32)
        vector = jnp.concatenate([gram(v), norm * place], axis=1)
        totals = summed(vector, ("shard", "rep"), None, shard_count * replicas)[0]
        return update(totals, v, weight, moment)

    cores = core[None]
    key_own, key_other = half_grads(cores, tokens, key_cotangent, 0, 2 * half)
    key_arrived = lax.ppermute(key_other, "rep", swap)
    value_own, value_other = half_grads(cores, tokens, value_cotangent, 0, 2 * half)
    value_arrived = lax.ppermute(value_other, "rep", swap)
    key_merged, key_norm = pair_merge(key_own, key_arrived)
    key_all = gathered(key_merged)
    value_merged, value_norm = pair_merge(value_own, value_arrived)
    value_all = gathered(value_merged)
    new_key_weight, new_key_moment = finish(key_all, key_norm, key_weight, key_moment)
    new_value_weight, new_value_moment = finish(value_all, value_norm, value_weight, value_moment)
    return (new_key_weight, new_value_weight, new_key_moment, new_value_moment)


def solution(mesh):
    in_specs = (
        P("rep", "shard"),
        P("rep", None),
        P("rep", None),
        P(("shard", "rep"), None),
        P(("shard", "rep"), None),
        P(("shard", "rep"), None),
        P(("shard", "rep"), None),
    )
    out_specs = (
        P(("shard", "rep"), None),
        P(("shard", "rep"), None),
        P(("shard", "rep"), None),
        P(("shard", "rep"), None),
    )
    return jax.shard_map(shards, mesh=mesh, in_specs=in_specs, out_specs=out_specs, check_vma=False)
```

```python
import functools
import math

import jax
import jax.numpy as jnp
from jax import lax
from jax.experimental import pallas as pl
from jax.experimental.pallas import tpu as pltpu
from jax.sharding import PartitionSpec as P

EPSILON = 1e-06
MOMENTUM_DECAY = 0.9
STEP_SIZE = 0.01
CHIPS = 16
ROWS = 64
FEATURES = 1024
SENT_NORM = 16384.0
MIB = 1 << 20
PAIRS = {pair: n for n, pair in enumerate((i, j) for i in range(CHIPS) for j in range(i, CHIPS))}


def params(mib):
    return pltpu.CompilerParams(vmem_limit_bytes=mib * MIB)


def cost(flops, moved):
    return pl.CostEstimate(flops=flops, bytes_accessed=moved, transcendentals=0)


VMEM = pl.BlockSpec(memory_space=pltpu.VMEM)
SMEM = pl.BlockSpec(memory_space=pltpu.SMEM)


def scaled_dot(rows, cotangent):
    product = jnp.dot(rows, cotangent, preferred_element_type=jnp.float32)
    return (product * (1.0 / math.sqrt(rows.shape[1]))).reshape(-1, ROWS, FEATURES)


def split_kernel(core_ref, x_hbm, y_hbm, grad_ref, own_ref, other_ref, x_ref, y_ref, x_sems, y_sem):
    steps, depth, width = x_ref.shape
    x_copies = [
        pltpu.make_async_copy(x_hbm.at[:, pl.ds(i * width, width)], x_ref.at[i], x_sems.at[i])
        for i in range(steps)
    ]
    y_copy = pltpu.make_async_copy(y_hbm, y_ref, y_sem)
    x_copies[0].start()
    y_copy.start()
    for copy in x_copies[1:]:
        copy.start()
    is_first = core_ref[0] == 0
    half = width // 2
    per = half // ROWS
    for i in range(steps):
        x_copies[i].wait()
        blocks = x_ref[i].T.reshape(-1, 2, ROWS, depth)
        first = blocks[:, 0].reshape(-1, depth)
        second = blocks[:, 1].reshape(-1, depth)
        own_ref[pl.ds(i * half, half), :] = jnp.where(is_first, first, second)
        other = jnp.where(is_first, second, first)
        other_ref[pl.ds(i * half, half), :] = other
        if i == 0:
            y_copy.wait()
        grad_ref[pl.ds(i * per, per)] = scaled_dot(other, y_ref[...])


def split_and_grad(core, tokens, cotangent):
    depth, width = tokens.shape
    step = 512
    half = jax.ShapeDtypeStruct((width // 2, depth), jnp.bfloat16)
    hbm = pl.BlockSpec(memory_space=pltpu.HBM)
    return pl.pallas_call(
        split_kernel,
        out_shape=(jax.ShapeDtypeStruct((CHIPS, ROWS, FEATURES), jnp.float32), half, half),
        in_specs=[SMEM, hbm, hbm],
        out_specs=(VMEM, VMEM, VMEM),
        scratch_shapes=[
            pltpu.VMEM((width // step, depth, step), jnp.bfloat16),
            pltpu.VMEM(cotangent.shape, jnp.bfloat16),
            pltpu.SemaphoreType.DMA((width // step,)),
            pltpu.SemaphoreType.DMA,
        ],
        compiler_params=params(32),
        cost_estimate=cost(depth * width * FEATURES, 24 * MIB),
    )(core, tokens, cotangent)


def grad_kernel(x_ref, y_ref, o_ref):
    step = 256

    @pl.loop(0, x_ref.shape[0] // step)
    def _(i):
        rows = x_ref[pl.ds(pl.multiple_of(i * step, step), step), :]
        o_ref[pl.ds(i * (step // ROWS), step // ROWS)] = scaled_dot(rows, y_ref[...])


def grad(rows, cotangent):
    count, depth = rows.shape
    return pl.pallas_call(
        grad_kernel,
        out_shape=jax.ShapeDtypeStruct((CHIPS, ROWS, FEATURES), jnp.float32),
        in_specs=[VMEM, VMEM],
        out_specs=VMEM,
        compiler_params=params(20),
        cost_estimate=cost(2 * depth * count * FEATURES, 12 * MIB),
    )(rows, cotangent)


def pair_kernel(core_ref, a_ref, b_ref, o_ref, acc_ref):
    step = pl.program_id(0)

    @pl.when(step == 0)
    def _():
        acc_ref[...] = jnp.zeros_like(acc_ref)

    a = a_ref[...].reshape(-1, 8, FEATURES)
    b = b_ref[...].reshape(-1, 8, FEATURES)
    is_first = core_ref[0] == 0
    own, other = jnp.sum(a * a, axis=0), jnp.sum(b * b, axis=0)
    acc_ref[0] += jnp.sum(a * b, axis=0)
    acc_ref[1] += jnp.where(is_first, own, other)
    acc_ref[2] += jnp.where(is_first, other, own)

    @pl.when(step == pl.num_programs(0) - 1)
    def _():
        rows = [jnp.sum(acc_ref[k], axis=0, keepdims=True) for k in range(3)]
        rows = [jnp.sum(row, axis=1, keepdims=True) for row in rows]
        rows = [jnp.broadcast_to(row, (1, 128)) for row in rows]
        tile = jnp.concatenate(rows + [jnp.zeros((5, 128), jnp.float32)], axis=0)
        o_ref[...] = jnp.broadcast_to(tile[None], o_ref.shape)


def pair_sums(core, a, b, copies):
    spec = pl.BlockSpec((4, ROWS, FEATURES), lambda i: (i, 0, 0))
    return pl.pallas_call(
        pair_kernel,
        out_shape=jax.ShapeDtypeStruct((copies, 8, 128), jnp.float32),
        grid=(CHIPS // 4,),
        in_specs=[SMEM, spec, spec],
        out_specs=pl.BlockSpec((copies, 8, 128), lambda i: (0, 0, 0)),
        scratch_shapes=[pltpu.VMEM((3, 8, FEATURES), jnp.float32)],
        compiler_params=params(12),
        cost_estimate=cost(6 * a.size, 8 * a.size),
    )(core, a, b)


def merge_kernel(core_ref, a_ref, b_ref, *refs):
    sums_refs, (o_ref, norm_ref) = refs[:-2], refs[-2:]
    sums = sum(jnp.sum(ref[...], axis=0) for ref in sums_refs)
    cross, p, q = sums[0:1], sums[1:2], sums[2:3]
    is_first = core_ref[0] == 0
    first = 1.0 - cross / (2.0 * (p + EPSILON))
    second = 1.0 - cross / (2.0 * (q + EPSILON))
    squares = first * first * p + second * second * q
    square = jnp.maximum(squares + 2.0 * first * second * cross, 1e-6 * squares)
    norm = jnp.sqrt(jnp.maximum(square, 1e-30))
    scale = SENT_NORM / norm
    norm_ref[...] = jnp.broadcast_to(norm * (1.0 / SENT_NORM), norm_ref.shape)
    own = jnp.where(is_first, first, second) * scale
    other = jnp.where(is_first, second, first) * scale
    own = jnp.concatenate([own] * (FEATURES // 128), axis=1)[None]
    other = jnp.concatenate([other] * (FEATURES // 128), axis=1)[None]
    o_ref[...] = own * a_ref[...] + other * b_ref[...]


def merge_pair(core, a, b, sums):
    spec = pl.BlockSpec((4, ROWS, FEATURES), lambda i: (i, 0, 0))
    return pl.pallas_call(
        merge_kernel,
        out_shape=(
            jax.ShapeDtypeStruct(a.shape, jnp.float32),
            jax.ShapeDtypeStruct((8, 128), jnp.float32),
        ),
        grid=(CHIPS // 4,),
        in_specs=[SMEM, spec, spec] + [VMEM] * len(sums),
        out_specs=(spec, pl.BlockSpec((8, 128), lambda i: (0, 0))),
        compiler_params=params(12),
        cost_estimate=cost(3 * a.size, 12 * a.size),
    )(core, a, b, *sums)


def gram_kernel(place_ref, v_ref, norm_ref, *refs):
    earlier_refs, (o_ref, t_ref) = refs[:-2], refs[-2:]
    t_ref[...] = jnp.zeros_like(t_ref)
    for gi in range(4):
        for gj in range(gi, 4):
            pairs = [
                (i, j)
                for i in range(4 * gi, 4 * gi + 4)
                for j in range(4 * gj, 4 * gj + 4)
                if i <= j
            ]

            def body(r, sums, pairs=pairs):
                sums = list(sums)
                rows = pl.ds(pl.multiple_of(r * 8, 8), 8)
                for lane in range(FEATURES // 128):
                    held = {}
                    for i, j in pairs:
                        for k in (i, j):
                            if k not in held:
                                held[k] = v_ref[k, rows, pl.ds(lane * 128, 128)]
                    for n, (i, j) in enumerate(pairs):
                        sums[n] = sums[n] + held[i] * held[j]
                return tuple(sums)

            zero = jnp.zeros((8, 128), jnp.float32)
            sums = lax.fori_loop(0, ROWS // 8, body, (zero,) * len(pairs))
            for pair, total in zip(pairs, sums):
                t_ref[pl.ds(PAIRS[pair], 1), :] = jnp.sum(total, axis=0, keepdims=True)
    lane = lax.broadcasted_iota(jnp.int32, (1, 128), 1)
    shown = (lane == 0) & (place_ref[1] == 1)
    t_ref[pl.ds(len(PAIRS) + place_ref[0], 1), :] = jnp.where(shown, norm_ref[0:1, :], 0.0)
    rows = [ref[...] for ref in earlier_refs]
    for part in range(2):
        rows.append(jnp.sum(t_ref[pl.ds(part * 128, 128), :].T, axis=0, keepdims=True))
    tile = jnp.concatenate(rows, axis=0)
    o_ref[...] = tile if o_ref.ndim == 2 else jnp.broadcast_to(tile[None], o_ref.shape)


def gram(place, v, norm, earlier, out_dims):
    return pl.pallas_call(
        gram_kernel,
        out_shape=jax.ShapeDtypeStruct(out_dims, jnp.float32),
        in_specs=[SMEM] + [VMEM] * (2 + len(earlier)),
        out_specs=VMEM,
        scratch_shapes=[pltpu.VMEM((256, 128), jnp.float32)],
        compiler_params=params(16),
        cost_estimate=cost(20 << 20, 4 * v.size),
    )(place, v, norm, *earlier)


def tree_coefs(read):
    count = CHIPS
    scales = [read(len(PAIRS) + i) for i in range(count)]
    table = {
        (i, j): read(PAIRS[i, j]) * (scales[i] * scales[j])
        for i in range(count)
        for j in range(i, count)
    }
    weights = list(scales)
    span = 1
    while count > 1:
        own = []
        for k in range(count // 2):
            cross = table[2 * k, 2 * k + 1]
            own.append(1.0 - cross / (2.0 * (table[2 * k, 2 * k] + EPSILON)))
            own.append(1.0 - cross / (2.0 * (table[2 * k + 1, 2 * k + 1] + EPSILON)))
        weights = [w * own[i // span] for i, w in enumerate(weights)]
        table = {key: value * (own[key[0]] * own[key[1]]) for key, value in table.items()}
        count //= 2
        merged = {}
        for k in range(count):
            merged[k, k] = (
                table[2 * k, 2 * k]
                + 2.0 * table[2 * k, 2 * k + 1]
                + table[2 * k + 1, 2 * k + 1]
            )
            for m in range(k + 1, count):
                merged[k, m] = (
                    table[2 * k, 2 * m]
                    + table[2 * k, 2 * m + 1]
                    + table[2 * k + 1, 2 * m]
                    + table[2 * k + 1, 2 * m + 1]
                )
        table = merged
        span *= 2
    return weights


def update_kernel(totals_ref, *refs):
    ins, outs, coef_ref = refs[:6], refs[6:10], refs[10]

    @pl.when(pl.program_id(0) == 0)
    def _():
        for t in range(2):
            weights = tree_coefs(lambda n, t=t: totals_ref[2 * t + n // 128, n % 128])
            for i, w in enumerate(weights):
                coef_ref[t * CHIPS + i] = w

    for t in range(2):
        v_ref, weight_ref, moment_ref = ins[3 * t : 3 * t + 3]
        new_weight_ref, new_moment_ref = outs[2 * t : 2 * t + 2]
        merged = coef_ref[t * CHIPS] * v_ref[0]
        for i in range(1, CHIPS):
            merged = merged + coef_ref[t * CHIPS + i] * v_ref[i]
        moment = MOMENTUM_DECAY * moment_ref[...] + merged
        new_moment_ref[...] = moment
        new_weight_ref[...] = weight_ref[...] - STEP_SIZE * moment


def update(totals, *arrays):
    step = 16
    rows = pl.BlockSpec((step, FEATURES), lambda i: (i, 0))
    whole = pl.BlockSpec((CHIPS, step, FEATURES), lambda i: (0, i, 0))
    out = jax.ShapeDtypeStruct((ROWS, FEATURES), jnp.float32)
    return pl.pallas_call(
        update_kernel,
        out_shape=(out,) * 4,
        grid=(ROWS // step,),
        in_specs=[SMEM] + [whole, rows, rows] * 2,
        out_specs=(rows,) * 4,
        scratch_shapes=[pltpu.SMEM((2 * CHIPS,), jnp.float32)],
        compiler_params=params(60),
        cost_estimate=cost(8 << 20, 10 * MIB),
    )(totals, *arrays)


def after(value, *others):
    return lax.optimization_barrier((value,) + others)[0]


def shards(
    tokens, key_cotangent, value_cotangent, key_weight, value_weight, key_moment, value_moment
):
    shard_count, replicas = lax.axis_size("shard"), lax.axis_size("rep")
    index = lax.axis_index("rep").astype(jnp.int32)
    core = (index & 1)[None]
    leader = ((lax.axis_index("shard") == 0) & (index & 1 == 0)).astype(jnp.int32)
    place = jnp.stack([index >> 1, leader])
    swap = [(i, i ^ 1) for i in range(replicas)]
    core_groups = [list(range(c, replicas, 2)) for c in range(2)]

    def summed(sums):
        sums = sums + lax.ppermute(sums, "rep", swap)
        shifts = [
            [(s, (s + d) % shard_count) for s in range(shard_count)] for d in range(1, shard_count)
        ]
        return [sums] + [lax.ppermute(sums, "shard", shift) for shift in shifts]

    def gathered(merged):
        sent = merged.astype(jnp.float16)
        return lax.all_to_all(sent, "rep", 0, 0, axis_index_groups=core_groups)

    key_other, own_rows, other_rows = split_and_grad(core, tokens, key_cotangent)
    key_arrived = lax.ppermute(key_other, "rep", swap)
    key_own = grad(own_rows, key_cotangent)
    key_sums = summed(pair_sums(core, key_own, key_arrived, 1))
    value_other = grad(other_rows, value_cotangent)
    value_arrived = lax.ppermute(value_other, "rep", swap)
    key_merged, key_norm = merge_pair(core, key_own, key_arrived, key_sums)
    key_all = gathered(key_merged)

    value_own = grad(after(own_rows, key_merged), value_cotangent)
    value_sums = summed(pair_sums(core, value_own, value_arrived, 1))
    value_merged, value_norm = merge_pair(core, value_own, value_arrived, value_sums)
    value_all = gathered(value_merged)

    key_v = key_all.astype(jnp.float32)
    key_vector = gram(place, key_v, key_norm, [], (2, 128))
    value_v = value_all.astype(jnp.float32)
    vectors = gram(place, value_v, value_norm, [key_vector], (shard_count * replicas, 4, 128))
    totals = jnp.sum(lax.all_to_all(vectors, ("shard", "rep"), 0, 0), axis=0)
    new_key_weight, new_key_moment, new_value_weight, new_value_moment = update(
        totals, key_v, key_weight, key_moment, value_v, value_weight, value_moment
    )
    return (new_key_weight, new_value_weight, new_key_moment, new_value_moment)


def solution(mesh):
    in_specs = (
        P("rep", "shard"),
        P("rep", None),
        P("rep", None),
        P(("shard", "rep"), None),
        P(("shard", "rep"), None),
        P(("shard", "rep"), None),
        P(("shard", "rep"), None),
    )
    out_specs = (
        P(("shard", "rep"), None),
        P(("shard", "rep"), None),
        P(("shard", "rep"), None),
        P(("shard", "rep"), None),
    )
    return jax.shard_map(shards, mesh=mesh, in_specs=in_specs, out_specs=out_specs, check_vma=False)
```

```python
import functools
import math

import jax
import jax.numpy as jnp
from jax import lax
from jax.experimental import pallas as pl
from jax.experimental.pallas import tpu as pltpu
from jax.sharding import PartitionSpec as P

EPSILON = 1e-06
MOMENTUM_DECAY = 0.9
STEP_SIZE = 0.01
CHIPS = 16
ROWS = 64
FEATURES = 1024
SENT_NORM = 16384.0
MIB = 1 << 20
PAIRS = {pair: n for n, pair in enumerate((i, j) for i in range(CHIPS) for j in range(i, CHIPS))}


def params(mib):
    return pltpu.CompilerParams(vmem_limit_bytes=mib * MIB)


def cost(flops, moved):
    return pl.CostEstimate(flops=flops, bytes_accessed=moved, transcendentals=0)


VMEM = pl.BlockSpec(memory_space=pltpu.VMEM)
SMEM = pl.BlockSpec(memory_space=pltpu.SMEM)


def scaled_dot(rows, cotangent):
    product = jnp.dot(rows, cotangent, preferred_element_type=jnp.float32)
    return (product * (1.0 / math.sqrt(rows.shape[1]))).reshape(-1, ROWS, FEATURES)


def split_part(is_first, x_ref, y_ref, grad_ref, own_ref, other_ref, i):
    depth, width = x_ref.shape
    half = width // 2
    per = half // ROWS
    blocks = x_ref[...].T.reshape(-1, 2, ROWS, depth)
    first = blocks[:, 0].reshape(-1, depth)
    second = blocks[:, 1].reshape(-1, depth)
    own_ref[pl.ds(i * half, half), :] = jnp.where(is_first, first, second)
    other = jnp.where(is_first, second, first)
    other_ref[pl.ds(i * half, half), :] = other
    if callable(y_ref):
        y_ref = y_ref()
    grad_ref[pl.ds(i * per, per)] = scaled_dot(other, y_ref[...])


def split_kernel(core_ref, x_hbm, y_hbm, grad_ref, own_ref, other_ref, y_ref, x_ref, x_sems, y_sem, *, start):
    steps, _, width = x_ref.shape
    x_copies = [
        pltpu.make_async_copy(
            x_hbm.at[:, pl.ds(start + i * width, width)], x_ref.at[i], x_sems.at[i]
        )
        for i in range(steps)
    ]
    y_copy = pltpu.make_async_copy(y_hbm, y_ref, y_sem)
    x_copies[0].start()
    y_copy.start()
    for copy in x_copies[1:]:
        copy.start()
    is_first = core_ref[0] == 0

    def waited():
        y_copy.wait()
        return y_ref

    for i in range(steps):
        x_copies[i].wait()
        y = waited if i == 0 else y_ref
        split_part(is_first, x_ref.at[i], y, grad_ref, own_ref, other_ref, i)


def split_and_grad(core, tokens, cotangent):
    depth, width = tokens.shape
    step = 512
    steps = width // (2 * step)
    half = jax.ShapeDtypeStruct((width // 4, depth), jnp.bfloat16)
    part = jax.ShapeDtypeStruct((CHIPS // 2, ROWS, FEATURES), jnp.float32)
    held = jax.ShapeDtypeStruct(cotangent.shape, jnp.bfloat16)
    hbm = pl.BlockSpec(memory_space=pltpu.HBM)
    halves = []
    for n in range(2):
        scratch = [
            pltpu.VMEM((steps, depth, step), jnp.bfloat16),
            pltpu.SemaphoreType.DMA((steps,)),
            pltpu.SemaphoreType.DMA,
        ]
        halves.append(
            pl.pallas_call(
                functools.partial(split_kernel, start=n * (width // 2)),
                out_shape=(part, half, half) + (held,) * n,
                in_specs=[SMEM, hbm, hbm],
                out_specs=(VMEM,) * (3 + n),
                scratch_shapes=([] if n else [pltpu.VMEM(held.shape, held.dtype)]) + scratch,
                compiler_params=params(42 if n else 52),
                cost_estimate=cost(depth * width * FEATURES // 2, 12 * MIB),
            )(core, tokens, cotangent)
        )
    return [half[:3] for half in halves], halves[1][3]


def grad_kernel(*refs, parts):
    x_refs, y_ref, o_ref = refs[:parts], refs[parts], refs[-1]
    step = 256
    at = 0
    for x_ref in x_refs:
        count = x_ref.shape[0] // step

        @pl.loop(0, count)
        def _(i, x_ref=x_ref, at=at):
            rows = x_ref[pl.ds(pl.multiple_of(i * step, step), step), :]
            per = step // ROWS
            o_ref[pl.ds(at + i * per, per)] = scaled_dot(rows, y_ref[...])

        at += x_ref.shape[0] // ROWS


def grad(rows, cotangent, kept=()):
    depth = cotangent.shape[0]
    count = sum(part.shape[0] for part in rows)
    return pl.pallas_call(
        functools.partial(grad_kernel, parts=len(rows)),
        out_shape=jax.ShapeDtypeStruct((count // ROWS, ROWS, FEATURES), jnp.float32),
        in_specs=[VMEM] * (len(rows) + 1 + len(kept)),
        out_specs=VMEM,
        compiler_params=params(8),
        cost_estimate=cost(count, MIB),
    )(*rows, cotangent, *kept)


def parts_specs(parts):
    steps = parts[0].shape[0] // 4
    return [
        pl.BlockSpec(
            (4, ROWS, FEATURES),
            lambda i, n=n: (jnp.clip(i - n * steps, 0, steps - 1), 0, 0),
        )
        for n in range(len(parts))
    ]


def block_of(refs, steps):
    block = refs[0][...]
    for n in range(1, len(refs)):
        block = jnp.where(pl.program_id(0) >= n * steps, refs[n][...], block)
    return block


def pair_kernel(core_ref, a_ref, *refs, steps):
    b_refs, (o_ref, acc_ref) = refs[:-2], refs[-2:]
    step = pl.program_id(0)

    @pl.when(step == 0)
    def _():
        acc_ref[...] = jnp.zeros_like(acc_ref)

    a = a_ref[...].reshape(-1, 8, FEATURES)
    b = block_of(b_refs, steps).reshape(-1, 8, FEATURES)
    is_first = core_ref[0] == 0
    own, other = jnp.sum(a * a, axis=0), jnp.sum(b * b, axis=0)
    acc_ref[0] += jnp.sum(a * b, axis=0)
    acc_ref[1] += jnp.where(is_first, own, other)
    acc_ref[2] += jnp.where(is_first, other, own)

    @pl.when(step == pl.num_programs(0) - 1)
    def _():
        rows = [jnp.sum(acc_ref[k], axis=0, keepdims=True) for k in range(3)]
        rows = [jnp.sum(row, axis=1, keepdims=True) for row in rows]
        rows = [jnp.broadcast_to(row, (1, 128)) for row in rows]
        tile = jnp.concatenate(rows + [jnp.zeros((5, 128), jnp.float32)], axis=0)
        o_ref[...] = jnp.broadcast_to(tile[None], o_ref.shape)


def pair_sums(core, a, b, copies):
    spec = pl.BlockSpec((4, ROWS, FEATURES), lambda i: (i, 0, 0))
    return pl.pallas_call(
        functools.partial(pair_kernel, steps=b[0].shape[0] // 4),
        out_shape=jax.ShapeDtypeStruct((copies, 8, 128), jnp.float32),
        grid=(CHIPS // 4,),
        in_specs=[SMEM, spec] + parts_specs(b),
        out_specs=pl.BlockSpec((copies, 8, 128), lambda i: (0, 0, 0)),
        scratch_shapes=[pltpu.VMEM((3, 8, FEATURES), jnp.float32)],
        compiler_params=params(10),
        cost_estimate=cost(a.size, a.size),
    )(core, a, *b)


def merge_kernel(core_ref, a_ref, *refs, parts, steps):
    b_refs, sums_refs, (o_ref, norm_ref) = refs[:parts], refs[parts:-2], refs[-2:]
    sums = sum(jnp.sum(ref[...], axis=0) for ref in sums_refs)
    cross, p, q = sums[0:1], sums[1:2], sums[2:3]
    is_first = core_ref[0] == 0
    first = 1.0 - cross / (2.0 * (p + EPSILON))
    second = 1.0 - cross / (2.0 * (q + EPSILON))
    squares = first * first * p + second * second * q
    square = jnp.maximum(squares + 2.0 * first * second * cross, 1e-6 * squares)
    norm = jnp.sqrt(jnp.maximum(square, 1e-30))
    scale = SENT_NORM / norm
    norm_ref[...] = jnp.broadcast_to(norm * (1.0 / SENT_NORM), norm_ref.shape)
    own = jnp.where(is_first, first, second) * scale
    other = jnp.where(is_first, second, first) * scale
    own = jnp.concatenate([own] * (FEATURES // 128), axis=1)[None]
    other = jnp.concatenate([other] * (FEATURES // 128), axis=1)[None]
    o_ref[...] = own * a_ref[...] + other * block_of(b_refs, steps)


def merge_pair(core, a, b, sums):
    spec = pl.BlockSpec((4, ROWS, FEATURES), lambda i: (i, 0, 0))
    return pl.pallas_call(
        functools.partial(merge_kernel, parts=len(b), steps=b[0].shape[0] // 4),
        out_shape=(
            jax.ShapeDtypeStruct(a.shape, jnp.float32),
            jax.ShapeDtypeStruct((8, 128), jnp.float32),
        ),
        grid=(CHIPS // 4,),
        in_specs=[SMEM, spec] + parts_specs(b) + [VMEM] * len(sums),
        out_specs=(spec, pl.BlockSpec((8, 128), lambda i: (0, 0))),
        compiler_params=params(12),
        cost_estimate=cost(a.size, a.size),
    )(core, a, *b, *sums)


def gram_kernel(place_ref, v_ref, norm_ref, *refs):
    earlier_refs, (o_ref, t_ref) = refs[:-2], refs[-2:]

    @pl.when(pl.program_id(0) == 0)
    def _():
        t_ref[...] = jnp.zeros_like(t_ref)

    for gi in range(4):
        for gj in range(gi, 4):
            pairs = [
                (i, j)
                for i in range(4 * gi, 4 * gi + 4)
                for j in range(4 * gj, 4 * gj + 4)
                if i <= j
            ]

            def body(r, sums, pairs=pairs):
                sums = list(sums)
                rows = pl.ds(pl.multiple_of(r * 8, 8), 8)
                for lane in range(FEATURES // 128):
                    held = {}
                    for i, j in pairs:
                        for k in (i, j):
                            if k not in held:
                                held[k] = v_ref[k, rows, pl.ds(lane * 128, 128)]
                    for n, (i, j) in enumerate(pairs):
                        sums[n] = sums[n] + held[i] * held[j]
                return tuple(sums)

            zero = jnp.zeros((8, 128), jnp.float32)
            sums = lax.fori_loop(0, v_ref.shape[1] // 8, body, (zero,) * len(pairs))
            for pair, total in zip(pairs, sums):
                t_ref[pl.ds(PAIRS[pair], 1), :] += jnp.sum(total, axis=0, keepdims=True)

    @pl.when(pl.program_id(0) == pl.num_programs(0) - 1)
    def _():
        lane = lax.broadcasted_iota(jnp.int32, (1, 128), 1)
        shown = (lane == 0) & (place_ref[1] == 1)
        t_ref[pl.ds(len(PAIRS) + place_ref[0], 1), :] = jnp.where(shown, norm_ref[0:1, :], 0.0)
        rows = [ref[...] for ref in earlier_refs]
        for part in range(2):
            rows.append(jnp.sum(t_ref[pl.ds(part * 128, 128), :].T, axis=0, keepdims=True))
        tile = jnp.concatenate(rows, axis=0)
        o_ref[...] = tile if o_ref.ndim == 2 else jnp.broadcast_to(tile[None], o_ref.shape)


def gram(place, v, norm, earlier, out_dims):
    step = 16
    return pl.pallas_call(
        gram_kernel,
        out_shape=jax.ShapeDtypeStruct(out_dims, jnp.float32),
        grid=(ROWS // step,),
        in_specs=[SMEM, pl.BlockSpec((CHIPS, step, FEATURES), lambda i: (0, i, 0))]
        + [VMEM] * (1 + len(earlier)),
        out_specs=VMEM,
        scratch_shapes=[pltpu.VMEM((256, 128), jnp.float32)],
        compiler_params=params(56),
        cost_estimate=cost(20 << 20, 4 * v.size),
    )(place, v, norm, *earlier)


def tree_coefs(read):
    count = CHIPS
    scales = [read(len(PAIRS) + i) for i in range(count)]
    table = {
        (i, j): read(PAIRS[i, j]) * (scales[i] * scales[j])
        for i in range(count)
        for j in range(i, count)
    }
    weights = list(scales)
    span = 1
    while count > 1:
        own = []
        for k in range(count // 2):
            cross = table[2 * k, 2 * k + 1]
            own.append(1.0 - cross / (2.0 * (table[2 * k, 2 * k] + EPSILON)))
            own.append(1.0 - cross / (2.0 * (table[2 * k + 1, 2 * k + 1] + EPSILON)))
        weights = [w * own[i // span] for i, w in enumerate(weights)]
        table = {key: value * (own[key[0]] * own[key[1]]) for key, value in table.items()}
        count //= 2
        merged = {}
        for k in range(count):
            merged[k, k] = (
                table[2 * k, 2 * k]
                + 2.0 * table[2 * k, 2 * k + 1]
                + table[2 * k + 1, 2 * k + 1]
            )
            for m in range(k + 1, count):
                merged[k, m] = (
                    table[2 * k, 2 * m]
                    + table[2 * k, 2 * m + 1]
                    + table[2 * k + 1, 2 * m]
                    + table[2 * k + 1, 2 * m + 1]
                )
        table = merged
        span *= 2
    return weights


def update_kernel(totals_ref, *refs):
    ins, outs, coef_ref = refs[:6], refs[6:10], refs[10]

    @pl.when(pl.program_id(0) == 0)
    def _():
        for t in range(2):
            weights = tree_coefs(lambda n, t=t: totals_ref[2 * t + n // 128, n % 128])
            for i, w in enumerate(weights):
                coef_ref[t * CHIPS + i] = w

    for t in range(2):
        v_ref, weight_ref, moment_ref = ins[3 * t : 3 * t + 3]
        new_weight_ref, new_moment_ref = outs[2 * t : 2 * t + 2]
        merged = coef_ref[t * CHIPS] * v_ref[0]
        for i in range(1, CHIPS):
            merged = merged + coef_ref[t * CHIPS + i] * v_ref[i]
        moment = MOMENTUM_DECAY * moment_ref[...] + merged
        new_moment_ref[...] = moment
        new_weight_ref[...] = weight_ref[...] - STEP_SIZE * moment


def update(totals, *arrays):
    step = 16
    rows = pl.BlockSpec((step, FEATURES), lambda i: (i, 0))
    whole = pl.BlockSpec((CHIPS, step, FEATURES), lambda i: (0, i, 0))
    out = jax.ShapeDtypeStruct((ROWS, FEATURES), jnp.float32)
    return pl.pallas_call(
        update_kernel,
        out_shape=(out,) * 4,
        grid=(ROWS // step,),
        in_specs=[SMEM] + [whole, rows, rows] * 2,
        out_specs=(rows,) * 4,
        scratch_shapes=[pltpu.SMEM((2 * CHIPS,), jnp.float32)],
        compiler_params=params(60),
        cost_estimate=cost(8 << 20, 10 * MIB),
    )(totals, *arrays)


def after(value, *others):
    return lax.optimization_barrier((value,) + others)[0]


def shards(
    tokens, key_cotangent, value_cotangent, key_weight, value_weight, key_moment, value_moment
):
    shard_count, replicas = lax.axis_size("shard"), lax.axis_size("rep")
    index = lax.axis_index("rep").astype(jnp.int32)
    core = (index & 1)[None]
    leader = ((lax.axis_index("shard") == 0) & (index & 1 == 0)).astype(jnp.int32)
    place = jnp.stack([index >> 1, leader])
    swap = [(i, i ^ 1) for i in range(replicas)]
    core_groups = [list(range(c, replicas, 2)) for c in range(2)]

    def summed(sums):
        sums = sums + lax.ppermute(sums, "rep", swap)
        shifts = [
            [(s, (s + d) % shard_count) for s in range(shard_count)] for d in range(1, shard_count)
        ]
        return [sums] + [lax.ppermute(sums, "shard", shift) for shift in shifts]

    def gathered(sent):
        return lax.all_to_all(sent, "rep", 0, 0, axis_index_groups=core_groups)

    halves, key_cotangent = split_and_grad(core, tokens, key_cotangent)
    own_rows = [half[1] for half in halves]
    other_rows = [half[2] for half in halves]
    key_arrived = [lax.ppermute(half[0], "rep", swap) for half in halves]
    key_own = grad(own_rows, key_cotangent)
    key_sums = summed(pair_sums(core, key_own, key_arrived, 1))
    value_other = grad(after(other_rows, key_sums[0]), value_cotangent, [key_own] + key_arrived)
    key_merged, key_norm = merge_pair(core, key_own, key_arrived, key_sums)
    key_sent = key_merged.astype(jnp.float16)
    key_all = gathered(key_sent)

    value_arrived = [lax.ppermute(after(value_other, key_sent), "rep", swap)]
    value_own = grad(after(own_rows, key_sent), value_cotangent)
    value_sums = summed(pair_sums(core, value_own, value_arrived, 1))
    value_merged, value_norm = merge_pair(core, value_own, value_arrived, value_sums)
    value_all = gathered(value_merged.astype(jnp.float16))

    key_v = key_all.astype(jnp.float32)
    key_vector = gram(place, key_v, key_norm, [], (2, 128))
    value_v = value_all.astype(jnp.float32)
    vectors = gram(place, value_v, value_norm, [key_vector], (shard_count * replicas, 4, 128))
    totals = jnp.sum(lax.all_to_all(vectors, ("shard", "rep"), 0, 0), axis=0)
    new_key_weight, new_key_moment, new_value_weight, new_value_moment = update(
        totals, key_v, key_weight, key_moment, value_v, value_weight, value_moment
    )
    return (new_key_weight, new_value_weight, new_key_moment, new_value_moment)


def solution(mesh):
    in_specs = (
        P("rep", "shard"),
        P("rep", None),
        P("rep", None),
        P(("shard", "rep"), None),
        P(("shard", "rep"), None),
        P(("shard", "rep"), None),
        P(("shard", "rep"), None),
    )
    out_specs = (
        P(("shard", "rep"), None),
        P(("shard", "rep"), None),
        P(("shard", "rep"), None),
        P(("shard", "rep"), None),
    )
    return jax.shard_map(shards, mesh=mesh, in_specs=in_specs, out_specs=out_specs, check_vma=False)
```

```python
import functools
import math

import jax
import jax.numpy as jnp
from jax import lax
from jax.experimental import pallas as pl
from jax.experimental.pallas import tpu as pltpu
from jax.sharding import PartitionSpec as P

EPSILON = 1e-06
MOMENTUM_DECAY = 0.9
STEP_SIZE = 0.01
CHIPS = 16
ROWS = 64
FEATURES = 1024
SENT_NORM = 16384.0
MIB = 1 << 20
PAIRS = {pair: n for n, pair in enumerate((i, j) for i in range(CHIPS) for j in range(i, CHIPS))}


def params(mib):
    return pltpu.CompilerParams(vmem_limit_bytes=mib * MIB)


def cost(flops, moved):
    return pl.CostEstimate(flops=flops, bytes_accessed=moved, transcendentals=0)


VMEM = pl.BlockSpec(memory_space=pltpu.VMEM)
SMEM = pl.BlockSpec(memory_space=pltpu.SMEM)


def scaled_dot(rows, cotangent):
    product = jnp.dot(rows, cotangent, preferred_element_type=jnp.float32)
    return (product * (1.0 / math.sqrt(rows.shape[1]))).reshape(-1, ROWS, FEATURES)


def split_kernel(core_ref, x_hbm, y_hbm, grad_ref, own_ref, other_ref, y_ref, x_ref, x_sems, y_sem):
    steps, depth, width = x_ref.shape
    x_copies = [
        pltpu.make_async_copy(x_hbm.at[:, pl.ds(i * width, width)], x_ref.at[i], x_sems.at[i])
        for i in range(steps)
    ]
    y_copy = pltpu.make_async_copy(y_hbm, y_ref, y_sem)
    x_copies[0].start()
    y_copy.start()
    for copy in x_copies[1:]:
        copy.start()
    is_first = core_ref[0] == 0
    half = width // 2
    per = half // ROWS
    for i in range(steps):
        x_copies[i].wait()
        blocks = x_ref[i].T.reshape(-1, 2, ROWS, depth)
        first = blocks[:, 0].reshape(-1, depth)
        second = blocks[:, 1].reshape(-1, depth)
        own_ref[pl.ds(i * half, half), :] = jnp.where(is_first, first, second)
        other = jnp.where(is_first, second, first)
        other_ref[pl.ds(i * half, half), :] = other
        if i == 0:
            y_copy.wait()
        grad_ref[pl.ds(i * per, per)] = scaled_dot(other, y_ref[...])


def split_and_grad(core, tokens, cotangent):
    depth, width = tokens.shape
    step = 512
    half = jax.ShapeDtypeStruct((width // 2, depth), jnp.bfloat16)
    hbm = pl.BlockSpec(memory_space=pltpu.HBM)
    return pl.pallas_call(
        split_kernel,
        out_shape=(
            jax.ShapeDtypeStruct((CHIPS, ROWS, FEATURES), jnp.float32),
            half,
            half,
            jax.ShapeDtypeStruct(cotangent.shape, jnp.bfloat16),
        ),
        in_specs=[SMEM, hbm, hbm],
        out_specs=(VMEM,) * 4,
        scratch_shapes=[
            pltpu.VMEM((width // step, depth, step), jnp.bfloat16),
            pltpu.SemaphoreType.DMA((width // step,)),
            pltpu.SemaphoreType.DMA,
        ],
        compiler_params=params(41),
        cost_estimate=cost(depth * width * FEATURES, 24 * MIB),
    )(core, tokens, cotangent)


def grad_kernel(x_ref, y_ref, *refs, start):
    o_ref = refs[-1]
    step = 256
    per = step // ROWS

    @pl.loop(0, o_ref.shape[0] // per)
    def _(i):
        rows = x_ref[pl.ds(pl.multiple_of(start + i * step, step), step), :]
        o_ref[pl.ds(i * per, per)] = scaled_dot(rows, y_ref[...])


def grad(rows, cotangent, start=0, count=None, kept=()):
    count = count or rows.shape[0]
    return pl.pallas_call(
        functools.partial(grad_kernel, start=start),
        out_shape=jax.ShapeDtypeStruct((count // ROWS, ROWS, FEATURES), jnp.float32),
        in_specs=[VMEM] * (2 + len(kept)),
        out_specs=VMEM,
        compiler_params=params(8),
        cost_estimate=cost(2 * cotangent.shape[0] * count * FEATURES, 12 * MIB),
    )(rows, cotangent, *kept)


def parts_specs(parts):
    steps = parts[0].shape[0] // 4
    return [
        pl.BlockSpec(
            (4, ROWS, FEATURES),
            lambda i, n=n: (jnp.clip(i - n * steps, 0, steps - 1), 0, 0),
        )
        for n in range(len(parts))
    ]


def block_of(refs, steps):
    block = refs[0][...]
    for n in range(1, len(refs)):
        block = jnp.where(pl.program_id(0) >= n * steps, refs[n][...], block)
    return block


def pair_kernel(core_ref, a_ref, *refs, steps):
    b_refs, (o_ref, acc_ref) = refs[:-2], refs[-2:]
    step = pl.program_id(0)

    @pl.when(step == 0)
    def _():
        acc_ref[...] = jnp.zeros_like(acc_ref)

    a = a_ref[...].reshape(-1, 8, FEATURES)
    b = block_of(b_refs, steps).reshape(-1, 8, FEATURES)
    is_first = core_ref[0] == 0
    own, other = jnp.sum(a * a, axis=0), jnp.sum(b * b, axis=0)
    acc_ref[0] += jnp.sum(a * b, axis=0)
    acc_ref[1] += jnp.where(is_first, own, other)
    acc_ref[2] += jnp.where(is_first, other, own)

    @pl.when(step == pl.num_programs(0) - 1)
    def _():
        rows = [jnp.sum(acc_ref[k], axis=0, keepdims=True) for k in range(3)]
        rows = [jnp.sum(row, axis=1, keepdims=True) for row in rows]
        rows = [jnp.broadcast_to(row, (1, 128)) for row in rows]
        tile = jnp.concatenate(rows + [jnp.zeros((5, 128), jnp.float32)], axis=0)
        o_ref[...] = jnp.broadcast_to(tile[None], o_ref.shape)


def pair_sums(core, a, b, copies):
    spec = pl.BlockSpec((4, ROWS, FEATURES), lambda i: (i, 0, 0))
    return pl.pallas_call(
        functools.partial(pair_kernel, steps=b[0].shape[0] // 4),
        out_shape=jax.ShapeDtypeStruct((copies, 8, 128), jnp.float32),
        grid=(CHIPS // 4,),
        in_specs=[SMEM, spec] + parts_specs(b),
        out_specs=pl.BlockSpec((copies, 8, 128), lambda i: (0, 0, 0)),
        scratch_shapes=[pltpu.VMEM((3, 8, FEATURES), jnp.float32)],
        compiler_params=params(10),
        cost_estimate=cost(a.size, a.size),
    )(core, a, *b)


def merge_kernel(core_ref, a_ref, *refs, parts, steps):
    b_refs, sums_refs, (o_ref, norm_ref) = refs[:parts], refs[parts:-2], refs[-2:]
    sums = sum(jnp.sum(ref[...], axis=0) for ref in sums_refs)
    cross, p, q = sums[0:1], sums[1:2], sums[2:3]
    is_first = core_ref[0] == 0
    first = 1.0 - cross / (2.0 * (p + EPSILON))
    second = 1.0 - cross / (2.0 * (q + EPSILON))
    squares = first * first * p + second * second * q
    square = jnp.maximum(squares + 2.0 * first * second * cross, 1e-6 * squares)
    norm = jnp.sqrt(jnp.maximum(square, 1e-30))
    scale = SENT_NORM / norm
    norm_ref[...] = jnp.broadcast_to(norm * (1.0 / SENT_NORM), norm_ref.shape)
    own = jnp.where(is_first, first, second) * scale
    other = jnp.where(is_first, second, first) * scale
    own = jnp.concatenate([own] * (FEATURES // 128), axis=1)[None]
    other = jnp.concatenate([other] * (FEATURES // 128), axis=1)[None]
    o_ref[...] = own * a_ref[...] + other * block_of(b_refs, steps)


def merge_pair(core, a, b, sums):
    spec = pl.BlockSpec((4, ROWS, FEATURES), lambda i: (i, 0, 0))
    return pl.pallas_call(
        functools.partial(merge_kernel, parts=len(b), steps=b[0].shape[0] // 4),
        out_shape=(
            jax.ShapeDtypeStruct(a.shape, jnp.float32),
            jax.ShapeDtypeStruct((8, 128), jnp.float32),
        ),
        grid=(CHIPS // 4,),
        in_specs=[SMEM, spec] + parts_specs(b) + [VMEM] * len(sums),
        out_specs=(spec, pl.BlockSpec((8, 128), lambda i: (0, 0))),
        compiler_params=params(12),
        cost_estimate=cost(a.size, a.size),
    )(core, a, *b, *sums)


def gram_kernel(place_ref, v_ref, norm_ref, *refs):
    earlier_refs, (o_ref, sums_ref, t_ref) = refs[:-3], refs[-3:]

    @pl.when(pl.program_id(0) == 0)
    def _():
        sums_ref[...] = jnp.zeros_like(sums_ref)

    for gi in range(4):
        for gj in range(gi, 4):
            pairs = [
                (i, j)
                for i in range(4 * gi, 4 * gi + 4)
                for j in range(4 * gj, 4 * gj + 4)
                if i <= j
            ]

            def body(r, sums, pairs=pairs):
                sums = list(sums)
                rows = pl.ds(pl.multiple_of(r * 8, 8), 8)
                for lane in range(FEATURES // 128):
                    held = {}
                    for i, j in pairs:
                        for k in (i, j):
                            if k not in held:
                                held[k] = v_ref[k, rows, pl.ds(lane * 128, 128)]
                    for n, (i, j) in enumerate(pairs):
                        sums[n] = sums[n] + held[i] * held[j]
                return tuple(sums)

            zero = jnp.zeros((8, 128), jnp.float32)
            sums = lax.fori_loop(0, v_ref.shape[1] // 8, body, (zero,) * len(pairs))
            for pair, total in zip(pairs, sums):
                sums_ref[PAIRS[pair]] += total

    @pl.when(pl.program_id(0) == pl.num_programs(0) - 1)
    def _():
        t_ref[pl.ds(0, len(PAIRS)), :] = jnp.sum(sums_ref[...], axis=1)
        t_ref[pl.ds(len(PAIRS), 256 - len(PAIRS)), :] = jnp.zeros((256 - len(PAIRS), 128), jnp.float32)
        lane = lax.broadcasted_iota(jnp.int32, (1, 128), 1)
        shown = (lane == 0) & (place_ref[1] == 1)
        t_ref[pl.ds(len(PAIRS) + place_ref[0], 1), :] = jnp.where(shown, norm_ref[0:1, :], 0.0)
        rows = [ref[...] for ref in earlier_refs]
        for part in range(2):
            rows.append(jnp.sum(t_ref[pl.ds(part * 128, 128), :].T, axis=0, keepdims=True))
        tile = jnp.concatenate(rows, axis=0)
        o_ref[...] = tile if o_ref.ndim == 2 else jnp.broadcast_to(tile[None], o_ref.shape)


def gram(place, v, norm, earlier, out_dims):
    step = 16
    return pl.pallas_call(
        gram_kernel,
        out_shape=jax.ShapeDtypeStruct(out_dims, jnp.float32),
        grid=(ROWS // step,),
        in_specs=[SMEM, pl.BlockSpec((CHIPS, step, FEATURES), lambda i: (0, i, 0))]
        + [VMEM] * (1 + len(earlier)),
        out_specs=VMEM,
        scratch_shapes=[
            pltpu.VMEM((len(PAIRS), 8, 128), jnp.float32),
            pltpu.VMEM((256, 128), jnp.float32),
        ],
        compiler_params=params(56),
        cost_estimate=cost(20 << 20, 4 * v.size),
    )(place, v, norm, *earlier)


def tree_coefs(read):
    count = CHIPS
    norms = [read(len(PAIRS) + i) for i in range(count)]
    table = {pair: read(n) for pair, n in PAIRS.items()}
    weights = list(norms)
    span = 1
    while count > 1:
        own = []
        for k in range(0, count, 2):
            cross = table[k, k + 1] * (norms[k] * norms[k + 1])
            for m in (k, k + 1):
                square = table[m, m] * (norms[m] * norms[m])
                own.append(1.0 - cross / (2.0 * (square + EPSILON)))
        weights = [w * own[i // span] for i, w in enumerate(weights)]
        factors = [c * n for c, n in zip(own, norms)]
        table = {key: value * (factors[key[0]] * factors[key[1]]) for key, value in table.items()}
        count //= 2
        merged = {}
        for k in range(count):
            merged[k, k] = (
                table[2 * k, 2 * k]
                + 2.0 * table[2 * k, 2 * k + 1]
                + table[2 * k + 1, 2 * k + 1]
            )
            for m in range(k + 1, count):
                merged[k, m] = (
                    table[2 * k, 2 * m]
                    + table[2 * k, 2 * m + 1]
                    + table[2 * k + 1, 2 * m]
                    + table[2 * k + 1, 2 * m + 1]
                )
        table = merged
        norms = [1.0] * count
        span *= 2
    return weights


def update_kernel(totals_ref, *refs):
    hbms, outs, held_refs, sems = refs[:6], refs[6:10], refs[10:16], refs[16]
    copies = [
        pltpu.make_async_copy(hbm, held, sems.at[n]) for n, (hbm, held) in enumerate(zip(hbms, held_refs))
    ]
    for copy in copies:
        copy.start()
    weights = [
        tree_coefs(lambda n, t=t: totals_ref[2 * t + n // 128, n % 128]) for t in range(2)
    ]
    for t in range(2):
        for copy in copies[3 * t : 3 * t + 3]:
            copy.wait()
        v_ref, weight_ref, moment_ref = held_refs[3 * t : 3 * t + 3]
        new_weight_ref, new_moment_ref = outs[2 * t : 2 * t + 2]

        @pl.loop(0, ROWS // 8)
        def _(r, t=t, v_ref=v_ref, weight_ref=weight_ref, moment_ref=moment_ref, new_weight_ref=new_weight_ref, new_moment_ref=new_moment_ref):
            rows = pl.ds(pl.multiple_of(r * 8, 8), 8)
            merged = weights[t][0] * v_ref[0, rows, :]
            for i in range(1, CHIPS):
                merged = merged + weights[t][i] * v_ref[i, rows, :]
            moment = MOMENTUM_DECAY * moment_ref[rows, :] + merged
            new_moment_ref[rows, :] = moment
            new_weight_ref[rows, :] = weight_ref[rows, :] - STEP_SIZE * moment


def update(totals, *arrays):
    out = jax.ShapeDtypeStruct((ROWS, FEATURES), jnp.float32)
    hbm = pl.BlockSpec(memory_space=pltpu.HBM)
    return pl.pallas_call(
        update_kernel,
        out_shape=(out,) * 4,
        in_specs=[SMEM] + [hbm] * 6,
        out_specs=(VMEM,) * 4,
        scratch_shapes=[pltpu.VMEM(a.shape, a.dtype) for a in arrays]
        + [pltpu.SemaphoreType.DMA((6,))],
        compiler_params=params(60),
        cost_estimate=cost(8 << 20, 10 * MIB),
    )(totals, *arrays)


def after(value, *others):
    return lax.optimization_barrier((value,) + others)[0]


def shards(
    tokens, key_cotangent, value_cotangent, key_weight, value_weight, key_moment, value_moment
):
    shard_count, replicas = lax.axis_size("shard"), lax.axis_size("rep")
    index = lax.axis_index("rep").astype(jnp.int32)
    core = (index & 1)[None]
    leader = ((lax.axis_index("shard") == 0) & (index & 1 == 0)).astype(jnp.int32)
    place = jnp.stack([index >> 1, leader])
    swap = [(i, i ^ 1) for i in range(replicas)]
    core_groups = [list(range(c, replicas, 2)) for c in range(2)]

    def summed(sums):
        sums = sums + lax.ppermute(sums, "rep", swap)
        shifts = [
            [(s, (s + d) % shard_count) for s in range(shard_count)] for d in range(1, shard_count)
        ]
        return [sums] + [lax.ppermute(sums, "shard", shift) for shift in shifts]

    def gathered(sent):
        return lax.all_to_all(sent, "rep", 0, 0, axis_index_groups=core_groups)

    key_other, own_rows, other_rows, key_cotangent = split_and_grad(core, tokens, key_cotangent)
    key_arrived = [lax.ppermute(key_other, "rep", swap)]
    key_own = grad(own_rows, key_cotangent)
    half = other_rows.shape[0] // 2
    value_first = grad(after(other_rows, key_own), value_cotangent, 0, half, [key_own])
    key_sums = summed(pair_sums(after(core, value_first), key_own, key_arrived, 1))
    value_second = grad(
        after(other_rows, key_sums[0]), value_cotangent, half, half, [key_own] + key_arrived
    )
    key_merged, key_norm = merge_pair(core, key_own, key_arrived, key_sums)
    key_sent = key_merged.astype(jnp.float16)
    key_all = gathered(key_sent)

    value_arrived = [
        lax.ppermute(value_first, "rep", swap),
        lax.ppermute(after(value_second, key_sent), "rep", swap),
    ]
    value_own = grad(after(own_rows, key_sent), value_cotangent)
    value_sums = summed(pair_sums(core, value_own, value_arrived, 1))
    value_merged, value_norm = merge_pair(core, value_own, value_arrived, value_sums)
    value_all = gathered(value_merged.astype(jnp.float16))

    key_v = key_all.astype(jnp.float32)
    key_vector = gram(place, key_v, key_norm, [], (2, 128))
    value_v = value_all.astype(jnp.float32)
    vectors = gram(place, value_v, value_norm, [key_vector], (shard_count * replicas, 4, 128))
    totals = jnp.sum(lax.all_to_all(vectors, ("shard", "rep"), 0, 0), axis=0)
    new_key_weight, new_key_moment, new_value_weight, new_value_moment = update(
        totals, key_v, key_weight, key_moment, value_v, value_weight, value_moment
    )
    return (new_key_weight, new_value_weight, new_key_moment, new_value_moment)


def solution(mesh):
    in_specs = (
        P("rep", "shard"),
        P("rep", None),
        P("rep", None),
        P(("shard", "rep"), None),
        P(("shard", "rep"), None),
        P(("shard", "rep"), None),
        P(("shard", "rep"), None),
    )
    out_specs = (
        P(("shard", "rep"), None),
        P(("shard", "rep"), None),
        P(("shard", "rep"), None),
        P(("shard", "rep"), None),
    )
    return jax.shard_map(shards, mesh=mesh, in_specs=in_specs, out_specs=out_specs, check_vma=False)
```

```python
import functools
import math

import jax
import jax.numpy as jnp
from jax import lax
from jax.experimental import pallas as pl
from jax.experimental.pallas import tpu as pltpu
from jax.sharding import PartitionSpec as P

EPSILON = 1e-06
MOMENTUM_DECAY = 0.9
STEP_SIZE = 0.01
CHIPS = 16
ROWS = 64
FEATURES = 1024
SENT_NORM = 16384.0
MIB = 1 << 20
PAIRS = {pair: n for n, pair in enumerate((i, j) for i in range(CHIPS) for j in range(i, CHIPS))}


def params(mib):
    return pltpu.CompilerParams(vmem_limit_bytes=mib * MIB)


def cost(flops, moved):
    return pl.CostEstimate(flops=flops, bytes_accessed=moved, transcendentals=0)


VMEM = pl.BlockSpec(memory_space=pltpu.VMEM)
SMEM = pl.BlockSpec(memory_space=pltpu.SMEM)


def scaled_dot(rows, cotangent):
    product = jnp.dot(rows, cotangent, preferred_element_type=jnp.float32)
    return (product * (1.0 / math.sqrt(rows.shape[1]))).reshape(-1, ROWS, FEATURES)


def split_kernel(core_ref, x_hbm, y_hbm, grad_ref, own_ref, other_ref, x_ref, y_ref, x_sems, y_sem):
    steps, depth, width = x_ref.shape
    x_copies = [
        pltpu.make_async_copy(x_hbm.at[:, pl.ds(i * width, width)], x_ref.at[i], x_sems.at[i])
        for i in range(steps)
    ]
    y_copy = pltpu.make_async_copy(y_hbm, y_ref, y_sem)
    x_copies[0].start()
    y_copy.start()
    for copy in x_copies[1:]:
        copy.start()
    is_first = core_ref[0] == 0
    half = width // 2
    per = half // ROWS
    for i in range(steps):
        x_copies[i].wait()
        blocks = x_ref[i].T.reshape(-1, 2, ROWS, depth)
        first = blocks[:, 0].reshape(-1, depth)
        second = blocks[:, 1].reshape(-1, depth)
        own_ref[pl.ds(i * half, half), :] = jnp.where(is_first, first, second)
        other = jnp.where(is_first, second, first)
        other_ref[pl.ds(i * half, half), :] = other
        if i == 0:
            y_copy.wait()
        grad_ref[pl.ds(i * per, per)] = scaled_dot(other, y_ref[...])


def split_and_grad(core, tokens, cotangent):
    depth, width = tokens.shape
    step = 512
    half = jax.ShapeDtypeStruct((width // 2, depth), jnp.bfloat16)
    hbm = pl.BlockSpec(memory_space=pltpu.HBM)
    return pl.pallas_call(
        split_kernel,
        out_shape=(
            jax.ShapeDtypeStruct((CHIPS, ROWS, FEATURES), jnp.float32),
            half,
            half,
        ),
        in_specs=[SMEM, hbm, hbm],
        out_specs=(VMEM,) * 3,
        scratch_shapes=[
            pltpu.VMEM((width // step, depth, step), jnp.bfloat16),
            pltpu.VMEM(cotangent.shape, jnp.bfloat16),
            pltpu.SemaphoreType.DMA((width // step,)),
            pltpu.SemaphoreType.DMA,
        ],
        compiler_params=params(32),
        cost_estimate=cost(depth * width * FEATURES, 24 * MIB),
    )(core, tokens, cotangent)


def grad_kernel(x_ref, y_ref, *refs, start):
    o_ref = refs[-1]
    step = 256
    per = step // ROWS

    @pl.loop(0, o_ref.shape[0] // per)
    def _(i):
        rows = x_ref[pl.ds(pl.multiple_of(start + i * step, step), step), :]
        o_ref[pl.ds(i * per, per)] = scaled_dot(rows, y_ref[...])


def grad(rows, cotangent, start=0, count=None, kept=()):
    count = count or rows.shape[0]
    return pl.pallas_call(
        functools.partial(grad_kernel, start=start),
        out_shape=jax.ShapeDtypeStruct((count // ROWS, ROWS, FEATURES), jnp.float32),
        in_specs=[VMEM] * (2 + len(kept)),
        out_specs=VMEM,
        compiler_params=params(8),
        cost_estimate=cost(2 * cotangent.shape[0] * count * FEATURES, 12 * MIB),
    )(rows, cotangent, *kept)


def parts_specs(parts):
    steps = parts[0].shape[0] // 4
    return [
        pl.BlockSpec(
            (4, ROWS, FEATURES),
            lambda i, n=n: (jnp.clip(i - n * steps, 0, steps - 1), 0, 0),
        )
        for n in range(len(parts))
    ]


def block_of(refs, steps):
    block = refs[0][...]
    for n in range(1, len(refs)):
        block = jnp.where(pl.program_id(0) >= n * steps, refs[n][...], block)
    return block


def pair_kernel(core_ref, a_ref, *refs, steps):
    b_refs, (o_ref, acc_ref) = refs[:-2], refs[-2:]
    step = pl.program_id(0)

    @pl.when(step == 0)
    def _():
        acc_ref[...] = jnp.zeros_like(acc_ref)

    a = a_ref[...].reshape(-1, 8, FEATURES)
    b = block_of(b_refs, steps).reshape(-1, 8, FEATURES)
    is_first = core_ref[0] == 0
    own, other = jnp.sum(a * a, axis=0), jnp.sum(b * b, axis=0)
    acc_ref[0] += jnp.sum(a * b, axis=0)
    acc_ref[1] += jnp.where(is_first, own, other)
    acc_ref[2] += jnp.where(is_first, other, own)

    @pl.when(step == pl.num_programs(0) - 1)
    def _():
        rows = [jnp.sum(acc_ref[k], axis=0, keepdims=True) for k in range(3)]
        rows = [jnp.sum(row, axis=1, keepdims=True) for row in rows]
        rows = [jnp.broadcast_to(row, (1, 128)) for row in rows]
        tile = jnp.concatenate(rows + [jnp.zeros((5, 128), jnp.float32)], axis=0)
        o_ref[...] = jnp.broadcast_to(tile[None], o_ref.shape)


def pair_sums(core, a, b, copies):
    spec = pl.BlockSpec((4, ROWS, FEATURES), lambda i: (i, 0, 0))
    return pl.pallas_call(
        functools.partial(pair_kernel, steps=b[0].shape[0] // 4),
        out_shape=jax.ShapeDtypeStruct((copies, 8, 128), jnp.float32),
        grid=(CHIPS // 4,),
        in_specs=[SMEM, spec] + parts_specs(b),
        out_specs=pl.BlockSpec((copies, 8, 128), lambda i: (0, 0, 0)),
        scratch_shapes=[pltpu.VMEM((3, 8, FEATURES), jnp.float32)],
        compiler_params=params(10),
        cost_estimate=cost(a.size, a.size),
    )(core, a, *b)


def merge_kernel(core_ref, a_ref, *refs, parts, steps):
    b_refs, sums_refs, (o_ref, norm_ref) = refs[:parts], refs[parts:-2], refs[-2:]
    sums = sum(jnp.sum(ref[...], axis=0) for ref in sums_refs)
    cross, p, q = sums[0:1], sums[1:2], sums[2:3]
    is_first = core_ref[0] == 0
    first = 1.0 - cross / (2.0 * (p + EPSILON))
    second = 1.0 - cross / (2.0 * (q + EPSILON))
    squares = first * first * p + second * second * q
    square = jnp.maximum(squares + 2.0 * first * second * cross, 1e-6 * squares)
    norm = jnp.sqrt(jnp.maximum(square, 1e-30))
    scale = SENT_NORM / norm
    norm_ref[...] = jnp.broadcast_to(norm * (1.0 / SENT_NORM), norm_ref.shape)
    own = jnp.where(is_first, first, second) * scale
    other = jnp.where(is_first, second, first) * scale
    own = jnp.concatenate([own] * (FEATURES // 128), axis=1)[None]
    other = jnp.concatenate([other] * (FEATURES // 128), axis=1)[None]
    o_ref[...] = own * a_ref[...] + other * block_of(b_refs, steps)


def merge_pair(core, a, b, sums):
    spec = pl.BlockSpec((4, ROWS, FEATURES), lambda i: (i, 0, 0))
    return pl.pallas_call(
        functools.partial(merge_kernel, parts=len(b), steps=b[0].shape[0] // 4),
        out_shape=(
            jax.ShapeDtypeStruct(a.shape, jnp.float32),
            jax.ShapeDtypeStruct((8, 128), jnp.float32),
        ),
        grid=(CHIPS // 4,),
        in_specs=[SMEM, spec] + parts_specs(b) + [VMEM] * len(sums),
        out_specs=(spec, pl.BlockSpec((8, 128), lambda i: (0, 0))),
        compiler_params=params(12),
        cost_estimate=cost(a.size, a.size),
    )(core, a, *b, *sums)


def gram_kernel(place_ref, v_ref, norm_ref, *refs):
    earlier_refs, (o_ref, t_ref) = refs[:-2], refs[-2:]
    t_ref[...] = jnp.zeros_like(t_ref)
    for gi in range(4):
        for gj in range(gi, 4):
            pairs = [
                (i, j)
                for i in range(4 * gi, 4 * gi + 4)
                for j in range(4 * gj, 4 * gj + 4)
                if i <= j
            ]

            def body(r, sums, pairs=pairs):
                sums = list(sums)
                rows = pl.ds(pl.multiple_of(r * 8, 8), 8)
                for lane in range(FEATURES // 128):
                    held = {}
                    for i, j in pairs:
                        for k in (i, j):
                            if k not in held:
                                held[k] = v_ref[k, rows, pl.ds(lane * 128, 128)]
                    for n, (i, j) in enumerate(pairs):
                        sums[n] = sums[n] + held[i] * held[j]
                return tuple(sums)

            zero = jnp.zeros((8, 128), jnp.float32)
            sums = lax.fori_loop(0, ROWS // 8, body, (zero,) * len(pairs))
            for pair, total in zip(pairs, sums):
                t_ref[pl.ds(PAIRS[pair], 1), :] = jnp.sum(total, axis=0, keepdims=True)
    lane = lax.broadcasted_iota(jnp.int32, (1, 128), 1)
    shown = (lane == 0) & (place_ref[1] == 1)
    t_ref[pl.ds(len(PAIRS) + place_ref[0], 1), :] = jnp.where(shown, norm_ref[0:1, :], 0.0)
    rows = [ref[...] for ref in earlier_refs]
    for part in range(2):
        rows.append(jnp.sum(t_ref[pl.ds(part * 128, 128), :].T, axis=0, keepdims=True))
    tile = jnp.concatenate(rows, axis=0)
    o_ref[...] = tile if o_ref.ndim == 2 else jnp.broadcast_to(tile[None], o_ref.shape)


def gram(place, v, norm, earlier, out_dims):
    return pl.pallas_call(
        gram_kernel,
        out_shape=jax.ShapeDtypeStruct(out_dims, jnp.float32),
        in_specs=[SMEM] + [VMEM] * (2 + len(earlier)),
        out_specs=VMEM,
        scratch_shapes=[pltpu.VMEM((256, 128), jnp.float32)],
        compiler_params=params(16),
        cost_estimate=cost(20 << 20, 4 * v.size),
    )(place, v, norm, *earlier)


def tree_coefs(read):
    count = CHIPS
    norms = [read(len(PAIRS) + i) for i in range(count)]
    table = {pair: read(n) for pair, n in PAIRS.items()}
    weights = list(norms)
    span = 1
    while count > 1:
        own = []
        for k in range(0, count, 2):
            cross = table[k, k + 1] * (norms[k] * norms[k + 1])
            for m in (k, k + 1):
                square = table[m, m] * (norms[m] * norms[m])
                own.append(1.0 - cross / (2.0 * (square + EPSILON)))
        weights = [w * own[i // span] for i, w in enumerate(weights)]
        factors = [c * n for c, n in zip(own, norms)]
        table = {key: value * (factors[key[0]] * factors[key[1]]) for key, value in table.items()}
        count //= 2
        merged = {}
        for k in range(count):
            merged[k, k] = (
                table[2 * k, 2 * k]
                + 2.0 * table[2 * k, 2 * k + 1]
                + table[2 * k + 1, 2 * k + 1]
            )
            for m in range(k + 1, count):
                merged[k, m] = (
                    table[2 * k, 2 * m]
                    + table[2 * k, 2 * m + 1]
                    + table[2 * k + 1, 2 * m]
                    + table[2 * k + 1, 2 * m + 1]
                )
        table = merged
        norms = [1.0] * count
        span *= 2
    return weights


def update_kernel(totals_ref, *refs):
    hbms, outs, held_refs, sems = refs[:6], refs[6:10], refs[10:16], refs[16]
    copies = [
        pltpu.make_async_copy(hbm, held, sems.at[n]) for n, (hbm, held) in enumerate(zip(hbms, held_refs))
    ]
    for copy in copies:
        copy.start()
    weights = [
        tree_coefs(lambda n, t=t: totals_ref[2 * t + n // 128, n % 128]) for t in range(2)
    ]
    for t in range(2):
        for copy in copies[3 * t : 3 * t + 3]:
            copy.wait()
        v_ref, weight_ref, moment_ref = held_refs[3 * t : 3 * t + 3]
        new_weight_ref, new_moment_ref = outs[2 * t : 2 * t + 2]

        @pl.loop(0, ROWS // 8)
        def _(r, t=t, v_ref=v_ref, weight_ref=weight_ref, moment_ref=moment_ref, new_weight_ref=new_weight_ref, new_moment_ref=new_moment_ref):
            rows = pl.ds(pl.multiple_of(r * 8, 8), 8)
            merged = weights[t][0] * v_ref[0, rows, :]
            for i in range(1, CHIPS):
                merged = merged + weights[t][i] * v_ref[i, rows, :]
            moment = MOMENTUM_DECAY * moment_ref[rows, :] + merged
            new_moment_ref[rows, :] = moment
            new_weight_ref[rows, :] = weight_ref[rows, :] - STEP_SIZE * moment


def update(totals, *arrays):
    out = jax.ShapeDtypeStruct((ROWS, FEATURES), jnp.float32)
    hbm = pl.BlockSpec(memory_space=pltpu.HBM)
    return pl.pallas_call(
        update_kernel,
        out_shape=(out,) * 4,
        in_specs=[SMEM] + [hbm] * 6,
        out_specs=(VMEM,) * 4,
        scratch_shapes=[pltpu.VMEM(a.shape, a.dtype) for a in arrays]
        + [pltpu.SemaphoreType.DMA((6,))],
        compiler_params=params(60),
        cost_estimate=cost(8 << 20, 10 * MIB),
    )(totals, *arrays)


def after(value, *others):
    return lax.optimization_barrier((value,) + others)[0]


def shards(
    tokens, key_cotangent, value_cotangent, key_weight, value_weight, key_moment, value_moment
):
    shard_count, replicas = lax.axis_size("shard"), lax.axis_size("rep")
    index = lax.axis_index("rep").astype(jnp.int32)
    core = (index & 1)[None]
    leader = ((lax.axis_index("shard") == 0) & (index & 1 == 0)).astype(jnp.int32)
    place = jnp.stack([index >> 1, leader])
    swap = [(i, i ^ 1) for i in range(replicas)]
    core_groups = [list(range(c, replicas, 2)) for c in range(2)]

    def summed(sums):
        sums = sums + lax.ppermute(sums, "rep", swap)
        shifts = [
            [(s, (s + d) % shard_count) for s in range(shard_count)] for d in range(1, shard_count)
        ]
        return [sums] + [lax.ppermute(sums, "shard", shift) for shift in shifts]

    def gathered(sent):
        return lax.all_to_all(sent, "rep", 0, 0, axis_index_groups=core_groups)

    key_other, own_rows, other_rows = split_and_grad(core, tokens, key_cotangent)
    key_arrived = [lax.ppermute(key_other, "rep", swap)]
    key_own = grad(own_rows, key_cotangent)
    half = other_rows.shape[0] // 2
    value_first = grad(after(other_rows, key_own), value_cotangent, 0, half, [key_own])
    key_sums = summed(pair_sums(after(core, value_first), key_own, key_arrived, 1))
    value_second = grad(
        after(other_rows, key_sums[0]), value_cotangent, half, half, [key_own] + key_arrived
    )
    key_merged, key_norm = merge_pair(core, key_own, key_arrived, key_sums)
    key_sent = key_merged.astype(jnp.float16)
    key_all = gathered(key_sent)

    value_arrived = [
        lax.ppermute(value_first, "rep", swap),
        lax.ppermute(after(value_second, key_sent), "rep", swap),
    ]
    value_own = grad(after(own_rows, key_sent), value_cotangent)
    value_sums = summed(pair_sums(core, value_own, value_arrived, 1))
    value_merged, value_norm = merge_pair(core, value_own, value_arrived, value_sums)
    value_all = gathered(value_merged.astype(jnp.float16))

    key_v = key_all.astype(jnp.float32)
    key_vector = gram(place, key_v, key_norm, [], (2, 128))
    value_v = value_all.astype(jnp.float32)
    vectors = gram(place, value_v, value_norm, [key_vector], (shard_count * replicas, 4, 128))
    totals = jnp.sum(lax.all_to_all(vectors, ("shard", "rep"), 0, 0), axis=0)
    new_key_weight, new_key_moment, new_value_weight, new_value_moment = update(
        totals, key_v, key_weight, key_moment, value_v, value_weight, value_moment
    )
    return (new_key_weight, new_value_weight, new_key_moment, new_value_moment)


def solution(mesh):
    in_specs = (
        P("rep", "shard"),
        P("rep", None),
        P("rep", None),
        P(("shard", "rep"), None),
        P(("shard", "rep"), None),
        P(("shard", "rep"), None),
        P(("shard", "rep"), None),
    )
    out_specs = (
        P(("shard", "rep"), None),
        P(("shard", "rep"), None),
        P(("shard", "rep"), None),
        P(("shard", "rep"), None),
    )
    return jax.shard_map(shards, mesh=mesh, in_specs=in_specs, out_specs=out_specs, check_vma=False)
```

```python
import functools
import math

import jax
import jax.numpy as jnp
from jax import lax
from jax.experimental import pallas as pl
from jax.experimental.pallas import tpu as pltpu
from jax.sharding import PartitionSpec as P

EPSILON = 1e-06
MOMENTUM_DECAY = 0.9
STEP_SIZE = 0.01
CHIPS = 16
ROWS = 64
FEATURES = 1024
SENT_NORM = 16384.0
MIB = 1 << 20
PAIRS = {pair: n for n, pair in enumerate((i, j) for i in range(CHIPS) for j in range(i, CHIPS))}


def params(mib):
    return pltpu.CompilerParams(vmem_limit_bytes=mib * MIB)


def cost(flops, moved):
    return pl.CostEstimate(flops=flops, bytes_accessed=moved, transcendentals=0)


VMEM = pl.BlockSpec(memory_space=pltpu.VMEM)
SMEM = pl.BlockSpec(memory_space=pltpu.SMEM)


def scaled_dot(rows, cotangent):
    product = jnp.dot(rows, cotangent, preferred_element_type=jnp.float32)
    return (product * (1.0 / math.sqrt(rows.shape[1]))).reshape(-1, ROWS, FEATURES)


def split_kernel(core_ref, x_hbm, y_hbm, grad_ref, own_ref, other_ref, x_ref, y_ref, x_sems, y_sem):
    steps, depth, width = x_ref.shape
    x_copies = [
        pltpu.make_async_copy(
            x_hbm.at[:, pl.ds((steps - 1 - i) * width, width)], x_ref.at[i], x_sems.at[i]
        )
        for i in range(steps)
    ]
    y_copy = pltpu.make_async_copy(y_hbm, y_ref, y_sem)
    x_copies[0].start()
    y_copy.start()
    for copy in x_copies[1:]:
        copy.start()
    is_first = core_ref[0] == 0
    half = width // 2
    per = half // ROWS
    for i in range(steps):
        x_copies[i].wait()
        blocks = x_ref[i].T.reshape(-1, 2, ROWS, depth)
        order = range(blocks.shape[0] - 1, -1, -1)
        first = jnp.concatenate([blocks[n, 0] for n in order], axis=0)
        second = jnp.concatenate([blocks[n, 1] for n in order], axis=0)
        own_ref[pl.ds(i * half, half), :] = jnp.where(is_first, first, second)
        other = jnp.where(is_first, second, first)
        other_ref[pl.ds(i * half, half), :] = other
        if i == 0:
            y_copy.wait()
        grad_ref[pl.ds(i * per, per)] = scaled_dot(other, y_ref[...])


def split_and_grad(core, tokens, cotangent):
    depth, width = tokens.shape
    step = 512
    half = jax.ShapeDtypeStruct((width // 2, depth), jnp.bfloat16)
    hbm = pl.BlockSpec(memory_space=pltpu.HBM)
    return pl.pallas_call(
        split_kernel,
        out_shape=(
            jax.ShapeDtypeStruct((CHIPS, ROWS, FEATURES), jnp.float32),
            half,
            half,
        ),
        in_specs=[SMEM, hbm, hbm],
        out_specs=(VMEM,) * 3,
        scratch_shapes=[
            pltpu.VMEM((width // step, depth, step), jnp.bfloat16),
            pltpu.VMEM(cotangent.shape, jnp.bfloat16),
            pltpu.SemaphoreType.DMA((width // step,)),
            pltpu.SemaphoreType.DMA,
        ],
        compiler_params=params(32),
        cost_estimate=cost(depth * width * FEATURES, 24 * MIB),
    )(core, tokens, cotangent)


def grad_kernel(x_ref, y_ref, *refs, start):
    o_ref = refs[-1]
    step = 256
    per = step // ROWS

    @pl.loop(0, o_ref.shape[0] // per)
    def _(i):
        rows = x_ref[pl.ds(pl.multiple_of(start + i * step, step), step), :]
        o_ref[pl.ds(i * per, per)] = scaled_dot(rows, y_ref[...])


def grad(rows, cotangent, start=0, count=None, kept=()):
    count = count or rows.shape[0]
    return pl.pallas_call(
        functools.partial(grad_kernel, start=start),
        out_shape=jax.ShapeDtypeStruct((count // ROWS, ROWS, FEATURES), jnp.float32),
        in_specs=[VMEM] * (2 + len(kept)),
        out_specs=VMEM,
        compiler_params=params(8),
        cost_estimate=cost(2 * cotangent.shape[0] * count * FEATURES, 12 * MIB),
    )(rows, cotangent, *kept)


def parts_specs(parts):
    steps = parts[0].shape[0] // 4
    return [
        pl.BlockSpec(
            (4, ROWS, FEATURES),
            lambda i, n=n: (jnp.clip(i - n * steps, 0, steps - 1), 0, 0),
        )
        for n in range(len(parts))
    ]


def block_of(refs, steps):
    block = refs[0][...]
    for n in range(1, len(refs)):
        block = jnp.where(pl.program_id(0) >= n * steps, refs[n][...], block)
    return block


def pair_kernel(core_ref, a_ref, *refs, steps):
    b_refs, (o_ref, acc_ref) = refs[:-2], refs[-2:]
    step = pl.program_id(0)

    @pl.when(step == 0)
    def _():
        acc_ref[...] = jnp.zeros_like(acc_ref)

    a = a_ref[...].reshape(-1, 8, FEATURES)
    b = block_of(b_refs, steps).reshape(-1, 8, FEATURES)
    is_first = core_ref[0] == 0
    own, other = jnp.sum(a * a, axis=0), jnp.sum(b * b, axis=0)
    acc_ref[0] += jnp.sum(a * b, axis=0)
    acc_ref[1] += jnp.where(is_first, own, other)
    acc_ref[2] += jnp.where(is_first, other, own)

    @pl.when(step == pl.num_programs(0) - 1)
    def _():
        rows = [jnp.sum(acc_ref[k], axis=0, keepdims=True) for k in range(3)]
        rows = [jnp.sum(row, axis=1, keepdims=True) for row in rows]
        rows = [jnp.broadcast_to(row, (1, 128)) for row in rows]
        tile = jnp.concatenate(rows + [jnp.zeros((5, 128), jnp.float32)], axis=0)
        o_ref[...] = jnp.broadcast_to(tile[None], o_ref.shape)


def pair_sums(core, a, b, copies):
    spec = pl.BlockSpec((4, ROWS, FEATURES), lambda i: (i, 0, 0))
    return pl.pallas_call(
        functools.partial(pair_kernel, steps=b[0].shape[0] // 4),
        out_shape=jax.ShapeDtypeStruct((copies, 8, 128), jnp.float32),
        grid=(CHIPS // 4,),
        in_specs=[SMEM, spec] + parts_specs(b),
        out_specs=pl.BlockSpec((copies, 8, 128), lambda i: (0, 0, 0)),
        scratch_shapes=[pltpu.VMEM((3, 8, FEATURES), jnp.float32)],
        compiler_params=params(10),
        cost_estimate=cost(a.size, a.size),
    )(core, a, *b)


def merge_kernel(core_ref, a_ref, *refs, parts, steps):
    b_refs, sums_refs, (o_ref, norm_ref) = refs[:parts], refs[parts:-2], refs[-2:]
    sums = sum(jnp.sum(ref[...], axis=0) for ref in sums_refs)
    cross, p, q = sums[0:1], sums[1:2], sums[2:3]
    is_first = core_ref[0] == 0
    first = 1.0 - cross / (2.0 * (p + EPSILON))
    second = 1.0 - cross / (2.0 * (q + EPSILON))
    squares = first * first * p + second * second * q
    square = jnp.maximum(squares + 2.0 * first * second * cross, 1e-6 * squares)
    norm = jnp.sqrt(jnp.maximum(square, 1e-30))
    scale = SENT_NORM / norm
    norm_ref[...] = jnp.broadcast_to(norm * (1.0 / SENT_NORM), norm_ref.shape)
    own = jnp.where(is_first, first, second) * scale
    other = jnp.where(is_first, second, first) * scale
    own = jnp.concatenate([own] * (FEATURES // 128), axis=1)[None]
    other = jnp.concatenate([other] * (FEATURES // 128), axis=1)[None]
    o_ref[...] = own * a_ref[...] + other * block_of(b_refs, steps)


def merge_pair(core, a, b, sums):
    spec = pl.BlockSpec((4, ROWS, FEATURES), lambda i: (i, 0, 0))
    return pl.pallas_call(
        functools.partial(merge_kernel, parts=len(b), steps=b[0].shape[0] // 4),
        out_shape=(
            jax.ShapeDtypeStruct(a.shape, jnp.float32),
            jax.ShapeDtypeStruct((8, 128), jnp.float32),
        ),
        grid=(CHIPS // 4,),
        in_specs=[SMEM, spec] + parts_specs(b) + [VMEM] * len(sums),
        out_specs=(spec, pl.BlockSpec((8, 128), lambda i: (0, 0))),
        compiler_params=params(12),
        cost_estimate=cost(a.size, a.size),
    )(core, a, *b, *sums)


def gram_kernel(place_ref, v_ref, norm_ref, *refs):
    earlier_refs, (o_ref, t_ref) = refs[:-2], refs[-2:]
    t_ref[...] = jnp.zeros_like(t_ref)
    for gi in range(4):
        for gj in range(gi, 4):
            pairs = [
                (i, j)
                for i in range(4 * gi, 4 * gi + 4)
                for j in range(4 * gj, 4 * gj + 4)
                if i <= j
            ]

            def body(r, sums, pairs=pairs):
                sums = list(sums)
                rows = pl.ds(pl.multiple_of(r * 8, 8), 8)
                for lane in range(FEATURES // 128):
                    held = {}
                    for i, j in pairs:
                        for k in (i, j):
                            if k not in held:
                                held[k] = v_ref[k, rows, pl.ds(lane * 128, 128)]
                    for n, (i, j) in enumerate(pairs):
                        sums[n] = sums[n] + held[i] * held[j]
                return tuple(sums)

            zero = jnp.zeros((8, 128), jnp.float32)
            sums = lax.fori_loop(0, ROWS // 8, body, (zero,) * len(pairs))
            for pair, total in zip(pairs, sums):
                t_ref[pl.ds(PAIRS[pair], 1), :] = jnp.sum(total, axis=0, keepdims=True)
    lane = lax.broadcasted_iota(jnp.int32, (1, 128), 1)
    shown = (lane == 0) & (place_ref[1] == 1)
    t_ref[pl.ds(len(PAIRS) + place_ref[0], 1), :] = jnp.where(shown, norm_ref[0:1, :], 0.0)
    rows = [ref[...] for ref in earlier_refs]
    for part in range(2):
        rows.append(jnp.sum(t_ref[pl.ds(part * 128, 128), :].T, axis=0, keepdims=True))
    tile = jnp.concatenate(rows, axis=0)
    o_ref[...] = tile if o_ref.ndim == 2 else jnp.broadcast_to(tile[None], o_ref.shape)


def gram(place, v, norm, earlier, out_dims):
    return pl.pallas_call(
        gram_kernel,
        out_shape=jax.ShapeDtypeStruct(out_dims, jnp.float32),
        in_specs=[SMEM] + [VMEM] * (2 + len(earlier)),
        out_specs=VMEM,
        scratch_shapes=[pltpu.VMEM((256, 128), jnp.float32)],
        compiler_params=params(16),
        cost_estimate=cost(20 << 20, 4 * v.size),
    )(place, v, norm, *earlier)


def tree_coefs(read):
    count = CHIPS
    norms = [read(len(PAIRS) + i) for i in range(count)]
    table = {pair: read(n) for pair, n in PAIRS.items()}
    weights = list(norms)
    span = 1
    while count > 1:
        own = []
        for k in range(0, count, 2):
            cross = table[k, k + 1] * (norms[k] * norms[k + 1])
            for m in (k, k + 1):
                square = table[m, m] * (norms[m] * norms[m])
                own.append(1.0 - cross / (2.0 * (square + EPSILON)))
        weights = [w * own[i // span] for i, w in enumerate(weights)]
        factors = [c * n for c, n in zip(own, norms)]
        table = {key: value * (factors[key[0]] * factors[key[1]]) for key, value in table.items()}
        count //= 2
        merged = {}
        for k in range(count):
            merged[k, k] = (
                table[2 * k, 2 * k]
                + 2.0 * table[2 * k, 2 * k + 1]
                + table[2 * k + 1, 2 * k + 1]
            )
            for m in range(k + 1, count):
                merged[k, m] = (
                    table[2 * k, 2 * m]
                    + table[2 * k, 2 * m + 1]
                    + table[2 * k + 1, 2 * m]
                    + table[2 * k + 1, 2 * m + 1]
                )
        table = merged
        norms = [1.0] * count
        span *= 2
    return weights


def update_kernel(totals_ref, *refs):
    ins, outs, (sum_ref, scalar_ref, sem) = refs[:6], refs[6:10], refs[10:]
    sum_ref[...] = jnp.sum(totals_ref[...], axis=0)
    copy = pltpu.make_async_copy(sum_ref, scalar_ref, sem)
    copy.start()
    copy.wait()
    weights = [
        tree_coefs(lambda n, t=t: scalar_ref[2 * t + n // 128, n % 128]) for t in range(2)
    ]
    for t in range(2):
        v_ref, weight_ref, moment_ref = ins[3 * t : 3 * t + 3]
        new_weight_ref, new_moment_ref = outs[2 * t : 2 * t + 2]

        @pl.loop(0, ROWS // 8)
        def _(r, t=t, v_ref=v_ref, weight_ref=weight_ref, moment_ref=moment_ref, new_weight_ref=new_weight_ref, new_moment_ref=new_moment_ref):
            rows = pl.ds(pl.multiple_of(r * 8, 8), 8)
            merged = weights[t][0] * v_ref[0, rows, :]
            for i in range(1, CHIPS):
                merged = merged + weights[t][i] * v_ref[i, rows, :]
            moment = MOMENTUM_DECAY * moment_ref[rows, :] + merged
            new_moment_ref[rows, :] = moment
            new_weight_ref[rows, :] = weight_ref[rows, :] - STEP_SIZE * moment


def update(totals, *arrays):
    out = jax.ShapeDtypeStruct((ROWS, FEATURES), jnp.float32)
    return pl.pallas_call(
        update_kernel,
        out_shape=(out,) * 4,
        in_specs=[VMEM] * 7,
        out_specs=(VMEM,) * 4,
        scratch_shapes=[
            pltpu.VMEM((4, 128), jnp.float32),
            pltpu.SMEM((4, 128), jnp.float32),
            pltpu.SemaphoreType.DMA,
        ],
        compiler_params=params(8),
        cost_estimate=cost(8 << 20, 10 * MIB),
    )(totals, *arrays)


def after(value, *others):
    return lax.optimization_barrier((value,) + others)[0]


def shards(
    tokens, key_cotangent, value_cotangent, key_weight, value_weight, key_moment, value_moment
):
    shard_count, replicas = lax.axis_size("shard"), lax.axis_size("rep")
    index = lax.axis_index("rep").astype(jnp.int32)
    core = (index & 1)[None]
    leader = ((lax.axis_index("shard") == 0) & (index & 1 == 0)).astype(jnp.int32)
    place = jnp.stack([CHIPS - 1 - (index >> 1), leader])
    swap = [(i, i ^ 1) for i in range(replicas)]
    core_groups = [list(range(c, replicas, 2))[::-1] for c in range(2)]

    def summed(sums):
        sums = sums + lax.ppermute(sums, "rep", swap)
        shifts = [
            [(s, (s + d) % shard_count) for s in range(shard_count)] for d in range(1, shard_count)
        ]
        return [sums] + [lax.ppermute(sums, "shard", shift) for shift in shifts]

    def gathered(sent):
        return lax.all_to_all(sent, "rep", 0, 0, axis_index_groups=core_groups)

    key_other, own_rows, other_rows = split_and_grad(core, tokens, key_cotangent)
    key_arrived = [lax.ppermute(key_other, "rep", swap)]
    key_own = grad(own_rows, key_cotangent)
    half = other_rows.shape[0] // 2
    value_first = grad(after(other_rows, key_own), value_cotangent, 0, half, [key_own])
    key_sums = summed(pair_sums(after(core, value_first), key_own, key_arrived, 1))
    value_second = grad(
        after(other_rows, key_sums[0]), value_cotangent, half, half, [key_own] + key_arrived
    )
    key_merged, key_norm = merge_pair(core, key_own, key_arrived, key_sums)
    key_sent = key_merged.astype(jnp.float16)
    key_all = gathered(key_sent)

    value_arrived = [
        lax.ppermute(value_first, "rep", swap),
        lax.ppermute(after(value_second, key_sent), "rep", swap),
    ]
    value_own = grad(after(own_rows, key_sent), value_cotangent)
    value_sums = summed(pair_sums(core, value_own, value_arrived, 1))
    value_merged, value_norm = merge_pair(core, value_own, value_arrived, value_sums)
    value_all = gathered(value_merged.astype(jnp.float16))

    key_v = key_all.astype(jnp.float32)
    key_vector = gram(place, key_v, key_norm, [], (2, 128))
    value_v = value_all.astype(jnp.float32)
    vectors = gram(place, value_v, value_norm, [key_vector], (shard_count * replicas, 4, 128))
    totals = lax.all_to_all(vectors, ("shard", "rep"), 0, 0)
    new_key_weight, new_key_moment, new_value_weight, new_value_moment = update(
        totals, key_v, key_weight, key_moment, value_v, value_weight, value_moment
    )
    return (new_key_weight, new_value_weight, new_key_moment, new_value_moment)


def solution(mesh):
    in_specs = (
        P("rep", "shard"),
        P("rep", None),
        P("rep", None),
        P(("shard", "rep"), None),
        P(("shard", "rep"), None),
        P(("shard", "rep"), None),
        P(("shard", "rep"), None),
    )
    out_specs = (
        P(("shard", "rep"), None),
        P(("shard", "rep"), None),
        P(("shard", "rep"), None),
        P(("shard", "rep"), None),
    )
    return jax.shard_map(shards, mesh=mesh, in_specs=in_specs, out_specs=out_specs, check_vma=False)
```

```python
import functools
import math

import jax
import jax.numpy as jnp
from jax import lax
from jax.experimental import pallas as pl
from jax.experimental.pallas import tpu as pltpu
from jax.sharding import PartitionSpec as P

EPSILON = 1e-06
MOMENTUM_DECAY = 0.9
STEP_SIZE = 0.01
CHIPS = 16
ROWS = 64
FEATURES = 1024
SENT_NORM = 16384.0
MIB = 1 << 20
PAIRS = {pair: n for n, pair in enumerate((i, j) for i in range(CHIPS) for j in range(i, CHIPS))}


def params(mib):
    return pltpu.CompilerParams(vmem_limit_bytes=mib * MIB)


def cost(flops, moved):
    return pl.CostEstimate(flops=flops, bytes_accessed=moved, transcendentals=0)


VMEM = pl.BlockSpec(memory_space=pltpu.VMEM)
SMEM = pl.BlockSpec(memory_space=pltpu.SMEM)


def scaled_dot(rows, cotangent):
    product = jnp.dot(rows, cotangent, preferred_element_type=jnp.float32)
    return (product * (1.0 / math.sqrt(rows.shape[1]))).reshape(-1, ROWS, FEATURES)


def split_kernel(core_ref, x_hbm, y_hbm, grad_ref, own_ref, other_ref, x_ref, y_ref, x_sems, y_sem):
    steps, depth, width = x_ref.shape
    x_copies = [
        pltpu.make_async_copy(
            x_hbm.at[:, pl.ds((steps - 1 - i) * width, width)], x_ref.at[i], x_sems.at[i]
        )
        for i in range(steps)
    ]
    y_copy = pltpu.make_async_copy(y_hbm, y_ref, y_sem)
    x_copies[0].start()
    y_copy.start()
    for copy in x_copies[1:]:
        copy.start()
    is_first = core_ref[0] == 0
    half = width // 2
    per = half // ROWS
    for i in range(steps):
        x_copies[i].wait()
        blocks = x_ref[i].T.reshape(-1, 2, ROWS, depth)
        order = range(blocks.shape[0] - 1, -1, -1)
        first = jnp.concatenate([blocks[n, 0] for n in order], axis=0)
        second = jnp.concatenate([blocks[n, 1] for n in order], axis=0)
        own_ref[pl.ds(i * half, half), :] = jnp.where(is_first, first, second)
        other = jnp.where(is_first, second, first)
        other_ref[pl.ds(i * half, half), :] = other
        if i == 0:
            y_copy.wait()
        grad_ref[pl.ds(i * per, per)] = scaled_dot(other, y_ref[...])


def split_and_grad(core, tokens, cotangent):
    depth, width = tokens.shape
    step = 512
    half = jax.ShapeDtypeStruct((width // 2, depth), jnp.bfloat16)
    hbm = pl.BlockSpec(memory_space=pltpu.HBM)
    return pl.pallas_call(
        split_kernel,
        out_shape=(
            jax.ShapeDtypeStruct((CHIPS, ROWS, FEATURES), jnp.float32),
            half,
            half,
        ),
        in_specs=[SMEM, hbm, hbm],
        out_specs=(VMEM,) * 3,
        scratch_shapes=[
            pltpu.VMEM((width // step, depth, step), jnp.bfloat16),
            pltpu.VMEM(cotangent.shape, jnp.bfloat16),
            pltpu.SemaphoreType.DMA((width // step,)),
            pltpu.SemaphoreType.DMA,
        ],
        compiler_params=params(32),
        cost_estimate=cost(depth * width * FEATURES, 24 * MIB),
    )(core, tokens, cotangent)


def grad_kernel(x_ref, y_ref, *refs, start):
    o_ref = refs[-1]
    step = 256
    per = step // ROWS

    @pl.loop(0, o_ref.shape[0] // per)
    def _(i):
        rows = x_ref[pl.ds(pl.multiple_of(start + i * step, step), step), :]
        o_ref[pl.ds(i * per, per)] = scaled_dot(rows, y_ref[...])


def grad(rows, cotangent, start=0, count=None, kept=()):
    count = count or rows.shape[0]
    return pl.pallas_call(
        functools.partial(grad_kernel, start=start),
        out_shape=jax.ShapeDtypeStruct((count // ROWS, ROWS, FEATURES), jnp.float32),
        in_specs=[VMEM] * (2 + len(kept)),
        out_specs=VMEM,
        compiler_params=params(8),
        cost_estimate=cost(2 * cotangent.shape[0] * count * FEATURES, 12 * MIB),
    )(rows, cotangent, *kept)


def parts_specs(parts):
    steps = parts[0].shape[0] // 4
    return [
        pl.BlockSpec(
            (4, ROWS, FEATURES),
            lambda i, n=n: (jnp.clip(i - n * steps, 0, steps - 1), 0, 0),
        )
        for n in range(len(parts))
    ]


def block_of(refs, steps):
    block = refs[0][...]
    for n in range(1, len(refs)):
        block = jnp.where(pl.program_id(0) >= n * steps, refs[n][...], block)
    return block


def add_sums(is_first, a, b, acc_ref, o_ref):
    step = pl.program_id(0)

    @pl.when(step == 0)
    def _():
        acc_ref[...] = jnp.zeros_like(acc_ref)

    a = a.reshape(-1, 8, FEATURES)
    b = b.reshape(-1, 8, FEATURES)
    own, other = jnp.sum(a * a, axis=0), jnp.sum(b * b, axis=0)
    acc_ref[0] += jnp.sum(a * b, axis=0)
    acc_ref[1] += jnp.where(is_first, own, other)
    acc_ref[2] += jnp.where(is_first, other, own)

    @pl.when(step == pl.num_programs(0) - 1)
    def _():
        rows = [jnp.sum(acc_ref[k], axis=0, keepdims=True) for k in range(3)]
        rows = [jnp.sum(row, axis=1, keepdims=True) for row in rows]
        rows = [jnp.broadcast_to(row, (1, 128)) for row in rows]
        o_ref[0] = jnp.concatenate(rows + [jnp.zeros((5, 128), jnp.float32)], axis=0)


def pair_kernel(core_ref, a_ref, *refs, steps):
    b_refs, (o_ref, acc_ref) = refs[:-2], refs[-2:]
    add_sums(core_ref[0] == 0, a_ref[...], block_of(b_refs, steps), acc_ref, o_ref)


SUMS = jax.ShapeDtypeStruct((1, 8, 128), jnp.float32)
SUMS_SPEC = pl.BlockSpec((1, 8, 128), lambda i: (0, 0, 0))


def pair_sums(core, a, b):
    spec = pl.BlockSpec((4, ROWS, FEATURES), lambda i: (i, 0, 0))
    return pl.pallas_call(
        functools.partial(pair_kernel, steps=b[0].shape[0] // 4),
        out_shape=SUMS,
        grid=(CHIPS // 4,),
        in_specs=[SMEM, spec] + parts_specs(b),
        out_specs=SUMS_SPEC,
        scratch_shapes=[pltpu.VMEM((3, 8, FEATURES), jnp.float32)],
        compiler_params=params(10),
        cost_estimate=cost(a.size, a.size),
    )(core, a, *b)


def grad_pair_kernel(core_ref, x_ref, y_ref, *refs, steps):
    b_refs, (grad_ref, o_ref, acc_ref) = refs[:-3], refs[-3:]
    grad_ref[...] = scaled_dot(x_ref[...], y_ref[...])
    add_sums(core_ref[0] == 0, grad_ref[...], block_of(b_refs, steps), acc_ref, o_ref)


def grad_and_pair_sums(core, rows, cotangent, b):
    count, depth = rows.shape
    step = 4 * ROWS
    return pl.pallas_call(
        functools.partial(grad_pair_kernel, steps=b[0].shape[0] // 4),
        out_shape=(jax.ShapeDtypeStruct((CHIPS, ROWS, FEATURES), jnp.float32), SUMS),
        grid=(count // step,),
        in_specs=[
            SMEM,
            pl.BlockSpec((step, depth), lambda i: (i, 0)),
            pl.BlockSpec((depth, FEATURES), lambda i: (0, 0)),
        ]
        + parts_specs(b),
        out_specs=(pl.BlockSpec((4, ROWS, FEATURES), lambda i: (i, 0, 0)), SUMS_SPEC),
        scratch_shapes=[pltpu.VMEM((3, 8, FEATURES), jnp.float32)],
        compiler_params=params(56),
        cost_estimate=cost(2 * depth * count * FEATURES, 16 * MIB),
    )(core, rows, cotangent, *b)


def merge_kernel(core_ref, a_ref, *refs, parts, steps):
    b_refs, sums_refs, (o_ref, norm_ref) = refs[:parts], refs[parts:-2], refs[-2:]
    sums = sum(jnp.sum(ref[...], axis=0) for ref in sums_refs)
    cross, p, q = sums[0:1], sums[1:2], sums[2:3]
    is_first = core_ref[0] == 0
    first = 1.0 - cross / (2.0 * (p + EPSILON))
    second = 1.0 - cross / (2.0 * (q + EPSILON))
    squares = first * first * p + second * second * q
    square = jnp.maximum(squares + 2.0 * first * second * cross, 1e-6 * squares)
    norm = jnp.sqrt(jnp.maximum(square, 1e-30))
    scale = SENT_NORM / norm
    norm_ref[...] = jnp.broadcast_to(norm * (1.0 / SENT_NORM), norm_ref.shape)
    own = jnp.where(is_first, first, second) * scale
    other = jnp.where(is_first, second, first) * scale
    own = jnp.concatenate([own] * (FEATURES // 128), axis=1)[None]
    other = jnp.concatenate([other] * (FEATURES // 128), axis=1)[None]
    o_ref[...] = own * a_ref[...] + other * block_of(b_refs, steps)


def merge_pair(core, a, b, sums, mib):
    spec = pl.BlockSpec((4, ROWS, FEATURES), lambda i: (i, 0, 0))
    return pl.pallas_call(
        functools.partial(merge_kernel, parts=len(b), steps=b[0].shape[0] // 4),
        out_shape=(
            jax.ShapeDtypeStruct(a.shape, jnp.float32),
            jax.ShapeDtypeStruct((8, 128), jnp.float32),
        ),
        grid=(CHIPS // 4,),
        in_specs=[SMEM, spec] + parts_specs(b) + [VMEM] * len(sums),
        out_specs=(spec, pl.BlockSpec((8, 128), lambda i: (0, 0))),
        compiler_params=params(mib),
        cost_estimate=cost(a.size, a.size),
    )(core, a, *b, *sums)


def gram_kernel(place_ref, v_ref, norm_ref, *refs):
    earlier_refs, (o_ref, t_ref) = refs[:-2], refs[-2:]
    t_ref[...] = jnp.zeros_like(t_ref)
    for gi in range(4):
        for gj in range(gi, 4):
            pairs = [
                (i, j)
                for i in range(4 * gi, 4 * gi + 4)
                for j in range(4 * gj, 4 * gj + 4)
                if i <= j
            ]

            def body(r, sums, pairs=pairs):
                sums = list(sums)
                rows = pl.ds(pl.multiple_of(r * 8, 8), 8)
                for lane in range(FEATURES // 128):
                    held = {}
                    for i, j in pairs:
                        for k in (i, j):
                            if k not in held:
                                held[k] = v_ref[k, rows, pl.ds(lane * 128, 128)]
                    for n, (i, j) in enumerate(pairs):
                        sums[n] = sums[n] + held[i] * held[j]
                return tuple(sums)

            zero = jnp.zeros((8, 128), jnp.float32)
            sums = lax.fori_loop(0, ROWS // 8, body, (zero,) * len(pairs))
            for pair, total in zip(pairs, sums):
                t_ref[pl.ds(PAIRS[pair], 1), :] = jnp.sum(total, axis=0, keepdims=True)
    lane = lax.broadcasted_iota(jnp.int32, (1, 128), 1)
    shown = (lane == 0) & (place_ref[1] == 1)
    t_ref[pl.ds(len(PAIRS) + place_ref[0], 1), :] = jnp.where(shown, norm_ref[0:1, :], 0.0)
    rows = [ref[...] for ref in earlier_refs]
    for part in range(2):
        rows.append(jnp.sum(t_ref[pl.ds(part * 128, 128), :].T, axis=0, keepdims=True))
    tile = jnp.concatenate(rows, axis=0)
    o_ref[...] = tile if o_ref.ndim == 2 else jnp.broadcast_to(tile[None], o_ref.shape)


def gram(place, v, norm, earlier, out_dims):
    return pl.pallas_call(
        gram_kernel,
        out_shape=jax.ShapeDtypeStruct(out_dims, jnp.float32),
        in_specs=[SMEM] + [VMEM] * (2 + len(earlier)),
        out_specs=VMEM,
        scratch_shapes=[pltpu.VMEM((256, 128), jnp.float32)],
        compiler_params=params(16),
        cost_estimate=cost(20 << 20, 4 * v.size),
    )(place, v, norm, *earlier)


def tree_coefs(read):
    count = CHIPS
    norms = [read(len(PAIRS) + i) for i in range(count)]
    table = {pair: read(n) for pair, n in PAIRS.items()}
    weights = list(norms)
    span = 1
    while count > 1:
        own = []
        for k in range(0, count, 2):
            cross = table[k, k + 1] * (norms[k] * norms[k + 1])
            for m in (k, k + 1):
                square = table[m, m] * (norms[m] * norms[m])
                own.append(1.0 - cross / (2.0 * (square + EPSILON)))
        weights = [w * own[i // span] for i, w in enumerate(weights)]
        factors = [c * n for c, n in zip(own, norms)]
        table = {key: value * (factors[key[0]] * factors[key[1]]) for key, value in table.items()}
        count //= 2
        merged = {}
        for k in range(count):
            merged[k, k] = (
                table[2 * k, 2 * k]
                + 2.0 * table[2 * k, 2 * k + 1]
                + table[2 * k + 1, 2 * k + 1]
            )
            for m in range(k + 1, count):
                merged[k, m] = (
                    table[2 * k, 2 * m]
                    + table[2 * k, 2 * m + 1]
                    + table[2 * k + 1, 2 * m]
                    + table[2 * k + 1, 2 * m + 1]
                )
        table = merged
        norms = [1.0] * count
        span *= 2
    return weights


def update_kernel(totals_ref, *refs):
    ins, outs, (sum_ref, scalar_ref, sem) = refs[:6], refs[6:10], refs[10:]
    sum_ref[...] = jnp.sum(totals_ref[...], axis=0)
    copy = pltpu.make_async_copy(sum_ref, scalar_ref, sem)
    copy.start()
    copy.wait()
    weights = [
        tree_coefs(lambda n, t=t: scalar_ref[2 * t + n // 128, n % 128]) for t in range(2)
    ]
    for t in range(2):
        v_ref, weight_ref, moment_ref = ins[3 * t : 3 * t + 3]
        new_weight_ref, new_moment_ref = outs[2 * t : 2 * t + 2]

        @pl.loop(0, ROWS // 8)
        def _(r, t=t, v_ref=v_ref, weight_ref=weight_ref, moment_ref=moment_ref, new_weight_ref=new_weight_ref, new_moment_ref=new_moment_ref):
            rows = pl.ds(pl.multiple_of(r * 8, 8), 8)
            merged = weights[t][0] * v_ref[0, rows, :]
            for i in range(1, CHIPS):
                merged = merged + weights[t][i] * v_ref[i, rows, :]
            moment = MOMENTUM_DECAY * moment_ref[rows, :] + merged
            new_moment_ref[rows, :] = moment
            new_weight_ref[rows, :] = weight_ref[rows, :] - STEP_SIZE * moment


def update(totals, *arrays):
    out = jax.ShapeDtypeStruct((ROWS, FEATURES), jnp.float32)
    return pl.pallas_call(
        update_kernel,
        out_shape=(out,) * 4,
        in_specs=[VMEM] * 7,
        out_specs=(VMEM,) * 4,
        scratch_shapes=[
            pltpu.VMEM((4, 128), jnp.float32),
            pltpu.SMEM((4, 128), jnp.float32),
            pltpu.SemaphoreType.DMA,
        ],
        compiler_params=params(8),
        cost_estimate=cost(8 << 20, 10 * MIB),
    )(totals, *arrays)


def after(value, *others):
    return lax.optimization_barrier((value,) + others)[0]


def shards(
    tokens, key_cotangent, value_cotangent, key_weight, value_weight, key_moment, value_moment
):
    shard_count, replicas = lax.axis_size("shard"), lax.axis_size("rep")
    index = lax.axis_index("rep").astype(jnp.int32)
    core = (index & 1)[None]
    leader = ((lax.axis_index("shard") == 0) & (index & 1 == 0)).astype(jnp.int32)
    place = jnp.stack([CHIPS - 1 - (index >> 1), leader])
    swap = [(i, i ^ 1) for i in range(replicas)]
    core_groups = [list(range(c, replicas, 2))[::-1] for c in range(2)]

    def summed(sums):
        sums = sums + lax.ppermute(sums, "rep", swap)
        shifts = [
            [(s, (s + d) % shard_count) for s in range(shard_count)] for d in range(1, shard_count)
        ]
        return [sums] + [lax.ppermute(sums, "shard", shift) for shift in shifts]

    def gathered(sent):
        return lax.all_to_all(sent, "rep", 0, 0, axis_index_groups=core_groups)

    key_other, own_rows, other_rows = split_and_grad(core, tokens, key_cotangent)
    key_arrived = [lax.ppermute(key_other, "rep", swap)]
    key_own = grad(own_rows, key_cotangent)
    half = other_rows.shape[0] // 2
    value_first = grad(after(other_rows, key_own), value_cotangent, 0, half, [key_own])
    key_sums = summed(pair_sums(after(core, value_first), key_own, key_arrived))
    value_second = grad(
        after(other_rows, key_sums[0]), value_cotangent, half, half, [key_own] + key_arrived
    )
    key_merged, key_norm = merge_pair(core, key_own, key_arrived, key_sums, 12)
    key_sent = key_merged.astype(jnp.float16)
    key_all = gathered(key_sent)

    value_arrived = [
        lax.ppermute(value_first, "rep", swap),
        lax.ppermute(after(value_second, key_sent), "rep", swap),
    ]
    value_own, value_sums = grad_and_pair_sums(
        core, after(own_rows, key_sent), value_cotangent, value_arrived
    )
    value_sums = summed(value_sums)
    value_merged, value_norm = merge_pair(core, value_own, value_arrived, value_sums, 50)
    value_all = gathered(value_merged.astype(jnp.float16))

    key_v = key_all.astype(jnp.float32)
    key_vector = gram(place, key_v, key_norm, [], (2, 128))
    value_v = value_all.astype(jnp.float32)
    vectors = gram(place, value_v, value_norm, [key_vector], (shard_count * replicas, 4, 128))
    totals = lax.all_to_all(vectors, ("shard", "rep"), 0, 0)
    new_key_weight, new_key_moment, new_value_weight, new_value_moment = update(
        totals, key_v, key_weight, key_moment, value_v, value_weight, value_moment
    )
    return (new_key_weight, new_value_weight, new_key_moment, new_value_moment)


def solution(mesh):
    in_specs = (
        P("rep", "shard"),
        P("rep", None),
        P("rep", None),
        P(("shard", "rep"), None),
        P(("shard", "rep"), None),
        P(("shard", "rep"), None),
        P(("shard", "rep"), None),
    )
    out_specs = (
        P(("shard", "rep"), None),
        P(("shard", "rep"), None),
        P(("shard", "rep"), None),
        P(("shard", "rep"), None),
    )
    return jax.shard_map(shards, mesh=mesh, in_specs=in_specs, out_specs=out_specs, check_vma=False)
```

```python
import functools
import math

import jax
import jax.numpy as jnp
from jax import lax
from jax.experimental import pallas as pl
from jax.experimental.pallas import tpu as pltpu
from jax.sharding import PartitionSpec as P

EPSILON = 1e-06
MOMENTUM_DECAY = 0.9
STEP_SIZE = 0.01
CHIPS = 16
ROWS = 64
FEATURES = 1024
SENT_NORM = 16384.0
MIB = 1 << 20
PAIRS = {pair: n for n, pair in enumerate((i, j) for i in range(CHIPS) for j in range(i, CHIPS))}


def params(mib):
    return pltpu.CompilerParams(vmem_limit_bytes=mib * MIB)


def cost(flops, moved):
    return pl.CostEstimate(flops=flops, bytes_accessed=moved, transcendentals=0)


VMEM = pl.BlockSpec(memory_space=pltpu.VMEM)
SMEM = pl.BlockSpec(memory_space=pltpu.SMEM)


def scaled_dot(rows, cotangent):
    product = jnp.dot(rows, cotangent, preferred_element_type=jnp.float32)
    return (product * (1.0 / math.sqrt(rows.shape[1]))).reshape(-1, ROWS, FEATURES)


def split_kernel(core_ref, x_hbm, y_hbm, grad_ref, own_ref, other_ref, x_ref, y_ref, x_sems, y_sem):
    steps, depth, width = x_ref.shape
    x_copies = [
        pltpu.make_async_copy(
            x_hbm.at[:, pl.ds((steps - 1 - i) * width, width)], x_ref.at[i], x_sems.at[i]
        )
        for i in range(steps)
    ]
    y_copy = pltpu.make_async_copy(y_hbm, y_ref, y_sem)
    x_copies[0].start()
    y_copy.start()
    for copy in x_copies[1:]:
        copy.start()
    is_first = core_ref[0] == 0
    half = width // 2
    per = half // ROWS
    for i in range(steps):
        x_copies[i].wait()
        blocks = x_ref[i].T.reshape(-1, 2, ROWS, depth)
        order = range(blocks.shape[0] - 1, -1, -1)
        first = jnp.concatenate([blocks[n, 0] for n in order], axis=0)
        second = jnp.concatenate([blocks[n, 1] for n in order], axis=0)
        own_ref[pl.ds(i * half, half), :] = jnp.where(is_first, first, second)
        other = jnp.where(is_first, second, first)
        other_ref[pl.ds(i * half, half), :] = other
        if i == 0:
            y_copy.wait()
        grad_ref[pl.ds(i * per, per)] = scaled_dot(other, y_ref[...])


def split_and_grad(core, tokens, cotangent):
    depth, width = tokens.shape
    step = 512
    half = jax.ShapeDtypeStruct((width // 2, depth), jnp.bfloat16)
    hbm = pl.BlockSpec(memory_space=pltpu.HBM)
    return pl.pallas_call(
        split_kernel,
        out_shape=(
            jax.ShapeDtypeStruct((CHIPS, ROWS, FEATURES), jnp.float32),
            half,
            half,
        ),
        in_specs=[SMEM, hbm, hbm],
        out_specs=(VMEM,) * 3,
        scratch_shapes=[
            pltpu.VMEM((width // step, depth, step), jnp.bfloat16),
            pltpu.VMEM(cotangent.shape, jnp.bfloat16),
            pltpu.SemaphoreType.DMA((width // step,)),
            pltpu.SemaphoreType.DMA,
        ],
        compiler_params=params(32),
        cost_estimate=cost(depth * width * FEATURES, 24 * MIB),
    )(core, tokens, cotangent)


def grad_kernel(x_ref, y_ref, *refs, start):
    o_ref = refs[-1]
    step = 256
    per = step // ROWS

    @pl.loop(0, o_ref.shape[0] // per)
    def _(i):
        rows = x_ref[pl.ds(pl.multiple_of(start + i * step, step), step), :]
        o_ref[pl.ds(i * per, per)] = scaled_dot(rows, y_ref[...])


def grad(rows, cotangent, start=0, count=None, kept=()):
    count = count or rows.shape[0]
    return pl.pallas_call(
        functools.partial(grad_kernel, start=start),
        out_shape=jax.ShapeDtypeStruct((count // ROWS, ROWS, FEATURES), jnp.float32),
        in_specs=[VMEM] * (2 + len(kept)),
        out_specs=VMEM,
        compiler_params=params(8),
        cost_estimate=cost(2 * cotangent.shape[0] * count * FEATURES, 12 * MIB),
    )(rows, cotangent, *kept)


def parts_specs(parts):
    steps = parts[0].shape[0] // 4
    return [
        pl.BlockSpec(
            (4, ROWS, FEATURES),
            lambda i, n=n: (jnp.clip(i - n * steps, 0, steps - 1), 0, 0),
        )
        for n in range(len(parts))
    ]


def block_of(refs, steps):
    block = refs[0][...]
    for n in range(1, len(refs)):
        block = jnp.where(pl.program_id(0) >= n * steps, refs[n][...], block)
    return block


def add_sums(is_first, a, b, acc_ref, o_ref):
    step = pl.program_id(0)

    @pl.when(step == 0)
    def _():
        acc_ref[...] = jnp.zeros_like(acc_ref)

    a = a.reshape(-1, 8, FEATURES)
    b = b.reshape(-1, 8, FEATURES)
    own, other = jnp.sum(a * a, axis=0), jnp.sum(b * b, axis=0)
    acc_ref[0] += jnp.sum(a * b, axis=0)
    acc_ref[1] += jnp.where(is_first, own, other)
    acc_ref[2] += jnp.where(is_first, other, own)

    @pl.when(step == pl.num_programs(0) - 1)
    def _():
        rows = [jnp.sum(acc_ref[k], axis=0, keepdims=True) for k in range(3)]
        rows = [jnp.sum(row, axis=1, keepdims=True) for row in rows]
        rows = [jnp.broadcast_to(row, (1, 128)) for row in rows]
        o_ref[0] = jnp.concatenate(rows + [jnp.zeros((5, 128), jnp.float32)], axis=0)


def pair_kernel(core_ref, a_ref, *refs, steps):
    b_refs, (o_ref, acc_ref) = refs[:-2], refs[-2:]
    add_sums(core_ref[0] == 0, a_ref[...], block_of(b_refs, steps), acc_ref, o_ref)


SUMS = jax.ShapeDtypeStruct((1, 8, 128), jnp.float32)
SUMS_SPEC = pl.BlockSpec((1, 8, 128), lambda i: (0, 0, 0))


def pair_sums(core, a, b):
    spec = pl.BlockSpec((4, ROWS, FEATURES), lambda i: (i, 0, 0))
    return pl.pallas_call(
        functools.partial(pair_kernel, steps=b[0].shape[0] // 4),
        out_shape=SUMS,
        grid=(CHIPS // 4,),
        in_specs=[SMEM, spec] + parts_specs(b),
        out_specs=SUMS_SPEC,
        scratch_shapes=[pltpu.VMEM((3, 8, FEATURES), jnp.float32)],
        compiler_params=params(10),
        cost_estimate=cost(a.size, a.size),
    )(core, a, *b)


def grad_pair_kernel(core_ref, x_ref, y_ref, *refs, steps):
    b_refs, (grad_ref, o_ref, acc_ref) = refs[:-3], refs[-3:]
    grad_ref[...] = scaled_dot(x_ref[...], y_ref[...])
    add_sums(core_ref[0] == 0, grad_ref[...], block_of(b_refs, steps), acc_ref, o_ref)


def grad_and_pair_sums(core, rows, cotangent, b):
    count, depth = rows.shape
    step = 4 * ROWS
    return pl.pallas_call(
        functools.partial(grad_pair_kernel, steps=b[0].shape[0] // 4),
        out_shape=(jax.ShapeDtypeStruct((CHIPS, ROWS, FEATURES), jnp.float32), SUMS),
        grid=(count // step,),
        in_specs=[
            SMEM,
            pl.BlockSpec((step, depth), lambda i: (i, 0)),
            pl.BlockSpec((depth, FEATURES), lambda i: (0, 0)),
        ]
        + parts_specs(b),
        out_specs=(pl.BlockSpec((4, ROWS, FEATURES), lambda i: (i, 0, 0)), SUMS_SPEC),
        scratch_shapes=[pltpu.VMEM((3, 8, FEATURES), jnp.float32)],
        compiler_params=params(24),
        cost_estimate=cost(2 * depth * count * FEATURES, 16 * MIB),
    )(core, rows, cotangent, *b)


def merge_kernel(core_ref, a_ref, *refs, parts, steps):
    b_refs, sums_refs, (o_ref, norm_ref) = refs[:parts], refs[parts:-2], refs[-2:]
    sums = sum(jnp.sum(ref[...], axis=0) for ref in sums_refs)
    cross, p, q = sums[0:1], sums[1:2], sums[2:3]
    is_first = core_ref[0] == 0
    first = 1.0 - cross / (2.0 * (p + EPSILON))
    second = 1.0 - cross / (2.0 * (q + EPSILON))
    squares = first * first * p + second * second * q
    square = jnp.maximum(squares + 2.0 * first * second * cross, 1e-6 * squares)
    norm = jnp.sqrt(jnp.maximum(square, 1e-30))
    scale = SENT_NORM / norm
    norm_ref[...] = jnp.broadcast_to(norm * (1.0 / SENT_NORM), norm_ref.shape)
    own = jnp.where(is_first, first, second) * scale
    other = jnp.where(is_first, second, first) * scale
    own = jnp.concatenate([own] * (FEATURES // 128), axis=1)[None]
    other = jnp.concatenate([other] * (FEATURES // 128), axis=1)[None]
    o_ref[...] = own * a_ref[...] + other * block_of(b_refs, steps)


def merge_pair(core, a, b, sums, mib):
    spec = pl.BlockSpec((4, ROWS, FEATURES), lambda i: (i, 0, 0))
    return pl.pallas_call(
        functools.partial(merge_kernel, parts=len(b), steps=b[0].shape[0] // 4),
        out_shape=(
            jax.ShapeDtypeStruct(a.shape, jnp.float32),
            jax.ShapeDtypeStruct((8, 128), jnp.float32),
        ),
        grid=(CHIPS // 4,),
        in_specs=[SMEM, spec] + parts_specs(b) + [VMEM] * len(sums),
        out_specs=(spec, pl.BlockSpec((8, 128), lambda i: (0, 0))),
        compiler_params=params(mib),
        cost_estimate=cost(a.size, a.size),
    )(core, a, *b, *sums)


def gram_kernel(place_ref, v_ref, norm_ref, *refs):
    earlier_refs, (o_ref, t_ref) = refs[:-2], refs[-2:]
    t_ref[...] = jnp.zeros_like(t_ref)
    for gi in range(4):
        for gj in range(gi, 4):
            pairs = [
                (i, j)
                for i in range(4 * gi, 4 * gi + 4)
                for j in range(4 * gj, 4 * gj + 4)
                if i <= j
            ]

            def body(r, sums, pairs=pairs):
                sums = list(sums)
                rows = pl.ds(pl.multiple_of(r * 8, 8), 8)
                for lane in range(FEATURES // 128):
                    held = {}
                    for i, j in pairs:
                        for k in (i, j):
                            if k not in held:
                                held[k] = v_ref[k, rows, pl.ds(lane * 128, 128)]
                    for n, (i, j) in enumerate(pairs):
                        sums[n] = sums[n] + held[i] * held[j]
                return tuple(sums)

            zero = jnp.zeros((8, 128), jnp.float32)
            sums = lax.fori_loop(0, ROWS // 8, body, (zero,) * len(pairs))
            for pair, total in zip(pairs, sums):
                t_ref[pl.ds(PAIRS[pair], 1), :] = jnp.sum(total, axis=0, keepdims=True)
    lane = lax.broadcasted_iota(jnp.int32, (1, 128), 1)
    shown = (lane == 0) & (place_ref[1] == 1)
    t_ref[pl.ds(len(PAIRS) + place_ref[0], 1), :] = jnp.where(shown, norm_ref[0:1, :], 0.0)
    rows = [ref[...] for ref in earlier_refs]
    for part in range(2):
        rows.append(jnp.sum(t_ref[pl.ds(part * 128, 128), :].T, axis=0, keepdims=True))
    tile = jnp.concatenate(rows, axis=0)
    o_ref[...] = tile if o_ref.ndim == 2 else jnp.broadcast_to(tile[None], o_ref.shape)


def gram(place, v, norm, earlier, out_dims):
    return pl.pallas_call(
        gram_kernel,
        out_shape=jax.ShapeDtypeStruct(out_dims, jnp.float32),
        in_specs=[SMEM] + [VMEM] * (2 + len(earlier)),
        out_specs=VMEM,
        scratch_shapes=[pltpu.VMEM((256, 128), jnp.float32)],
        compiler_params=params(16),
        cost_estimate=cost(20 << 20, 4 * v.size),
    )(place, v, norm, *earlier)


def tree_coefs(read):
    count = CHIPS
    norms = [read(len(PAIRS) + i) for i in range(count)]
    table = {pair: read(n) for pair, n in PAIRS.items()}
    weights = list(norms)
    span = 1
    while count > 1:
        own = []
        for k in range(0, count, 2):
            cross = table[k, k + 1] * (norms[k] * norms[k + 1])
            for m in (k, k + 1):
                square = table[m, m] * (norms[m] * norms[m])
                own.append(1.0 - cross / (2.0 * (square + EPSILON)))
        weights = [w * own[i // span] for i, w in enumerate(weights)]
        factors = [c * n for c, n in zip(own, norms)]
        table = {key: value * (factors[key[0]] * factors[key[1]]) for key, value in table.items()}
        count //= 2
        merged = {}
        for k in range(count):
            merged[k, k] = (
                table[2 * k, 2 * k]
                + 2.0 * table[2 * k, 2 * k + 1]
                + table[2 * k + 1, 2 * k + 1]
            )
            for m in range(k + 1, count):
                merged[k, m] = (
                    table[2 * k, 2 * m]
                    + table[2 * k, 2 * m + 1]
                    + table[2 * k + 1, 2 * m]
                    + table[2 * k + 1, 2 * m + 1]
                )
        table = merged
        norms = [1.0] * count
        span *= 2
    return weights


def update_kernel(totals_ref, *refs):
    ins, outs, (sum_ref, scalar_ref, sem) = refs[:6], refs[6:10], refs[10:]
    sum_ref[...] = jnp.sum(totals_ref[...], axis=0)
    copy = pltpu.make_async_copy(sum_ref, scalar_ref, sem)
    copy.start()
    copy.wait()
    weights = [
        tree_coefs(lambda n, t=t: scalar_ref[2 * t + n // 128, n % 128]) for t in range(2)
    ]
    for t in range(2):
        v_ref, weight_ref, moment_ref = ins[3 * t : 3 * t + 3]
        new_weight_ref, new_moment_ref = outs[2 * t : 2 * t + 2]

        @pl.loop(0, ROWS // 8)
        def _(r, t=t, v_ref=v_ref, weight_ref=weight_ref, moment_ref=moment_ref, new_weight_ref=new_weight_ref, new_moment_ref=new_moment_ref):
            rows = pl.ds(pl.multiple_of(r * 8, 8), 8)
            merged = weights[t][0] * v_ref[0, rows, :]
            for i in range(1, CHIPS):
                merged = merged + weights[t][i] * v_ref[i, rows, :]
            moment = MOMENTUM_DECAY * moment_ref[rows, :] + merged
            new_moment_ref[rows, :] = moment
            new_weight_ref[rows, :] = weight_ref[rows, :] - STEP_SIZE * moment


def update(totals, *arrays):
    out = jax.ShapeDtypeStruct((ROWS, FEATURES), jnp.float32)
    return pl.pallas_call(
        update_kernel,
        out_shape=(out,) * 4,
        in_specs=[VMEM] * 7,
        out_specs=(VMEM,) * 4,
        scratch_shapes=[
            pltpu.VMEM((4, 128), jnp.float32),
            pltpu.SMEM((4, 128), jnp.float32),
            pltpu.SemaphoreType.DMA,
        ],
        compiler_params=params(8),
        cost_estimate=cost(8 << 20, 10 * MIB),
    )(totals, *arrays)


def after(value, *others):
    return lax.optimization_barrier((value,) + others)[0]


def shards(
    tokens, key_cotangent, value_cotangent, key_weight, value_weight, key_moment, value_moment
):
    shard_count, replicas = lax.axis_size("shard"), lax.axis_size("rep")
    index = lax.axis_index("rep").astype(jnp.int32)
    core = (index & 1)[None]
    leader = ((lax.axis_index("shard") == 0) & (index & 1 == 0)).astype(jnp.int32)
    place = jnp.stack([CHIPS - 1 - (index >> 1), leader])
    swap = [(i, i ^ 1) for i in range(replicas)]
    core_groups = [list(range(c, replicas, 2))[::-1] for c in range(2)]

    def summed(sums):
        sums = sums + lax.ppermute(sums, "rep", swap)
        shifts = [
            [(s, (s + d) % shard_count) for s in range(shard_count)] for d in range(1, shard_count)
        ]
        return [sums] + [lax.ppermute(sums, "shard", shift) for shift in shifts]

    def gathered(sent):
        return lax.all_to_all(sent, "rep", 0, 0, axis_index_groups=core_groups)

    key_other, own_rows, other_rows = split_and_grad(core, tokens, key_cotangent)
    key_arrived = [lax.ppermute(key_other, "rep", swap)]
    key_own = grad(own_rows, key_cotangent)
    half = other_rows.shape[0] // 2
    value_first = grad(after(other_rows, key_own), value_cotangent, 0, half, [key_own])
    key_sums = summed(pair_sums(after(core, value_first), key_own, key_arrived))
    value_second = grad(
        after(other_rows, key_sums[0]), value_cotangent, half, half, [key_own] + key_arrived
    )
    key_merged, key_norm = merge_pair(core, key_own, key_arrived, key_sums, 12)
    key_sent = key_merged.astype(jnp.float16)
    key_all = gathered(key_sent)

    value_arrived = [
        lax.ppermute(value_first, "rep", swap),
        lax.ppermute(after(value_second, key_sent), "rep", swap),
    ]
    value_own, value_sums = grad_and_pair_sums(
        core, after(own_rows, key_sent), value_cotangent, value_arrived
    )
    value_sums = summed(value_sums)
    value_merged, value_norm = merge_pair(core, value_own, value_arrived, value_sums, 12)
    value_all = gathered(value_merged.astype(jnp.float16))

    key_v = key_all.astype(jnp.float32)
    key_vector = gram(place, key_v, key_norm, [], (2, 128))
    value_v = value_all.astype(jnp.float32)
    vectors = gram(place, value_v, value_norm, [key_vector], (shard_count * replicas, 4, 128))
    totals = lax.all_to_all(vectors, ("shard", "rep"), 0, 0)
    new_key_weight, new_key_moment, new_value_weight, new_value_moment = update(
        totals, key_v, key_weight, key_moment, value_v, value_weight, value_moment
    )
    return (new_key_weight, new_value_weight, new_key_moment, new_value_moment)


def solution(mesh):
    in_specs = (
        P("rep", "shard"),
        P("rep", None),
        P("rep", None),
        P(("shard", "rep"), None),
        P(("shard", "rep"), None),
        P(("shard", "rep"), None),
        P(("shard", "rep"), None),
    )
    out_specs = (
        P(("shard", "rep"), None),
        P(("shard", "rep"), None),
        P(("shard", "rep"), None),
        P(("shard", "rep"), None),
    )
    return jax.shard_map(shards, mesh=mesh, in_specs=in_specs, out_specs=out_specs, check_vma=False)
```

```python
import functools
import math

import jax
import jax.numpy as jnp
from jax import lax
from jax.experimental import pallas as pl
from jax.experimental.pallas import tpu as pltpu
from jax.sharding import PartitionSpec as P

EPSILON = 1e-06
MOMENTUM_DECAY = 0.9
STEP_SIZE = 0.01
CHIPS = 16
ROWS = 64
FEATURES = 1024
SENT_NORM = 16384.0
MIB = 1 << 20
PAIRS = {pair: n for n, pair in enumerate((i, j) for i in range(CHIPS) for j in range(i, CHIPS))}


def params(mib):
    return pltpu.CompilerParams(vmem_limit_bytes=mib * MIB)


def cost(flops, moved):
    return pl.CostEstimate(flops=flops, bytes_accessed=moved, transcendentals=0)


VMEM = pl.BlockSpec(memory_space=pltpu.VMEM)
SMEM = pl.BlockSpec(memory_space=pltpu.SMEM)


def scaled_dot(rows, cotangent):
    product = jnp.dot(rows, cotangent, preferred_element_type=jnp.float32)
    return (product * (1.0 / math.sqrt(rows.shape[1]))).reshape(-1, ROWS, FEATURES)


def split_kernel(core_ref, x_hbm, y_hbm, grad_ref, own_ref, other_ref, x_ref, y_ref, x_sems, y_sem):
    steps, depth, width = x_ref.shape
    x_copies = [
        pltpu.make_async_copy(
            x_hbm.at[:, pl.ds(i * width, width)], x_ref.at[i], x_sems.at[i]
        )
        for i in range(steps)
    ]
    y_copy = pltpu.make_async_copy(y_hbm, y_ref, y_sem)
    x_copies[0].start()
    y_copy.start()
    for copy in x_copies[1:]:
        copy.start()
    is_first = core_ref[0] == 0
    half = width // 2
    per = half // ROWS
    for i in range(steps):
        x_copies[i].wait()
        blocks = x_ref[i].T.reshape(-1, 2, ROWS, depth)
        first = blocks[:, 0].reshape(-1, depth)
        second = blocks[:, 1].reshape(-1, depth)
        own_ref[pl.ds(i * half, half), :] = jnp.where(is_first, first, second)
        other = jnp.where(is_first, second, first)
        other_ref[pl.ds(i * half, half), :] = other
        if i == 0:
            y_copy.wait()
        grad_ref[pl.ds(i * per, per)] = scaled_dot(other, y_ref[...])


def split_and_grad(core, tokens, cotangent):
    depth, width = tokens.shape
    step = 512
    half = jax.ShapeDtypeStruct((width // 2, depth), jnp.bfloat16)
    hbm = pl.BlockSpec(memory_space=pltpu.HBM)
    return pl.pallas_call(
        split_kernel,
        out_shape=(
            jax.ShapeDtypeStruct((CHIPS, ROWS, FEATURES), jnp.float32),
            half,
            half,
        ),
        in_specs=[SMEM, hbm, hbm],
        out_specs=(VMEM,) * 3,
        scratch_shapes=[
            pltpu.VMEM((width // step, depth, step), jnp.bfloat16),
            pltpu.VMEM(cotangent.shape, jnp.bfloat16),
            pltpu.SemaphoreType.DMA((width // step,)),
            pltpu.SemaphoreType.DMA,
        ],
        compiler_params=params(32),
        cost_estimate=cost(depth * width * FEATURES, 24 * MIB),
    )(core, tokens, cotangent)


def grad_kernel(x_ref, y_ref, *refs, start):
    o_ref = refs[-1]
    step = 256
    per = step // ROWS

    @pl.loop(0, o_ref.shape[0] // per)
    def _(i):
        rows = x_ref[pl.ds(pl.multiple_of(start + i * step, step), step), :]
        o_ref[pl.ds(i * per, per)] = scaled_dot(rows, y_ref[...])


def grad(rows, cotangent, start=0, count=None, kept=()):
    count = count or rows.shape[0]
    return pl.pallas_call(
        functools.partial(grad_kernel, start=start),
        out_shape=jax.ShapeDtypeStruct((count // ROWS, ROWS, FEATURES), jnp.float32),
        in_specs=[VMEM] * (2 + len(kept)),
        out_specs=VMEM,
        compiler_params=params(8),
        cost_estimate=cost(2 * cotangent.shape[0] * count * FEATURES, 12 * MIB),
    )(rows, cotangent, *kept)


def parts_specs(parts):
    steps = parts[0].shape[0] // 4
    return [
        pl.BlockSpec(
            (4, ROWS, FEATURES),
            lambda i, n=n: (jnp.clip(i - n * steps, 0, steps - 1), 0, 0),
        )
        for n in range(len(parts))
    ]


def block_of(refs, steps):
    block = refs[0][...]
    for n in range(1, len(refs)):
        block = jnp.where(pl.program_id(0) >= n * steps, refs[n][...], block)
    return block


def add_sums(is_first, a, b, acc_ref, o_ref):
    step = pl.program_id(0)

    @pl.when(step == 0)
    def _():
        acc_ref[...] = jnp.zeros_like(acc_ref)

    a = a.reshape(-1, 8, FEATURES)
    b = b.reshape(-1, 8, FEATURES)
    own, other = jnp.sum(a * a, axis=0), jnp.sum(b * b, axis=0)
    acc_ref[0] += jnp.sum(a * b, axis=0)
    acc_ref[1] += jnp.where(is_first, own, other)
    acc_ref[2] += jnp.where(is_first, other, own)

    @pl.when(step == pl.num_programs(0) - 1)
    def _():
        rows = [jnp.sum(acc_ref[k], axis=0, keepdims=True) for k in range(3)]
        rows = [jnp.sum(row, axis=1, keepdims=True) for row in rows]
        rows = [jnp.broadcast_to(row, (1, 128)) for row in rows]
        o_ref[0] = jnp.concatenate(rows + [jnp.zeros((5, 128), jnp.float32)], axis=0)


def pair_kernel(core_ref, a_ref, *refs, steps):
    b_refs, (o_ref, acc_ref) = refs[:-2], refs[-2:]
    add_sums(core_ref[0] == 0, a_ref[...], block_of(b_refs, steps), acc_ref, o_ref)


SUMS = jax.ShapeDtypeStruct((1, 8, 128), jnp.float32)
SUMS_SPEC = pl.BlockSpec((1, 8, 128), lambda i: (0, 0, 0))


def pair_sums(core, a, b):
    spec = pl.BlockSpec((4, ROWS, FEATURES), lambda i: (i, 0, 0))
    return pl.pallas_call(
        functools.partial(pair_kernel, steps=b[0].shape[0] // 4),
        out_shape=SUMS,
        grid=(CHIPS // 4,),
        in_specs=[SMEM, spec] + parts_specs(b),
        out_specs=SUMS_SPEC,
        scratch_shapes=[pltpu.VMEM((3, 8, FEATURES), jnp.float32)],
        compiler_params=params(10),
        cost_estimate=cost(a.size, a.size),
    )(core, a, *b)


def grad_pair_kernel(core_ref, x_ref, y_ref, *refs, steps):
    b_refs, (grad_ref, o_ref, acc_ref) = refs[:-3], refs[-3:]
    grad_ref[...] = scaled_dot(x_ref[...], y_ref[...])
    add_sums(core_ref[0] == 0, grad_ref[...], block_of(b_refs, steps), acc_ref, o_ref)


def grad_and_pair_sums(core, rows, cotangent, b):
    count, depth = rows.shape
    step = 4 * ROWS
    return pl.pallas_call(
        functools.partial(grad_pair_kernel, steps=b[0].shape[0] // 4),
        out_shape=(jax.ShapeDtypeStruct((CHIPS, ROWS, FEATURES), jnp.float32), SUMS),
        grid=(count // step,),
        in_specs=[
            SMEM,
            pl.BlockSpec((step, depth), lambda i: (i, 0)),
            pl.BlockSpec((depth, FEATURES), lambda i: (0, 0)),
        ]
        + parts_specs(b),
        out_specs=(pl.BlockSpec((4, ROWS, FEATURES), lambda i: (i, 0, 0)), SUMS_SPEC),
        scratch_shapes=[pltpu.VMEM((3, 8, FEATURES), jnp.float32)],
        compiler_params=params(24),
        cost_estimate=cost(2 * depth * count * FEATURES, 16 * MIB),
    )(core, rows, cotangent, *b)


def merge_kernel(core_ref, a_ref, *refs, parts, steps, backwards):
    b_refs, sums_refs, (o_ref, norm_ref) = refs[:parts], refs[parts:-2], refs[-2:]
    sums = sum(jnp.sum(ref[...], axis=0) for ref in sums_refs)
    cross, p, q = sums[0:1], sums[1:2], sums[2:3]
    is_first = core_ref[0] == 0
    first = 1.0 - cross / (2.0 * (p + EPSILON))
    second = 1.0 - cross / (2.0 * (q + EPSILON))
    squares = first * first * p + second * second * q
    square = jnp.maximum(squares + 2.0 * first * second * cross, 1e-6 * squares)
    norm = jnp.sqrt(jnp.maximum(square, 1e-30))
    scale = SENT_NORM / norm
    norm_ref[...] = jnp.broadcast_to(norm * (1.0 / SENT_NORM), norm_ref.shape)
    own = jnp.where(is_first, first, second) * scale
    other = jnp.where(is_first, second, first) * scale
    own = jnp.concatenate([own] * (FEATURES // 128), axis=1)[None]
    other = jnp.concatenate([other] * (FEATURES // 128), axis=1)[None]
    merged = own * a_ref[...] + other * block_of(b_refs, steps)
    count = merged.shape[0]
    for n in range(count):
        o_ref[n] = merged[count - 1 - n if backwards else n]


def merge_pair(core, a, b, sums, backwards):
    steps = CHIPS // 4
    out_spec = pl.BlockSpec(
        (4, ROWS, FEATURES), lambda i: (steps - 1 - i if backwards else i, 0, 0)
    )
    spec = pl.BlockSpec((4, ROWS, FEATURES), lambda i: (i, 0, 0))
    return pl.pallas_call(
        functools.partial(
            merge_kernel, parts=len(b), steps=b[0].shape[0] // 4, backwards=backwards
        ),
        out_shape=(
            jax.ShapeDtypeStruct(a.shape, jnp.float32),
            jax.ShapeDtypeStruct((8, 128), jnp.float32),
        ),
        grid=(CHIPS // 4,),
        in_specs=[SMEM, spec] + parts_specs(b) + [VMEM] * len(sums),
        out_specs=(out_spec, pl.BlockSpec((8, 128), lambda i: (0, 0))),
        compiler_params=params(12),
        cost_estimate=cost(a.size, a.size),
    )(core, a, *b, *sums)


def gram_kernel(place_ref, v_ref, norm_ref, *refs):
    earlier_refs, (o_ref, t_ref) = refs[:-2], refs[-2:]
    t_ref[...] = jnp.zeros_like(t_ref)
    for gi in range(4):
        for gj in range(gi, 4):
            pairs = [
                (i, j)
                for i in range(4 * gi, 4 * gi + 4)
                for j in range(4 * gj, 4 * gj + 4)
                if i <= j
            ]

            def body(r, sums, pairs=pairs):
                sums = list(sums)
                rows = pl.ds(pl.multiple_of(r * 8, 8), 8)
                for lane in range(FEATURES // 128):
                    held = {}
                    for i, j in pairs:
                        for k in (i, j):
                            if k not in held:
                                held[k] = v_ref[k, rows, pl.ds(lane * 128, 128)]
                    for n, (i, j) in enumerate(pairs):
                        sums[n] = sums[n] + held[i] * held[j]
                return tuple(sums)

            zero = jnp.zeros((8, 128), jnp.float32)
            sums = lax.fori_loop(0, ROWS // 8, body, (zero,) * len(pairs))
            for pair, total in zip(pairs, sums):
                t_ref[pl.ds(PAIRS[pair], 1), :] = jnp.sum(total, axis=0, keepdims=True)
    lane = lax.broadcasted_iota(jnp.int32, (1, 128), 1)
    shown = (lane == 0) & (place_ref[1] == 1)
    t_ref[pl.ds(len(PAIRS) + place_ref[0], 1), :] = jnp.where(shown, norm_ref[0:1, :], 0.0)
    rows = [ref[...] for ref in earlier_refs]
    for part in range(2):
        rows.append(jnp.sum(t_ref[pl.ds(part * 128, 128), :].T, axis=0, keepdims=True))
    tile = jnp.concatenate(rows, axis=0)
    o_ref[...] = tile if o_ref.ndim == 2 else jnp.broadcast_to(tile[None], o_ref.shape)


def gram(place, v, norm, earlier, out_dims):
    return pl.pallas_call(
        gram_kernel,
        out_shape=jax.ShapeDtypeStruct(out_dims, jnp.float32),
        in_specs=[SMEM] + [VMEM] * (2 + len(earlier)),
        out_specs=VMEM,
        scratch_shapes=[pltpu.VMEM((256, 128), jnp.float32)],
        compiler_params=params(16),
        cost_estimate=cost(20 << 20, 4 * v.size),
    )(place, v, norm, *earlier)


def tree_coefs(read):
    count = CHIPS
    norms = [read(len(PAIRS) + i) for i in range(count)]
    table = {pair: read(n) for pair, n in PAIRS.items()}
    weights = list(norms)
    span = 1
    while count > 1:
        own = []
        for k in range(0, count, 2):
            cross = table[k, k + 1] * (norms[k] * norms[k + 1])
            for m in (k, k + 1):
                square = table[m, m] * (norms[m] * norms[m])
                own.append(1.0 - cross / (2.0 * (square + EPSILON)))
        weights = [w * own[i // span] for i, w in enumerate(weights)]
        factors = [c * n for c, n in zip(own, norms)]
        table = {key: value * (factors[key[0]] * factors[key[1]]) for key, value in table.items()}
        count //= 2
        merged = {}
        for k in range(count):
            merged[k, k] = (
                table[2 * k, 2 * k]
                + 2.0 * table[2 * k, 2 * k + 1]
                + table[2 * k + 1, 2 * k + 1]
            )
            for m in range(k + 1, count):
                merged[k, m] = (
                    table[2 * k, 2 * m]
                    + table[2 * k, 2 * m + 1]
                    + table[2 * k + 1, 2 * m]
                    + table[2 * k + 1, 2 * m + 1]
                )
        table = merged
        norms = [1.0] * count
        span *= 2
    return weights


def update_kernel(totals_ref, *refs):
    ins, outs, (sum_ref, scalar_ref, sem) = refs[:6], refs[6:10], refs[10:]
    sum_ref[...] = jnp.sum(totals_ref[...], axis=0)
    copy = pltpu.make_async_copy(sum_ref, scalar_ref, sem)
    copy.start()
    copy.wait()
    weights = [
        tree_coefs(lambda n, t=t: scalar_ref[2 * t + n // 128, n % 128]) for t in range(2)
    ]
    for t in range(2):
        v_ref, weight_ref, moment_ref = ins[3 * t : 3 * t + 3]
        new_weight_ref, new_moment_ref = outs[2 * t : 2 * t + 2]

        @pl.loop(0, ROWS // 8)
        def _(r, t=t, v_ref=v_ref, weight_ref=weight_ref, moment_ref=moment_ref, new_weight_ref=new_weight_ref, new_moment_ref=new_moment_ref):
            rows = pl.ds(pl.multiple_of(r * 8, 8), 8)
            merged = weights[t][0] * v_ref[0, rows, :]
            for i in range(1, CHIPS):
                merged = merged + weights[t][i] * v_ref[i, rows, :]
            moment = MOMENTUM_DECAY * moment_ref[rows, :] + merged
            new_moment_ref[rows, :] = moment
            new_weight_ref[rows, :] = weight_ref[rows, :] - STEP_SIZE * moment


def update(totals, *arrays):
    out = jax.ShapeDtypeStruct((ROWS, FEATURES), jnp.float32)
    return pl.pallas_call(
        update_kernel,
        out_shape=(out,) * 4,
        in_specs=[VMEM] * 7,
        out_specs=(VMEM,) * 4,
        scratch_shapes=[
            pltpu.VMEM((4, 128), jnp.float32),
            pltpu.SMEM((4, 128), jnp.float32),
            pltpu.SemaphoreType.DMA,
        ],
        compiler_params=params(8),
        cost_estimate=cost(8 << 20, 10 * MIB),
    )(totals, *arrays)


def after(value, *others):
    return lax.optimization_barrier((value,) + others)[0]


def shards(
    tokens, key_cotangent, value_cotangent, key_weight, value_weight, key_moment, value_moment
):
    shard_count, replicas = lax.axis_size("shard"), lax.axis_size("rep")
    index = lax.axis_index("rep").astype(jnp.int32)
    core = (index & 1)[None]
    leader = ((lax.axis_index("shard") == 0) & (index & 1 == 0)).astype(jnp.int32)
    place = jnp.stack([index >> 1, leader])
    backwards_place = jnp.stack([CHIPS - 1 - (index >> 1), leader])
    swap = [(i, i ^ 1) for i in range(replicas)]
    core_groups = [list(range(c, replicas, 2)) for c in range(2)]
    backwards_groups = [group[::-1] for group in core_groups]

    def summed(sums):
        sums = sums + lax.ppermute(sums, "rep", swap)
        shifts = [
            [(s, (s + d) % shard_count) for s in range(shard_count)] for d in range(1, shard_count)
        ]
        return [sums] + [lax.ppermute(sums, "shard", shift) for shift in shifts]

    def gathered(sent, groups):
        return lax.all_to_all(sent, "rep", 0, 0, axis_index_groups=groups)

    key_other, own_rows, other_rows = split_and_grad(core, tokens, key_cotangent)
    key_arrived = [lax.ppermute(key_other, "rep", swap)]
    key_own = grad(own_rows, key_cotangent)
    half = other_rows.shape[0] // 2
    value_first = grad(after(other_rows, key_own), value_cotangent, 0, half, [key_own])
    key_sums = summed(pair_sums(after(core, value_first), key_own, key_arrived))
    value_second = grad(
        after(other_rows, key_sums[0]), value_cotangent, half, half, [key_own] + key_arrived
    )
    key_merged, key_norm = merge_pair(core, key_own, key_arrived, key_sums, False)
    key_sent = key_merged.astype(jnp.float16)
    key_all = gathered(key_sent, core_groups)

    value_arrived = [
        lax.ppermute(value_first, "rep", swap),
        lax.ppermute(after(value_second, key_sent), "rep", swap),
    ]
    value_own, value_sums = grad_and_pair_sums(
        core, after(own_rows, key_sent), value_cotangent, value_arrived
    )
    value_sums = summed(value_sums)
    value_merged, value_norm = merge_pair(core, value_own, value_arrived, value_sums, True)
    value_all = gathered(value_merged.astype(jnp.float16), backwards_groups)

    key_v = key_all.astype(jnp.float32)
    key_vector = gram(place, key_v, key_norm, [], (2, 128))
    value_v = value_all.astype(jnp.float32)
    vectors = gram(backwards_place, value_v, value_norm, [key_vector], (shard_count * replicas, 4, 128))
    totals = lax.all_to_all(vectors, ("shard", "rep"), 0, 0)
    new_key_weight, new_key_moment, new_value_weight, new_value_moment = update(
        totals, key_v, key_weight, key_moment, value_v, value_weight, value_moment
    )
    return (new_key_weight, new_value_weight, new_key_moment, new_value_moment)


def solution(mesh):
    in_specs = (
        P("rep", "shard"),
        P("rep", None),
        P("rep", None),
        P(("shard", "rep"), None),
        P(("shard", "rep"), None),
        P(("shard", "rep"), None),
        P(("shard", "rep"), None),
    )
    out_specs = (
        P(("shard", "rep"), None),
        P(("shard", "rep"), None),
        P(("shard", "rep"), None),
        P(("shard", "rep"), None),
    )
    return jax.shard_map(shards, mesh=mesh, in_specs=in_specs, out_specs=out_specs, check_vma=False)
```

```python
import functools
import math

import jax
import jax.numpy as jnp
from jax import lax
from jax.experimental import pallas as pl
from jax.experimental.pallas import tpu as pltpu
from jax.sharding import PartitionSpec as P

EPSILON = 1e-06
MOMENTUM_DECAY = 0.9
STEP_SIZE = 0.01
CHIPS = 16
ROWS = 64
FEATURES = 1024
SENT_NORM = 16384.0
MIB = 1 << 20
PAIRS = {pair: n for n, pair in enumerate((i, j) for i in range(CHIPS) for j in range(i, CHIPS))}


def params(mib):
    return pltpu.CompilerParams(vmem_limit_bytes=mib * MIB)


def cost(flops, moved):
    return pl.CostEstimate(flops=flops, bytes_accessed=moved, transcendentals=0)


VMEM = pl.BlockSpec(memory_space=pltpu.VMEM)
SMEM = pl.BlockSpec(memory_space=pltpu.SMEM)


def scaled_dot(rows, cotangent):
    product = jnp.dot(rows, cotangent, preferred_element_type=jnp.float32)
    return (product * (1.0 / math.sqrt(rows.shape[1]))).reshape(-1, ROWS, FEATURES)


def split_kernel(core_ref, x_hbm, y_hbm, grad_ref, own_ref, other_ref, x_ref, y_ref, x_sems, y_sem):
    steps, depth, width = x_ref.shape
    x_copies = [
        pltpu.make_async_copy(
            x_hbm.at[:, pl.ds(i * width, width)], x_ref.at[i], x_sems.at[i]
        )
        for i in range(steps)
    ]
    y_copy = pltpu.make_async_copy(y_hbm, y_ref, y_sem)
    x_copies[0].start()
    y_copy.start()
    for copy in x_copies[1:]:
        copy.start()
    is_first = core_ref[0] == 0
    half = width // 2
    per = half // ROWS
    for i in range(steps):
        x_copies[i].wait()
        blocks = x_ref[i].T.reshape(-1, 2, ROWS, depth)
        first = blocks[:, 0].reshape(-1, depth)
        second = blocks[:, 1].reshape(-1, depth)
        own_ref[pl.ds(i * half, half), :] = jnp.where(is_first, first, second)
        other = jnp.where(is_first, second, first)
        other_ref[pl.ds(i * half, half), :] = other
        if i == 0:
            y_copy.wait()
        grad_ref[pl.ds(i * per, per)] = scaled_dot(other, y_ref[...])


def split_and_grad(core, tokens, cotangent):
    depth, width = tokens.shape
    step = 512
    half = jax.ShapeDtypeStruct((width // 2, depth), jnp.bfloat16)
    hbm = pl.BlockSpec(memory_space=pltpu.HBM)
    return pl.pallas_call(
        split_kernel,
        out_shape=(
            jax.ShapeDtypeStruct((CHIPS, ROWS, FEATURES), jnp.float32),
            half,
            half,
        ),
        in_specs=[SMEM, hbm, hbm],
        out_specs=(VMEM,) * 3,
        scratch_shapes=[
            pltpu.VMEM((width // step, depth, step), jnp.bfloat16),
            pltpu.VMEM(cotangent.shape, jnp.bfloat16),
            pltpu.SemaphoreType.DMA((width // step,)),
            pltpu.SemaphoreType.DMA,
        ],
        compiler_params=params(32),
        cost_estimate=cost(depth * width * FEATURES, 24 * MIB),
    )(core, tokens, cotangent)


def grad_kernel(x_ref, y_ref, *refs, start):
    o_ref = refs[-1]
    step = 256
    per = step // ROWS

    @pl.loop(0, o_ref.shape[0] // per)
    def _(i):
        rows = x_ref[pl.ds(pl.multiple_of(start + i * step, step), step), :]
        o_ref[pl.ds(i * per, per)] = scaled_dot(rows, y_ref[...])


def grad(rows, cotangent, start=0, count=None, kept=()):
    count = count or rows.shape[0]
    return pl.pallas_call(
        functools.partial(grad_kernel, start=start),
        out_shape=jax.ShapeDtypeStruct((count // ROWS, ROWS, FEATURES), jnp.float32),
        in_specs=[VMEM] * (2 + len(kept)),
        out_specs=VMEM,
        compiler_params=params(8),
        cost_estimate=cost(2 * cotangent.shape[0] * count * FEATURES, 12 * MIB),
    )(rows, cotangent, *kept)


def parts_specs(parts):
    steps = parts[0].shape[0] // 4
    return [
        pl.BlockSpec(
            (4, ROWS, FEATURES),
            lambda i, n=n: (jnp.clip(i - n * steps, 0, steps - 1), 0, 0),
        )
        for n in range(len(parts))
    ]


def block_of(refs, steps):
    block = refs[0][...]
    for n in range(1, len(refs)):
        block = jnp.where(pl.program_id(0) >= n * steps, refs[n][...], block)
    return block


def add_sums(is_first, a, b, acc_ref, o_ref):
    step = pl.program_id(0)

    @pl.when(step == 0)
    def _():
        acc_ref[...] = jnp.zeros_like(acc_ref)

    a = a.reshape(-1, 8, FEATURES)
    b = b.reshape(-1, 8, FEATURES)
    own, other = jnp.sum(a * a, axis=0), jnp.sum(b * b, axis=0)
    acc_ref[0] += jnp.sum(a * b, axis=0)
    acc_ref[1] += jnp.where(is_first, own, other)
    acc_ref[2] += jnp.where(is_first, other, own)

    @pl.when(step == pl.num_programs(0) - 1)
    def _():
        rows = [jnp.sum(acc_ref[k], axis=0, keepdims=True) for k in range(3)]
        rows = [jnp.sum(row, axis=1, keepdims=True) for row in rows]
        rows = [jnp.broadcast_to(row, (1, 128)) for row in rows]
        o_ref[0] = jnp.concatenate(rows + [jnp.zeros((5, 128), jnp.float32)], axis=0)


def pair_kernel(core_ref, a_ref, *refs, steps):
    b_refs, (o_ref, acc_ref) = refs[:-2], refs[-2:]
    add_sums(core_ref[0] == 0, a_ref[...], block_of(b_refs, steps), acc_ref, o_ref)


SUMS = jax.ShapeDtypeStruct((1, 8, 128), jnp.float32)
SUMS_SPEC = pl.BlockSpec((1, 8, 128), lambda i: (0, 0, 0))


def pair_sums(core, a, b):
    spec = pl.BlockSpec((4, ROWS, FEATURES), lambda i: (i, 0, 0))
    return pl.pallas_call(
        functools.partial(pair_kernel, steps=b[0].shape[0] // 4),
        out_shape=SUMS,
        grid=(CHIPS // 4,),
        in_specs=[SMEM, spec] + parts_specs(b),
        out_specs=SUMS_SPEC,
        scratch_shapes=[pltpu.VMEM((3, 8, FEATURES), jnp.float32)],
        compiler_params=params(10),
        cost_estimate=cost(a.size, a.size),
    )(core, a, *b)


def grad_pair_kernel(core_ref, x_ref, y_ref, *refs, steps):
    b_refs, (grad_ref, o_ref, acc_ref) = refs[:-3], refs[-3:]
    grad_ref[...] = scaled_dot(x_ref[...], y_ref[...])
    add_sums(core_ref[0] == 0, grad_ref[...], block_of(b_refs, steps), acc_ref, o_ref)


def grad_and_pair_sums(core, rows, cotangent, b):
    count, depth = rows.shape
    step = 4 * ROWS
    return pl.pallas_call(
        functools.partial(grad_pair_kernel, steps=b[0].shape[0] // 4),
        out_shape=(jax.ShapeDtypeStruct((CHIPS, ROWS, FEATURES), jnp.float32), SUMS),
        grid=(count // step,),
        in_specs=[
            SMEM,
            pl.BlockSpec((step, depth), lambda i: (i, 0)),
            pl.BlockSpec((depth, FEATURES), lambda i: (0, 0)),
        ]
        + parts_specs(b),
        out_specs=(pl.BlockSpec((4, ROWS, FEATURES), lambda i: (i, 0, 0)), SUMS_SPEC),
        scratch_shapes=[pltpu.VMEM((3, 8, FEATURES), jnp.float32)],
        compiler_params=params(24),
        cost_estimate=cost(2 * depth * count * FEATURES, 16 * MIB),
    )(core, rows, cotangent, *b)


def merge_kernel(core_ref, a_ref, *refs, parts, steps, backwards):
    b_refs, sums_refs, (o_ref, norm_ref) = refs[:parts], refs[parts:-2], refs[-2:]
    sums = sum(jnp.sum(ref[...], axis=0) for ref in sums_refs)
    cross, p, q = sums[0:1], sums[1:2], sums[2:3]
    is_first = core_ref[0] == 0
    first = 1.0 - cross / (2.0 * (p + EPSILON))
    second = 1.0 - cross / (2.0 * (q + EPSILON))
    squares = first * first * p + second * second * q
    square = jnp.maximum(squares + 2.0 * first * second * cross, 1e-6 * squares)
    norm = jnp.sqrt(jnp.maximum(square, 1e-30))
    scale = SENT_NORM / norm
    norm_ref[...] = jnp.broadcast_to(norm * (1.0 / SENT_NORM), norm_ref.shape)
    own = jnp.where(is_first, first, second) * scale
    other = jnp.where(is_first, second, first) * scale
    own = jnp.concatenate([own] * (FEATURES // 128), axis=1)[None]
    other = jnp.concatenate([other] * (FEATURES // 128), axis=1)[None]
    merged = own * a_ref[...] + other * block_of(b_refs, steps)
    count = merged.shape[0]
    for n in range(count):
        o_ref[n] = merged[count - 1 - n if backwards else n]


def merge_pair(core, a, b, sums, backwards):
    steps = CHIPS // 4
    out_spec = pl.BlockSpec(
        (4, ROWS, FEATURES), lambda i: (steps - 1 - i if backwards else i, 0, 0)
    )
    spec = pl.BlockSpec((4, ROWS, FEATURES), lambda i: (i, 0, 0))
    return pl.pallas_call(
        functools.partial(
            merge_kernel, parts=len(b), steps=b[0].shape[0] // 4, backwards=backwards
        ),
        out_shape=(
            jax.ShapeDtypeStruct(a.shape, jnp.float32),
            jax.ShapeDtypeStruct((8, 128), jnp.float32),
        ),
        grid=(CHIPS // 4,),
        in_specs=[SMEM, spec] + parts_specs(b) + [VMEM] * len(sums),
        out_specs=(out_spec, pl.BlockSpec((8, 128), lambda i: (0, 0))),
        compiler_params=params(12),
        cost_estimate=cost(a.size, a.size),
    )(core, a, *b, *sums)


def gram_kernel(place_ref, v_ref, norm_ref, *refs):
    earlier_refs, (o_ref, t_ref) = refs[:-2], refs[-2:]
    t_ref[...] = jnp.zeros_like(t_ref)
    for gi in range(4):
        for gj in range(gi, 4):
            pairs = [
                (i, j)
                for i in range(4 * gi, 4 * gi + 4)
                for j in range(4 * gj, 4 * gj + 4)
                if i <= j
            ]

            def body(r, sums, pairs=pairs):
                sums = list(sums)
                rows = pl.ds(pl.multiple_of(r * 8, 8), 8)
                for lane in range(FEATURES // 128):
                    held = {}
                    for i, j in pairs:
                        for k in (i, j):
                            if k not in held:
                                held[k] = v_ref[k, rows, pl.ds(lane * 128, 128)]
                    for n, (i, j) in enumerate(pairs):
                        sums[n] = sums[n] + held[i] * held[j]
                return tuple(sums)

            zero = jnp.zeros((8, 128), jnp.float32)
            sums = lax.fori_loop(0, ROWS // 8, body, (zero,) * len(pairs))
            for pair, total in zip(pairs, sums):
                t_ref[pl.ds(PAIRS[pair], 1), :] = jnp.sum(total, axis=0, keepdims=True)
    lane = lax.broadcasted_iota(jnp.int32, (1, 128), 1)
    shown = (lane == 0) & (place_ref[1] == 1)
    t_ref[pl.ds(len(PAIRS) + place_ref[0], 1), :] = jnp.where(shown, norm_ref[0:1, :], 0.0)
    rows = [ref[...] for ref in earlier_refs]
    for part in range(2):
        rows.append(jnp.sum(t_ref[pl.ds(part * 128, 128), :].T, axis=0, keepdims=True))
    tile = jnp.concatenate(rows, axis=0)
    o_ref[...] = tile if o_ref.ndim == 2 else jnp.broadcast_to(tile[None], o_ref.shape)


def gram(place, v, norm, earlier, out_dims):
    return pl.pallas_call(
        gram_kernel,
        out_shape=jax.ShapeDtypeStruct(out_dims, jnp.float32),
        in_specs=[SMEM] + [VMEM] * (2 + len(earlier)),
        out_specs=VMEM,
        scratch_shapes=[pltpu.VMEM((256, 128), jnp.float32)],
        compiler_params=params(16),
        cost_estimate=cost(20 << 20, 4 * v.size),
    )(place, v, norm, *earlier)


def tree_coefs(read):
    count = CHIPS
    norms = [read(len(PAIRS) + i) for i in range(count)]
    table = {pair: read(n) for pair, n in PAIRS.items()}
    weights = list(norms)
    span = 1
    while count > 1:
        own = []
        for k in range(0, count, 2):
            cross = table[k, k + 1] * (norms[k] * norms[k + 1])
            for m in (k, k + 1):
                square = table[m, m] * (norms[m] * norms[m])
                own.append(1.0 - cross / (2.0 * (square + EPSILON)))
        weights = [w * own[i // span] for i, w in enumerate(weights)]
        factors = [c * n for c, n in zip(own, norms)]
        table = {key: value * (factors[key[0]] * factors[key[1]]) for key, value in table.items()}
        count //= 2
        merged = {}
        for k in range(count):
            merged[k, k] = (
                table[2 * k, 2 * k]
                + 2.0 * table[2 * k, 2 * k + 1]
                + table[2 * k + 1, 2 * k + 1]
            )
            for m in range(k + 1, count):
                merged[k, m] = (
                    table[2 * k, 2 * m]
                    + table[2 * k, 2 * m + 1]
                    + table[2 * k + 1, 2 * m]
                    + table[2 * k + 1, 2 * m + 1]
                )
        table = merged
        norms = [1.0] * count
        span *= 2
    return weights


def update_kernel(totals_ref, *refs):
    ins, outs, (sum_ref, scalar_ref, sem) = refs[:6], refs[6:10], refs[10:]
    sum_ref[...] = jnp.sum(totals_ref[...], axis=0)
    copy = pltpu.make_async_copy(sum_ref, scalar_ref, sem)
    copy.start()
    copy.wait()
    weights = [
        tree_coefs(lambda n, t=t: scalar_ref[2 * t + n // 128, n % 128]) for t in range(2)
    ]
    for t in range(2):
        v_ref, weight_ref, moment_ref = ins[3 * t : 3 * t + 3]
        new_weight_ref, new_moment_ref = outs[2 * t : 2 * t + 2]

        @pl.loop(0, ROWS // 8)
        def _(r, t=t, v_ref=v_ref, weight_ref=weight_ref, moment_ref=moment_ref, new_weight_ref=new_weight_ref, new_moment_ref=new_moment_ref):
            rows = pl.ds(pl.multiple_of(r * 8, 8), 8)
            merged = weights[t][0] * v_ref[0, rows, :]
            for i in range(1, CHIPS):
                merged = merged + weights[t][i] * v_ref[i, rows, :]
            moment = MOMENTUM_DECAY * moment_ref[rows, :] + merged
            new_moment_ref[rows, :] = moment
            new_weight_ref[rows, :] = weight_ref[rows, :] - STEP_SIZE * moment


def update(totals, *arrays):
    out = jax.ShapeDtypeStruct((ROWS, FEATURES), jnp.float32)
    return pl.pallas_call(
        update_kernel,
        out_shape=(out,) * 4,
        in_specs=[VMEM] * 7,
        out_specs=(VMEM,) * 4,
        scratch_shapes=[
            pltpu.VMEM((4, 128), jnp.float32),
            pltpu.SMEM((4, 128), jnp.float32),
            pltpu.SemaphoreType.DMA,
        ],
        compiler_params=params(8),
        cost_estimate=cost(8 << 20, 10 * MIB),
    )(totals, *arrays)


def after(value, *others):
    return lax.optimization_barrier((value,) + others)[0]


def shards(
    tokens, key_cotangent, value_cotangent, key_weight, value_weight, key_moment, value_moment
):
    shard_count, replicas = lax.axis_size("shard"), lax.axis_size("rep")
    index = lax.axis_index("rep").astype(jnp.int32)
    core = (index & 1)[None]
    leader = ((lax.axis_index("shard") == 0) & (index & 1 == 0)).astype(jnp.int32)
    place = jnp.stack([index >> 1, leader])
    backwards_place = jnp.stack([CHIPS - 1 - (index >> 1), leader])
    swap = [(i, i ^ 1) for i in range(replicas)]
    core_groups = [list(range(c, replicas, 2)) for c in range(2)]
    backwards_groups = [group[::-1] for group in core_groups]

    def summed(sums):
        sums = sums + lax.ppermute(sums, "rep", swap)
        shifts = [
            [(s, (s + d) % shard_count) for s in range(shard_count)] for d in range(1, shard_count)
        ]
        return [sums] + [lax.ppermute(sums, "shard", shift) for shift in shifts]

    def gathered(sent, groups):
        return lax.all_to_all(sent, "rep", 0, 0, axis_index_groups=groups)

    key_other, own_rows, other_rows = split_and_grad(core, tokens, key_cotangent)
    key_arrived = [lax.ppermute(key_other, "rep", swap)]
    key_own = grad(own_rows, key_cotangent)
    half = other_rows.shape[0] // 2
    value_first = grad(after(other_rows, key_own), value_cotangent, 0, half, [key_own])
    key_sums = summed(pair_sums(after(core, value_first), key_own, key_arrived))
    value_second = grad(
        after(other_rows, key_sums[0]), value_cotangent, half, half, [key_own] + key_arrived
    )
    key_merged, key_norm = merge_pair(core, key_own, key_arrived, key_sums, False)
    key_sent = key_merged.astype(jnp.float16)
    key_all = gathered(key_sent, core_groups)

    value_arrived = [
        lax.ppermute(value_first, "rep", swap),
        lax.ppermute(after(value_second, key_sent), "rep", swap),
    ]
    value_own, value_sums = grad_and_pair_sums(
        core, after(own_rows, key_sent), value_cotangent, value_arrived
    )
    value_sums = summed(value_sums)
    value_merged, value_norm = merge_pair(core, value_own, value_arrived, value_sums, True)
    value_all = gathered(value_merged.astype(jnp.float16), backwards_groups)

    key_v = key_all.astype(jnp.float32)
    key_vector = gram(place, key_v, key_norm, [], (2, 128))
    value_v = value_all.astype(jnp.float32)
    vectors = gram(backwards_place, value_v, value_norm, [key_vector], (shard_count * replicas, 4, 128))
    everyone = list(range(shard_count * replicas))[::-1]
    totals = lax.all_to_all(vectors, ("shard", "rep"), 0, 0, axis_index_groups=[everyone])
    new_key_weight, new_key_moment, new_value_weight, new_value_moment = update(
        totals, key_v, key_weight, key_moment, value_v, value_weight, value_moment
    )
    return (new_key_weight, new_value_weight, new_key_moment, new_value_moment)


def solution(mesh):
    in_specs = (
        P("rep", "shard"),
        P("rep", None),
        P("rep", None),
        P(("shard", "rep"), None),
        P(("shard", "rep"), None),
        P(("shard", "rep"), None),
        P(("shard", "rep"), None),
    )
    out_specs = (
        P(("shard", "rep"), None),
        P(("shard", "rep"), None),
        P(("shard", "rep"), None),
        P(("shard", "rep"), None),
    )
    return jax.shard_map(shards, mesh=mesh, in_specs=in_specs, out_specs=out_specs, check_vma=False)
```

```python
import functools
import math

import jax
import jax.numpy as jnp
from jax import lax
from jax.experimental import pallas as pl
from jax.experimental.pallas import tpu as pltpu
from jax.sharding import PartitionSpec as P

EPSILON = 1e-06
MOMENTUM_DECAY = 0.9
STEP_SIZE = 0.01
CHIPS = 16
ROWS = 64
FEATURES = 1024
SENT_NORM = 16384.0
MIB = 1 << 20
PAIRS = {pair: n for n, pair in enumerate((i, j) for i in range(CHIPS) for j in range(i, CHIPS))}


def params(mib):
    return pltpu.CompilerParams(vmem_limit_bytes=mib * MIB)


def cost(flops, moved):
    return pl.CostEstimate(flops=flops, bytes_accessed=moved, transcendentals=0)


VMEM = pl.BlockSpec(memory_space=pltpu.VMEM)
SMEM = pl.BlockSpec(memory_space=pltpu.SMEM)


def scaled_dot(rows, cotangent):
    product = jnp.dot(rows, cotangent, preferred_element_type=jnp.float32)
    return (product * (1.0 / math.sqrt(rows.shape[1]))).reshape(-1, ROWS, FEATURES)


def split_kernel(core_ref, x_hbm, y_hbm, grad_ref, own_ref, other_ref, x_ref, y_ref, x_sems, y_sem):
    steps, depth, width = x_ref.shape
    x_copies = [
        pltpu.make_async_copy(
            x_hbm.at[:, pl.ds(i * width, width)], x_ref.at[i], x_sems.at[i]
        )
        for i in range(steps)
    ]
    y_copy = pltpu.make_async_copy(y_hbm, y_ref, y_sem)
    x_copies[0].start()
    y_copy.start()
    for copy in x_copies[1:]:
        copy.start()
    is_first = core_ref[0] == 0
    half = width // 2
    per = half // ROWS
    for i in range(steps):
        x_copies[i].wait()
        blocks = x_ref[i].T.reshape(-1, 2, ROWS, depth)
        first = blocks[:, 0].reshape(-1, depth)
        second = blocks[:, 1].reshape(-1, depth)
        own_ref[pl.ds(i * half, half), :] = jnp.where(is_first, first, second)
        other = jnp.where(is_first, second, first)
        other_ref[pl.ds(i * half, half), :] = other
        if i == 0:
            y_copy.wait()
        grad_ref[pl.ds(i * per, per)] = scaled_dot(other, y_ref[...])


def split_and_grad(core, tokens, cotangent):
    depth, width = tokens.shape
    step = 512
    half = jax.ShapeDtypeStruct((width // 2, depth), jnp.bfloat16)
    hbm = pl.BlockSpec(memory_space=pltpu.HBM)
    return pl.pallas_call(
        split_kernel,
        out_shape=(
            jax.ShapeDtypeStruct((CHIPS, ROWS, FEATURES), jnp.float32),
            half,
            half,
        ),
        in_specs=[SMEM, hbm, hbm],
        out_specs=(VMEM,) * 3,
        scratch_shapes=[
            pltpu.VMEM((width // step, depth, step), jnp.bfloat16),
            pltpu.VMEM(cotangent.shape, jnp.bfloat16),
            pltpu.SemaphoreType.DMA((width // step,)),
            pltpu.SemaphoreType.DMA,
        ],
        compiler_params=params(32),
        cost_estimate=cost(depth * width * FEATURES, 24 * MIB),
    )(core, tokens, cotangent)


def grad_kernel(x_ref, y_ref, *refs, start):
    o_ref = refs[-1]
    step = 256
    per = step // ROWS

    @pl.loop(0, o_ref.shape[0] // per)
    def _(i):
        rows = x_ref[pl.ds(pl.multiple_of(start + i * step, step), step), :]
        o_ref[pl.ds(i * per, per)] = scaled_dot(rows, y_ref[...])


def grad(rows, cotangent, start=0, count=None, kept=()):
    count = count or rows.shape[0]
    return pl.pallas_call(
        functools.partial(grad_kernel, start=start),
        out_shape=jax.ShapeDtypeStruct((count // ROWS, ROWS, FEATURES), jnp.float32),
        in_specs=[VMEM] * (2 + len(kept)),
        out_specs=VMEM,
        compiler_params=params(8),
        cost_estimate=cost(2 * cotangent.shape[0] * count * FEATURES, 12 * MIB),
    )(rows, cotangent, *kept)


def parts_specs(parts):
    steps = parts[0].shape[0] // 4
    return [
        pl.BlockSpec(
            (4, ROWS, FEATURES),
            lambda i, n=n: (jnp.clip(i - n * steps, 0, steps - 1), 0, 0),
        )
        for n in range(len(parts))
    ]


def block_of(refs, steps):
    block = refs[0][...]
    for n in range(1, len(refs)):
        block = jnp.where(pl.program_id(0) >= n * steps, refs[n][...], block)
    return block


def add_sums(is_first, a, b, acc_ref, o_ref):
    step = pl.program_id(0)

    @pl.when(step == 0)
    def _():
        acc_ref[...] = jnp.zeros_like(acc_ref)

    a = a.reshape(-1, 8, FEATURES)
    b = b.reshape(-1, 8, FEATURES)
    own, other = jnp.sum(a * a, axis=0), jnp.sum(b * b, axis=0)
    acc_ref[0] += jnp.sum(a * b, axis=0)
    acc_ref[1] += jnp.where(is_first, own, other)
    acc_ref[2] += jnp.where(is_first, other, own)

    @pl.when(step == pl.num_programs(0) - 1)
    def _():
        rows = [jnp.sum(acc_ref[k], axis=0, keepdims=True) for k in range(3)]
        rows = [jnp.sum(row, axis=1, keepdims=True) for row in rows]
        rows = [jnp.broadcast_to(row, (1, 128)) for row in rows]
        o_ref[0] = jnp.concatenate(rows + [jnp.zeros((5, 128), jnp.float32)], axis=0)


def pair_kernel(core_ref, a_ref, *refs, steps):
    b_refs, (o_ref, acc_ref) = refs[:-2], refs[-2:]
    add_sums(core_ref[0] == 0, a_ref[...], block_of(b_refs, steps), acc_ref, o_ref)


SUMS = jax.ShapeDtypeStruct((1, 8, 128), jnp.float32)
SUMS_SPEC = pl.BlockSpec((1, 8, 128), lambda i: (0, 0, 0))


def pair_sums(core, a, b):
    spec = pl.BlockSpec((4, ROWS, FEATURES), lambda i: (i, 0, 0))
    return pl.pallas_call(
        functools.partial(pair_kernel, steps=b[0].shape[0] // 4),
        out_shape=SUMS,
        grid=(CHIPS // 4,),
        in_specs=[SMEM, spec] + parts_specs(b),
        out_specs=SUMS_SPEC,
        scratch_shapes=[pltpu.VMEM((3, 8, FEATURES), jnp.float32)],
        compiler_params=params(10),
        cost_estimate=cost(a.size, a.size),
    )(core, a, *b)


def grad_pair_kernel(core_ref, x_ref, y_ref, *refs, steps):
    b_refs, (grad_ref, o_ref, acc_ref) = refs[:-3], refs[-3:]
    grad_ref[...] = scaled_dot(x_ref[...], y_ref[...])
    add_sums(core_ref[0] == 0, grad_ref[...], block_of(b_refs, steps), acc_ref, o_ref)


def grad_and_pair_sums(core, rows, cotangent, b):
    count, depth = rows.shape
    step = 4 * ROWS
    return pl.pallas_call(
        functools.partial(grad_pair_kernel, steps=b[0].shape[0] // 4),
        out_shape=(jax.ShapeDtypeStruct((CHIPS, ROWS, FEATURES), jnp.float32), SUMS),
        grid=(count // step,),
        in_specs=[
            SMEM,
            pl.BlockSpec((step, depth), lambda i: (i, 0)),
            pl.BlockSpec((depth, FEATURES), lambda i: (0, 0)),
        ]
        + parts_specs(b),
        out_specs=(pl.BlockSpec((4, ROWS, FEATURES), lambda i: (i, 0, 0)), SUMS_SPEC),
        scratch_shapes=[pltpu.VMEM((3, 8, FEATURES), jnp.float32)],
        compiler_params=params(24),
        cost_estimate=cost(2 * depth * count * FEATURES, 16 * MIB),
    )(core, rows, cotangent, *b)


def merge_kernel(core_ref, a_ref, *refs, parts, steps, backwards):
    b_refs, sums_refs, (o_ref, norm_ref) = refs[:parts], refs[parts:-2], refs[-2:]
    sums = sum(jnp.sum(ref[...], axis=0) for ref in sums_refs)
    cross, p, q = sums[0:1], sums[1:2], sums[2:3]
    is_first = core_ref[0] == 0
    first = 1.0 - cross / (2.0 * (p + EPSILON))
    second = 1.0 - cross / (2.0 * (q + EPSILON))
    squares = first * first * p + second * second * q
    square = jnp.maximum(squares + 2.0 * first * second * cross, 1e-6 * squares)
    norm = jnp.sqrt(jnp.maximum(square, 1e-30))
    scale = SENT_NORM / norm
    norm_ref[...] = jnp.broadcast_to(norm * (1.0 / SENT_NORM), norm_ref.shape)
    own = jnp.where(is_first, first, second) * scale
    other = jnp.where(is_first, second, first) * scale
    own = jnp.concatenate([own] * (FEATURES // 128), axis=1)[None]
    other = jnp.concatenate([other] * (FEATURES // 128), axis=1)[None]
    merged = own * a_ref[...] + other * block_of(b_refs, steps)
    count = merged.shape[0]
    for n in range(count):
        o_ref[n] = merged[count - 1 - n if backwards else n]


def merge_pair(core, a, b, sums, backwards):
    steps = CHIPS // 4
    out_spec = pl.BlockSpec(
        (4, ROWS, FEATURES), lambda i: (steps - 1 - i if backwards else (i + steps // 2) % steps, 0, 0)
    )
    spec = pl.BlockSpec((4, ROWS, FEATURES), lambda i: (i, 0, 0))
    return pl.pallas_call(
        functools.partial(
            merge_kernel, parts=len(b), steps=b[0].shape[0] // 4, backwards=backwards
        ),
        out_shape=(
            jax.ShapeDtypeStruct(a.shape, jnp.float32),
            jax.ShapeDtypeStruct((8, 128), jnp.float32),
        ),
        grid=(CHIPS // 4,),
        in_specs=[SMEM, spec] + parts_specs(b) + [VMEM] * len(sums),
        out_specs=(out_spec, pl.BlockSpec((8, 128), lambda i: (0, 0))),
        compiler_params=params(12),
        cost_estimate=cost(a.size, a.size),
    )(core, a, *b, *sums)


def gram_kernel(place_ref, v_ref, norm_ref, *refs):
    earlier_refs, (o_ref, t_ref) = refs[:-2], refs[-2:]
    t_ref[...] = jnp.zeros_like(t_ref)
    for gi in range(4):
        for gj in range(gi, 4):
            pairs = [
                (i, j)
                for i in range(4 * gi, 4 * gi + 4)
                for j in range(4 * gj, 4 * gj + 4)
                if i <= j
            ]

            def body(r, sums, pairs=pairs):
                sums = list(sums)
                rows = pl.ds(pl.multiple_of(r * 8, 8), 8)
                for lane in range(FEATURES // 128):
                    held = {}
                    for i, j in pairs:
                        for k in (i, j):
                            if k not in held:
                                held[k] = v_ref[k, rows, pl.ds(lane * 128, 128)]
                    for n, (i, j) in enumerate(pairs):
                        sums[n] = sums[n] + held[i] * held[j]
                return tuple(sums)

            zero = jnp.zeros((8, 128), jnp.float32)
            sums = lax.fori_loop(0, ROWS // 8, body, (zero,) * len(pairs))
            for pair, total in zip(pairs, sums):
                t_ref[pl.ds(PAIRS[pair], 1), :] = jnp.sum(total, axis=0, keepdims=True)
    lane = lax.broadcasted_iota(jnp.int32, (1, 128), 1)
    shown = (lane == 0) & (place_ref[1] == 1)
    t_ref[pl.ds(len(PAIRS) + place_ref[0], 1), :] = jnp.where(shown, norm_ref[0:1, :], 0.0)
    rows = [ref[...] for ref in earlier_refs]
    for part in range(2):
        rows.append(jnp.sum(t_ref[pl.ds(part * 128, 128), :].T, axis=0, keepdims=True))
    tile = jnp.concatenate(rows, axis=0)
    o_ref[...] = tile if o_ref.ndim == 2 else jnp.broadcast_to(tile[None], o_ref.shape)


def gram(place, v, norm, earlier, out_dims):
    return pl.pallas_call(
        gram_kernel,
        out_shape=jax.ShapeDtypeStruct(out_dims, jnp.float32),
        in_specs=[SMEM] + [VMEM] * (2 + len(earlier)),
        out_specs=VMEM,
        scratch_shapes=[pltpu.VMEM((256, 128), jnp.float32)],
        compiler_params=params(16),
        cost_estimate=cost(20 << 20, 4 * v.size),
    )(place, v, norm, *earlier)


def tree_coefs(read):
    count = CHIPS
    norms = [read(len(PAIRS) + i) for i in range(count)]
    table = {pair: read(n) for pair, n in PAIRS.items()}
    weights = list(norms)
    span = 1
    while count > 1:
        own = []
        for k in range(0, count, 2):
            cross = table[k, k + 1] * (norms[k] * norms[k + 1])
            for m in (k, k + 1):
                square = table[m, m] * (norms[m] * norms[m])
                own.append(1.0 - cross / (2.0 * (square + EPSILON)))
        weights = [w * own[i // span] for i, w in enumerate(weights)]
        factors = [c * n for c, n in zip(own, norms)]
        table = {key: value * (factors[key[0]] * factors[key[1]]) for key, value in table.items()}
        count //= 2
        merged = {}
        for k in range(count):
            merged[k, k] = (
                table[2 * k, 2 * k]
                + 2.0 * table[2 * k, 2 * k + 1]
                + table[2 * k + 1, 2 * k + 1]
            )
            for m in range(k + 1, count):
                merged[k, m] = (
                    table[2 * k, 2 * m]
                    + table[2 * k, 2 * m + 1]
                    + table[2 * k + 1, 2 * m]
                    + table[2 * k + 1, 2 * m + 1]
                )
        table = merged
        norms = [1.0] * count
        span *= 2
    return weights


def update_kernel(totals_ref, *refs):
    ins, outs, (sum_ref, scalar_ref, sem) = refs[:6], refs[6:10], refs[10:]
    sum_ref[...] = jnp.sum(totals_ref[...], axis=0)
    copy = pltpu.make_async_copy(sum_ref, scalar_ref, sem)
    copy.start()
    copy.wait()
    weights = [
        tree_coefs(lambda n, t=t: scalar_ref[2 * t + n // 128, n % 128]) for t in range(2)
    ]
    for t in range(2):
        v_ref, weight_ref, moment_ref = ins[3 * t : 3 * t + 3]
        new_weight_ref, new_moment_ref = outs[2 * t : 2 * t + 2]

        @pl.loop(0, ROWS // 8)
        def _(r, t=t, v_ref=v_ref, weight_ref=weight_ref, moment_ref=moment_ref, new_weight_ref=new_weight_ref, new_moment_ref=new_moment_ref):
            rows = pl.ds(pl.multiple_of(r * 8, 8), 8)
            merged = weights[t][0] * v_ref[0, rows, :]
            for i in range(1, CHIPS):
                merged = merged + weights[t][i] * v_ref[i, rows, :]
            moment = MOMENTUM_DECAY * moment_ref[rows, :] + merged
            new_moment_ref[rows, :] = moment
            new_weight_ref[rows, :] = weight_ref[rows, :] - STEP_SIZE * moment


def update(totals, *arrays):
    out = jax.ShapeDtypeStruct((ROWS, FEATURES), jnp.float32)
    return pl.pallas_call(
        update_kernel,
        out_shape=(out,) * 4,
        in_specs=[VMEM] * 7,
        out_specs=(VMEM,) * 4,
        scratch_shapes=[
            pltpu.VMEM((4, 128), jnp.float32),
            pltpu.SMEM((4, 128), jnp.float32),
            pltpu.SemaphoreType.DMA,
        ],
        compiler_params=params(8),
        cost_estimate=cost(8 << 20, 10 * MIB),
    )(totals, *arrays)


def after(value, *others):
    return lax.optimization_barrier((value,) + others)[0]


def shards(
    tokens, key_cotangent, value_cotangent, key_weight, value_weight, key_moment, value_moment
):
    shard_count, replicas = lax.axis_size("shard"), lax.axis_size("rep")
    index = lax.axis_index("rep").astype(jnp.int32)
    core = (index & 1)[None]
    leader = ((lax.axis_index("shard") == 0) & (index & 1 == 0)).astype(jnp.int32)
    place = jnp.stack([(index >> 1) ^ CHIPS // 2, leader])
    backwards_place = jnp.stack([CHIPS - 1 - (index >> 1), leader])
    swap = [(i, i ^ 1) for i in range(replicas)]
    core_groups = [list(range(c, replicas, 2)) for c in range(2)]
    halves_groups = [group[CHIPS // 2 :] + group[: CHIPS // 2] for group in core_groups]
    backwards_groups = [group[::-1] for group in core_groups]

    def summed(sums):
        sums = sums + lax.ppermute(sums, "rep", swap)
        shifts = [
            [(s, (s + d) % shard_count) for s in range(shard_count)] for d in range(1, shard_count)
        ]
        return [sums] + [lax.ppermute(sums, "shard", shift) for shift in shifts]

    def gathered(sent, groups):
        return lax.all_to_all(sent, "rep", 0, 0, axis_index_groups=groups)

    key_other, own_rows, other_rows = split_and_grad(core, tokens, key_cotangent)
    key_arrived = [lax.ppermute(key_other, "rep", swap)]
    key_own = grad(own_rows, key_cotangent)
    half = other_rows.shape[0] // 2
    value_first = grad(after(other_rows, key_own), value_cotangent, 0, half, [key_own])
    key_sums = summed(pair_sums(after(core, value_first), key_own, key_arrived))
    value_second = grad(
        after(other_rows, key_sums[0]), value_cotangent, half, half, [key_own] + key_arrived
    )
    key_merged, key_norm = merge_pair(core, key_own, key_arrived, key_sums, False)
    key_sent = key_merged.astype(jnp.float16)
    key_all = gathered(key_sent, halves_groups)

    value_arrived = [
        lax.ppermute(value_first, "rep", swap),
        lax.ppermute(after(value_second, key_sent), "rep", swap),
    ]
    value_own, value_sums = grad_and_pair_sums(
        core, after(own_rows, key_sent), value_cotangent, value_arrived
    )
    value_sums = summed(value_sums)
    value_merged, value_norm = merge_pair(core, value_own, value_arrived, value_sums, True)
    value_all = gathered(value_merged.astype(jnp.float16), backwards_groups)

    key_v = key_all.astype(jnp.float32)
    key_vector = gram(place, key_v, key_norm, [], (2, 128))
    value_v = value_all.astype(jnp.float32)
    vectors = gram(backwards_place, value_v, value_norm, [key_vector], (shard_count * replicas, 4, 128))
    everyone = list(range(shard_count * replicas))[::-1]
    totals = lax.all_to_all(vectors, ("shard", "rep"), 0, 0, axis_index_groups=[everyone])
    new_key_weight, new_key_moment, new_value_weight, new_value_moment = update(
        totals, key_v, key_weight, key_moment, value_v, value_weight, value_moment
    )
    return (new_key_weight, new_value_weight, new_key_moment, new_value_moment)


def solution(mesh):
    in_specs = (
        P("rep", "shard"),
        P("rep", None),
        P("rep", None),
        P(("shard", "rep"), None),
        P(("shard", "rep"), None),
        P(("shard", "rep"), None),
        P(("shard", "rep"), None),
    )
    out_specs = (
        P(("shard", "rep"), None),
        P(("shard", "rep"), None),
        P(("shard", "rep"), None),
        P(("shard", "rep"), None),
    )
    return jax.shard_map(shards, mesh=mesh, in_specs=in_specs, out_specs=out_specs, check_vma=False)
```
